32 devices in a mesh: dp: 8 (over y, x, core), seq: 4 (over z).
Axes of the slice: x: 2, y: 2, z: 4, core: 2. Of those that a mesh axis runs over, the one named last changes fastest.
Arguments:
- tokens: bfloat16 [16, 1024, 1024], P('dp', 'seq'), may hold values from -6 to 6
- source: bfloat16 [16, 1024, 1024], P('dp', 'seq'), may hold values from -6 to 6
- target_lengths: int32 [16, 4], P('dp'), may hold values from 1 to 896, 1024 in all within a row
- source_lengths: int32 [16], P('dp'), may hold values from 896 to 1024, as said below
- step_index: int32 [1], replicated, may hold values from 0 to 4
- self_query: bfloat16 [1024, 1024], P('dp'), may hold values from -0.1875 to 0.1875
- self_key: bfloat16 [1024, 1024], P('dp'), may hold values from -0.1875 to 0.1875
- self_value: bfloat16 [1024, 1024], P('dp'), may hold values from -0.1875 to 0.1875
- self_out: bfloat16 [1024, 1024], P('dp'), may hold values from -0.75 to 0.75
- cross_query: bfloat16 [1024, 1024], P('dp'), may hold values from -0.1875 to 0.1875
- cross_key: bfloat16 [1024, 1024], P('dp'), may hold values from -0.1875 to 0.1875
- cross_value: bfloat16 [1024, 1024], P('dp'), may hold values from -0.1875 to 0.1875
- cross_out: bfloat16 [1024, 1024], P('dp'), may hold values from -0.75 to 0.75
- ffn_expand: bfloat16 [1024, 4096], P('dp'), may hold values from -0.1875 to 0.1875
- ffn_contract: bfloat16 [4096, 1024], P('dp'), may hold values from -0.09375 to 0.09375
- adapter_down: bfloat16 [1024, 512], replicated, may hold values from -0.1875 to 0.1875
- adapter_up: bfloat16 [512, 1024], replicated, may hold values from -0.25 to 0.25
- grad_output: bfloat16 [16, 1024, 1024], P('dp', 'seq'), may hold values from -6 to 6
Outputs:
- output: bfloat16 [16, 1024, 1024], P('dp', 'seq')
- grad_tokens: bfloat16 [16, 1024, 1024], P('dp', 'seq')
- grad_source: bfloat16 [16, 1024, 1024], P('dp', 'seq')
- grad_down: float32 [1024, 512], replicated
- grad_up: float32 [512, 1024], replicated
The draws below stay inside these ranges and needn't reach their ends.
Inputs may be any that keep to these rules, and one draw needn't show every extreme that they name: `target_lengths`: each row's lengths sum to 1024; the largest of each row is exactly 896. `source_lengths`: some row has exactly 1024, some row exactly 896.
All inputs are finite; a program needn't handle non-finite values.
Results may differ from the reference program's by a relative error of at most 0.02.
Values may be sent and summed in bfloat16 or wider, within the bound.
No kernel may reach another device: no remote copies, remote signals or barrier semaphores. Data moves between devices by JAX's collectives and lax.ppermute only.
A program may use at most 320 MiB of HBM per device.

```python
import math
import jax
import jax.numpy as jnp
import numpy as np
from jax import lax

D = 1024
HEADS = 16
HEAD = 64
FF = 4096
AD = 512
LEN = 1024
SRC = 1024
DOCS = 4
ROWS = 16
LONGEST = 896


def draw_source_lengths(key, part):
    key = jax.random.fold_in(key, 7)
    first_key, second_key = jax.random.split(key)
    drawn = jax.random.randint(first_key, (ROWS,), SRC - SRC // 8, SRC + 1)
    order = jax.random.permutation(second_key, ROWS)
    drawn = drawn.at[order[0]].set(SRC)
    drawn = drawn.at[order[1]].set(SRC - SRC // 8)
    return drawn.astype(jnp.int32)


def steps_of(own_key, dims, cuts, least, largest):
    loudness, own = 1.0, jax.random.fold_in(own_key, 6)
    for axis_at, parts in cuts:
        heights = jnp.exp(jax.random.uniform(jax.random.fold_in(own, axis_at), (parts,), jnp.float32, least / len(cuts), largest / len(cuts)))
        loudness = loudness * jnp.repeat(heights, dims[axis_at] // parts).reshape([-1 if axis == axis_at else 1 for axis in range(len(dims))])
    return loudness


def split_up(amount, total, most, slope):
    weights = [(1 << 20) // math.isqrt(rank ** slope) + 1 for rank in range(2, amount + 1)]
    spare, counts = total - most - (amount - 1), [1] * (amount - 1)
    while spare > 0:
        candidates = [i for i in range(amount - 1) if counts[i] < most]
        mass, budget = sum([weights[i] for i in candidates]), spare
        for i in candidates:
            extra = min(most - counts[i], max(1, budget * weights[i] // mass), spare)
            counts[i] = counts[i] + extra
            spare = spare - extra
    return np.array([most] + counts)


def uneven_parts(rng, amount, total, most, skew):
    if amount == 2:
        one = jax.random.randint(rng, (), max(1, total - most), min(most, total - 1) + 1)
        return jnp.stack([one, total - one])
    tallies = jnp.asarray(split_up(amount, total, most, skew), jnp.int32)
    twos = (amount - 1) // 2
    giver, receiver = tallies[1:1 + 2 * twos:2], tallies[2:2 + 2 * twos:2]
    slack = jnp.minimum(giver - 1, most - receiver)
    moved = jax.random.randint(jax.random.fold_in(rng, 1), (twos,), 0, 1 << 20) % (slack + 1)
    tallies = tallies.at[1:1 + 2 * twos:2].set(giver - moved).at[2:2 + 2 * twos:2].set(receiver + moved)
    return tallies[jax.random.permutation(jax.random.fold_in(rng, 2), amount)]


def bell_draw(rng, dims, scale, most, cuts=(), kind=jnp.bfloat16):
    entries = scale * jax.random.normal(rng, dims, jnp.float32)
    if cuts:
        entries = entries * steps_of(rng, dims, cuts, -0.22, 0.18)
    return jnp.clip(entries, -most, most).astype(kind)


def setup_inputs(seed: int = 0) -> dict:
    splits = jax.random.split(jax.random.key(seed), 19)
    return {
        "tokens": bell_draw(splits[0], (ROWS, LEN, D), 1.0, 6.0, ((0, 8), (1, 4))),
        "source": bell_draw(splits[1], (ROWS, SRC, D), 1.0, 6.0, ((0, 8), (1, 4))),
        "target_lengths": jax.vmap(lambda own: uneven_parts(own, DOCS, LEN, LONGEST, 2))(jax.random.split(splits[2], ROWS)).reshape((ROWS, DOCS)).astype(jnp.int32),
        "source_lengths": draw_source_lengths(jax.random.fold_in(splits[18], 71), 0),
        "step_index": jax.random.randint(splits[4], (1,), 0, 5).astype(jnp.int32),
        "self_query": bell_draw(splits[5], (D, D), D ** -0.5, 0.1875, ((0, 8),)),
        "self_key": bell_draw(splits[6], (D, D), D ** -0.5, 0.1875, ((0, 8),)),
        "self_value": bell_draw(splits[7], (D, D), D ** -0.5, 0.1875, ((0, 8),)),
        "self_out": bell_draw(splits[8], (D, D), (D // 16) ** -0.5, 0.75, ((0, 8),)),
        "cross_query": bell_draw(splits[9], (D, D), D ** -0.5, 0.1875, ((0, 8),)),
        "cross_key": bell_draw(splits[10], (D, D), D ** -0.5, 0.1875, ((0, 8),)),
        "cross_value": bell_draw(splits[11], (D, D), D ** -0.5, 0.1875, ((0, 8),)),
        "cross_out": bell_draw(splits[12], (D, D), (D // 16) ** -0.5, 0.75, ((0, 8),)),
        "ffn_expand": bell_draw(splits[13], (D, FF), D ** -0.5, 0.1875, ((0, 8),)),
        "ffn_contract": bell_draw(splits[14], (FF, D), FF ** -0.5, 0.09375, ((0, 8),)),
        "adapter_down": bell_draw(splits[15], (D, AD), D ** -0.5, 0.1875),
        "adapter_up": bell_draw(splits[16], (AD, D), AD ** -0.5, 0.25),
        "grad_output": bell_draw(splits[17], (ROWS, LEN, D), 1.0, 6.0, ((0, 8), (1, 4))),
    }


@jax.custom_vjp
def low(v):
    return lax.optimization_barrier(v.astype(jnp.bfloat16)).astype(jnp.float32)

@jax.custom_vjp
def low_back(v):
    return v

def low_keep(v):
    return (low(v), None)

def low_pass(kept, grad):
    return (grad,)

def back_keep(v):
    return (v, None)

def back_low(kept, grad):
    return (low(grad),)
low.defvjp(low_keep, low_pass)
low_back.defvjp(back_keep, back_low)

def matmul(left, right):
    return jnp.dot(left, right, precision=lax.Precision.HIGHEST, preferred_element_type=jnp.float32)

def normalize(values):
    centered = values - lax.optimization_barrier(jnp.mean(values, axis=-1, keepdims=True))
    spread = lax.optimization_barrier(jnp.mean(centered * centered, axis=-1, keepdims=True))
    return centered * lax.rsqrt(spread + 1e-05)

def smooth(values):
    return jax.nn.gelu(values, approximate=False)

def attention(query, keys, values, allowed):
    key_heads = keys.reshape(keys.shape[0], HEADS, HEAD)
    value_heads = values.reshape(values.shape[0], HEADS, HEAD)
    scores = low_back(jnp.einsum('qhd,khd->hqk', query, key_heads, precision=lax.Precision.HIGHEST))
    scores = jnp.where(allowed[None], scores, -1e+30)
    shifted = jnp.exp(scores - lax.optimization_barrier(jnp.max(scores, axis=-1, keepdims=True)))
    probs = low(shifted / lax.optimization_barrier(jnp.sum(shifted, axis=-1, keepdims=True)))
    attended = jnp.einsum('hqk,khd->qhd', probs, value_heads, precision=lax.Precision.HIGHEST)
    return low(low_back(attended.reshape(query.shape[0], D)))

def decoder_layer(row_tokens, row_source, down, up, weights, doc_lens, src_len, branch_scale):
    w_query, w_key, w_value, w_out, c_query, c_key, c_value, c_out, w_expand, w_contract = weights
    positions = jnp.arange(LEN, dtype=jnp.int32)
    doc_ends = jnp.cumsum(doc_lens)[:-1]
    doc_of = lax.optimization_barrier(jnp.sum((positions[:, None] >= doc_ends[None, :]).astype(jnp.int32), axis=-1))
    self_allowed = (positions[None, :] <= positions[:, None]) & (doc_of[:, None] == doc_of[None, :])
    source_allowed = jnp.broadcast_to((jnp.arange(SRC, dtype=jnp.int32) < src_len)[None, :], (LEN, SRC))
    query = low(low_back(0.125 * matmul(row_tokens, w_query))).reshape(LEN, HEADS, HEAD)
    keys = low(low_back(matmul(row_tokens, w_key)))
    values = low(low_back(matmul(row_tokens, w_value)))
    first_sum = row_tokens + low_back(matmul(attention(query, keys, values, self_allowed), w_out))
    first_norm = normalize(first_sum)
    cross_q = low(low_back(0.125 * matmul(low(first_norm), c_query))).reshape(LEN, HEADS, HEAD)
    src_keys = low(low_back(matmul(row_source, c_key)))
    src_values = low(low_back(matmul(row_source, c_value)))
    second_sum = first_norm + low_back(matmul(attention(cross_q, src_keys, src_values, source_allowed), c_out))
    second_norm = normalize(second_sum)
    second_low = low(second_norm)
    hidden = low(smooth(low_back(matmul(second_low, w_expand))))
    squeezed = low(smooth(low_back(matmul(second_low, down))))
    third_sum = second_norm + low_back(matmul(hidden, w_contract)) + branch_scale * low_back(matmul(squeezed, up))
    return normalize(third_sum)

def reference(tokens, source, target_lengths, source_lengths, step_index, self_query, self_key, self_value, self_out, cross_query, cross_key, cross_value, cross_out, ffn_expand, ffn_contract, adapter_down, adapter_up, grad_output):
    weights = tuple((w.astype(jnp.float32) for w in (self_query, self_key, self_value, self_out, cross_query, cross_key, cross_value, cross_out, ffn_expand, ffn_contract)))
    down = adapter_down.astype(jnp.float32)
    up = adapter_up.astype(jnp.float32)
    branch_scale = (step_index[0] + 1).astype(jnp.float32) / 5.0

    def one_row(sums_so_far, row_items):
        row_tokens, row_source, doc_lens, src_len, row_grad = row_items

        def forward(tok_vals, src_vals, down_vals, up_vals):
            return decoder_layer(tok_vals, src_vals, down_vals, up_vals, weights, doc_lens, src_len, branch_scale)
        result, pullback = jax.vjp(forward, row_tokens.astype(jnp.float32), row_source.astype(jnp.float32), down, up)
        g_tok, g_src, g_down, g_up = pullback(row_grad.astype(jnp.float32))
        carried = (sums_so_far[0] + g_down, sums_so_far[1] + g_up)
        return (carried, (result.astype(jnp.bfloat16), g_tok.astype(jnp.bfloat16), g_src.astype(jnp.bfloat16)))
    start_sums = (jnp.zeros((D, AD), jnp.float32), jnp.zeros((AD, D), jnp.float32))
    (grad_down, grad_up), (output, grad_tokens, grad_source) = lax.scan(one_row, start_sums, (tokens, source, target_lengths, source_lengths, grad_output))
    return (output, grad_tokens, grad_source, grad_down, grad_up)
```

```python
import functools
import jax
import jax.numpy as jnp
from jax.sharding import PartitionSpec as P
from jax import lax
from jax.experimental import pallas as pl
from jax.experimental.pallas import tpu as pltpu
BF=jnp.bfloat16; F32=jnp.float32
NEG=-1e30
LOG2E=1.4426950408889634
VM=56*1024*1024

SELF_PLANS=(((((0,True),)), ((0,False),(2,False),(3,False),(1,True))),
            (((2,False),(0,True)), ((2,False),(0,False),(1,True))))
CROSS_PLANS=((((0,False),(1,False),(2,False),(3,False)),)*2,)

def nt(a,b): return lax.dot_general(a,b,(((1,),(1,)),((),())),preferred_element_type=F32)
def nn(a,b): return lax.dot_general(a,b,(((1,),(0,)),((),())),preferred_element_type=F32)

def half_mask(shape, h):
    l=lax.broadcasted_iota(jnp.int32, shape, 1)
    return (l<64) if h==0 else (l>=64)

def fwd_body(plan, C, q, ks, vs, qa, kas, o_ref, p_ref):
    n=0
    kaug=[[jnp.where(half_mask(k.shape,h),k,a) for k,a in zip(ks,kas)] for h in range(2)]
    vts=[v.T for v in vs]
    for slot,blocks in enumerate(plan):
        halves=[]
        for h in range(2):
            qs=q[slot*C:(slot+1)*C]; qas=qa[slot*C:(slot+1)*C]
            qh=jnp.where(half_mask(qs.shape,h),qs,qas)
            ss=[]
            for (kb,diag) in blocks:
                s=nt(kaug[h][kb],qh)
                if diag:
                    ki=lax.broadcasted_iota(jnp.int32,s.shape,0); qi=lax.broadcasted_iota(jnp.int32,s.shape,1)
                    s=jnp.where(ki<=qi,s,NEG)
                ss.append(s)
            m=functools.reduce(jnp.maximum,[jnp.max(s,axis=0,keepdims=True) for s in ss])
            ps=[jnp.exp2(s-m) for s in ss]
            l=functools.reduce(jnp.add,[jnp.sum(p,axis=0,keepdims=True) for p in ps])
            inv=1.0/l
            acc=None
            for i,((kb,_),p) in enumerate(zip(blocks,ps)):
                pb=(p*inv).astype(BF)
                p_ref[0,h,n+i]=pb
                t=nn(vts[kb][64*h:64*h+64],pb)
                acc=t if acc is None else acc+t
            halves.append(acc)
        n+=len(blocks)
        ot=jnp.concatenate(halves,axis=0)
        o_ref[slot*C:(slot+1)*C]=ot.T.astype(BF)

def fwd_kernel(plans, C, info, q_ref, ko, kp, vo, vp, qa, kao, kap, o_ref, p_ref):
    def run(plan):
        ks=[ko[0:C],ko[C:2*C],kp[0:C],kp[C:2*C]]
        vs=[vo[0:C],vo[C:2*C],vp[0:C],vp[C:2*C]]
        kas=[kao[0:C],kao[C:2*C],kap[0:C],kap[C:2*C]]
        fwd_body(plan,C,q_ref[...],ks,vs,qa[...],kas,o_ref,p_ref)
    if len(plans)==1: run(plans[0])
    else:
        for v,plan in enumerate(plans):
            pl.when(info[0]==v)(functools.partial(run,plan))

def attend(plans, info, q, ko, kp, vo, vp, qa, kao, kap):
    T,D=q.shape; C=T//2; pairs=D//128
    nb=sum(len(b) for b in plans[0])
    col=pl.BlockSpec((T,128),lambda h,*_:(0,h))
    fix=pl.BlockSpec((T,128),lambda h,*_:(0,0))
    return pl.pallas_call(
        functools.partial(fwd_kernel,plans,C),
        grid_spec=pltpu.PrefetchScalarGridSpec(num_scalar_prefetch=1,grid=(pairs,),
            in_specs=[col]*5+[fix]*3,
            out_specs=[col,pl.BlockSpec((1,2,nb,C,C),lambda h,*_:(h,0,0,0,0))]),
        out_shape=[jax.ShapeDtypeStruct((T,D),BF),jax.ShapeDtypeStruct((pairs,2,nb,C,C),BF)],
        compiler_params=pltpu.CompilerParams(vmem_limit_bytes=VM),
        cost_estimate=pl.CostEstimate(flops=2*2*nb*C*C*64*2*pairs*4,bytes_accessed=pairs*2*nb*C*C*2,transcendentals=0),
        name="attend")(info,q,ko,kp,vo,vp,qa,kao,kap)

def bwd_body(plan, C, q, ks, vs, do, o, p_ref, gq_ref, gko, gvo, gkp, gvp):
    lane=lax.broadcasted_iota(jnp.int32,(C,128),1)
    l64=lax.rem(lane,64)
    ones=jnp.where(l64<2,1.0,0.0).astype(BF)
    vaug=[[jnp.where(half_mask(v.shape,h),v,ones) for v in vs] for h in range(2)]
    kts=[k.T for k in ks]
    gk=[None]*4; gv=[None]*4
    n=0
    zero=jnp.zeros((C,128),BF)
    for slot,blocks in enumerate(plan):
        halves=[]
        for h in range(2):
            hm=lane<64 if h==0 else lane>=64
            dos=do[slot*C:(slot+1)*C]; os=o[slot*C:(slot+1)*C]; qs=q[slot*C:(slot+1)*C]
            prod=jnp.where(hm,dos.astype(F32)*os.astype(F32),0.0)
            d=-jnp.sum(prod,axis=1,keepdims=True)
            hi=d.astype(BF); lo=(d-hi.astype(F32)).astype(BF)
            doa=jnp.where(hm,dos,jnp.where(l64==0,jnp.broadcast_to(hi,(C,128)),jnp.where(l64==1,jnp.broadcast_to(lo,(C,128)),zero)))
            dom=jnp.where(hm,dos,zero)
            qm=jnp.where(hm,qs,zero)
            acc=None
            for i,(kb,_) in enumerate(blocks):
                pb=p_ref[0,h,n+i]
                dp=nt(vaug[h][kb],doa)
                ds=(pb.astype(F32)*dp).astype(BF)
                a=nn(pb,dom); gv[kb]=a if gv[kb] is None else gv[kb]+a
                b=nn(ds,qm); gk[kb]=b if gk[kb] is None else gk[kb]+b
                t=nn(kts[kb][64*h:64*h+64],ds)
                acc=t if acc is None else acc+t
            halves.append(acc)
        n+=len(blocks)
        gq_ref[slot*C:(slot+1)*C]=jnp.concatenate(halves,axis=0).T.astype(BF)
    for kb in range(4):
        rk,rv=(gko,gvo) if kb<2 else (gkp,gvp)
        sl=slice((kb%2)*C,(kb%2)*C+C)
        z=jnp.zeros((C,128),F32)
        rk[sl]=((gk[kb] if gk[kb] is not None else z)*(1.0/LOG2E)).astype(rk.dtype)
        rv[sl]=(gv[kb] if gv[kb] is not None else z).astype(rv.dtype)

def bwd_kernel(plans, C, info, q_ref, ko, kp, vo, vp, do, o, p_ref, gq, gko, gvo, gkp, gvp):
    def run(plan):
        ks=[ko[0:C],ko[C:2*C],kp[0:C],kp[C:2*C]]
        vs=[vo[0:C],vo[C:2*C],vp[0:C],vp[C:2*C]]
        bwd_body(plan,C,q_ref[...],ks,vs,do[...],o[...],p_ref,gq,gko,gvo,gkp,gvp)
    if len(plans)==1: run(plans[0])
    else:
        for v,plan in enumerate(plans):
            pl.when(info[0]==v)(functools.partial(run,plan))

def attend_back(plans, info, q, ko, kp, vo, vp, do, o, p):
    T,D=q.shape; C=T//2; pairs=D//128
    nb=p.shape[2]
    col=pl.BlockSpec((T,128),lambda h,*_:(0,h))
    return pl.pallas_call(
        functools.partial(bwd_kernel,plans,C),
        grid_spec=pltpu.PrefetchScalarGridSpec(num_scalar_prefetch=1,grid=(pairs,),
            in_specs=[col]*7+[pl.BlockSpec((1,2,nb,C,C),lambda h,*_:(h,0,0,0,0))],
            out_specs=[col]*5),
        out_shape=[jax.ShapeDtypeStruct((T,D),BF),jax.ShapeDtypeStruct((T,D),F32),jax.ShapeDtypeStruct((T,D),F32),
                   jax.ShapeDtypeStruct((T,D),BF),jax.ShapeDtypeStruct((T,D),BF)],
        compiler_params=pltpu.CompilerParams(vmem_limit_bytes=VM),
        cost_estimate=pl.CostEstimate(flops=2*4*nb*C*C*64*2*pairs*4,bytes_accessed=pairs*2*nb*C*C*2,transcendentals=0),
        name="attend_back")(info,q,ko,kp,vo,vp,do,o,p)


def product(left, right):
    return jnp.dot(left, right, preferred_element_type=F32)


def normalize(values):
    centered = values - jnp.mean(values, axis=-1, keepdims=True)
    spread = jnp.mean(centered * centered, axis=-1, keepdims=True)
    return centered * lax.rsqrt(spread + 1e-05)


def smooth(values):
    return jax.nn.gelu(values, approximate=False)


def normalize_back(values, grads):
    return jax.vjp(normalize, values)[1](grads)[0]


def smooth_back(values, grads):
    return jax.vjp(smooth, values)[1](grads)[0]


def move(value, target):
    dp, seq = lax.axis_size("dp"), lax.axis_size("seq")
    pairs = []
    for d in range(dp):
        for s in range(seq):
            a, b = target(d, s)
            pairs.append((d * seq + s, a * seq + b))
    return lax.ppermute(value, ("dp", "seq"), pairs)


def flip(value, bit):
    return move(value, lambda d, s: (d ^ bit, s))


def core_of(chunk):
    return (0, 1, 1, 0)[chunk]


def pick(flag, first, second):
    return jnp.where(flag, first, second)


def reshard_in(value, d, s):
    got = []
    for k in range(2):
        piece = lax.dynamic_index_in_dim(value, (s + k) % 2, 0, keepdims=False)
        got.append(
            move(piece, lambda a, q: (2 * (a // 2) + core_of(q), 2 * (a % 2) + (q + k) % 2))
        )
    even = (s + d) % 2 == 0
    return jnp.concatenate([pick(even, got[0], got[1]), pick(even, got[1], got[0])], axis=0)


def reshard_out(value, d, s):
    C = value.shape[0] // 2
    dp, seq = lax.axis_size("dp"), lax.axis_size("seq")
    got = []
    for k in range(2):
        slot = (s + k + d) % 2
        piece = lax.dynamic_slice_in_dim(value, slot * C, C, 0)
        back = {}
        for a in range(dp):
            for q in range(seq):
                back[(2 * (a // 2) + core_of(q), 2 * (a % 2) + (q + k) % 2)] = (a, q)
        got.append(move(piece, lambda a, b: back[(a, b)]))
    even = s % 2 == 0
    return jnp.stack([pick(even, got[0], got[1]), pick(even, got[1], got[0])])


def spread_pieces(shard, low, order):
    b1, b2 = order
    pieces = {0: shard}
    pieces[b1] = flip(shard, b1 * low)
    for m in (0, b1):
        pieces[m ^ b2] = flip(pieces[m], b2 * low)
    for m in (0, b1, b2, b1 ^ b2):
        pieces[m ^ 1] = flip(pieces[m], low)
    return [pieces[m] for m in range(8)]


def assemble_kernel(parts, n_in, info, *refs):
    ins, rest = refs[:n_in], refs[n_in:]
    outs, sem = rest[:-1], rest[-1]
    copies = []
    for which, src, rows, out, stride, base in parts:
        for m in range(8):
            owner = info[1] ^ m
            at = pl.multiple_of(owner * stride + base, 16)
            copies.append(
                pltpu.make_async_copy(
                    ins[which * 8 + m].at[pl.ds(src, rows)],
                    outs[out].at[pl.ds(at, rows)],
                    sem.at[len(copies)],
                )
            )
    for c in copies:
        c.start()
    for c in copies:
        c.wait()


def assemble(info, sets, parts, shapes):
    flat = [p for s in sets for p in s]
    return pl.pallas_call(
        functools.partial(assemble_kernel, parts, len(flat)),
        grid_spec=pltpu.PrefetchScalarGridSpec(
            num_scalar_prefetch=1,
            grid=(1,),
            in_specs=[pl.BlockSpec(memory_space=pl.ANY)] * len(flat),
            out_specs=[pl.BlockSpec(memory_space=pl.ANY)] * len(shapes),
            scratch_shapes=[pltpu.SemaphoreType.DMA((len(parts) * 8,))],
        ),
        out_shape=[jax.ShapeDtypeStruct(s, BF) for s in shapes],
        name="assemble",
    )(info, *flat)


def reduce_all(value, d, s, steps):
    def other(v, step):
        axis, bit = step
        if axis == "dp":
            return move(v, lambda a, b: (a ^ bit, b))
        return move(v, lambda a, b: (a, b ^ bit))

    def high(step):
        axis, bit = step
        return ((d if axis == "dp" else s) // bit) % 2 == 1

    for step in steps:
        half = value.shape[0] // 2
        up = high(step)
        lo, hi = value[:half], value[half:]
        sent = pick(up, lo, hi).astype(BF)
        kept = pick(up, hi, lo)
        value = kept.astype(F32) + other(sent, step).astype(F32)
    value = value.astype(BF)
    for step in reversed(steps):
        up = high(step)
        got = other(value, step)
        value = jnp.concatenate([pick(up, got, value), pick(up, value, got)], axis=0)
    return value.astype(F32)


def local(tokens, source, target_lengths, source_lengths, step_index, self_query, self_key, self_value,
          self_out, cross_query, cross_key, cross_value, cross_out, ffn_expand, ffn_contract, adapter_down,
          adapter_up, grad_output):
    rows, C, D = tokens.shape
    dp, seq = lax.axis_size("dp"), lax.axis_size("seq")
    assert rows == 2 and seq == 4 and dp % 8 == 0
    low = dp // 8
    d, s = lax.axis_index("dp"), lax.axis_index("seq")
    core = d % 2
    info = jnp.stack([core, d // low]).astype(jnp.int32)

    x = reshard_in(tokens, d, s)

    def widen(shard):
        if low == 1:
            return shard
        groups = [[g * low + i for i in range(low)] for g in range(8)]
        return lax.all_gather(shard, "dp", axis=0, tiled=True, axis_index_groups=groups)

    def two(a, b):
        return jnp.concatenate([a, b], axis=0)

    wide = [widen(w) for w in (self_query, self_key, self_value, self_out, cross_query, cross_key,
                               cross_value, cross_out, ffn_expand, ffn_contract)]
    sq, sk, sv, so, cq_, ck_, cv_, co_, ex, con = wide
    n = sq.shape[0]
    f = con.shape[0]
    XY, YX = (2, 4), (4, 2)
    a1 = spread_pieces(two(sq, sv), low, XY)
    b1 = spread_pieces(two(sk, ck_), low, YX)
    a2 = spread_pieces(two(so, cv_), low, XY)
    b2 = spread_pieces(two(cq_, co_), low, YX)
    a3 = spread_pieces(ex[: n // 2], low, XY)
    b3 = spread_pieces(ex[n // 2 :], low, YX)
    a4 = spread_pieces(con[: f // 2], low, XY)
    b4 = spread_pieces(con[f // 2 :], low, YX)
    four = ((0, 0, n, 0, n, 0), (0, n, n, 1, n, 0), (1, 0, n, 2, n, 0), (1, n, n, 3, n, 0))
    w_query, w_value, w_key, c_key = assemble(info, [a1, b1], four, [(D, D)] * 4)
    w_out, c_value, c_query, c_out = assemble(info, [a2, b2], four, [(D, D)] * 4)
    FF = ex.shape[1]
    (w_expand,) = assemble(info, [a3, b3], ((0, 0, n // 2, 0, n, 0), (1, 0, n // 2, 0, n, n // 2)), [(D, FF)])
    (w_contract,) = assemble(info, [a4, b4], ((0, 0, f // 2, 0, f, 0), (1, 0, f // 2, 0, f, f // 2)), [(FF, D)])
    src = reshard_in(source, d, s)
    g_out = reshard_in(grad_output, d, s)

    mine = jnp.concatenate([target_lengths, source_lengths[:, None]], axis=1)
    other = flip(mine, 1)
    table = jnp.concatenate([pick(core == 0, mine, other), pick(core == 0, other, mine)], axis=0)
    row = lax.dynamic_index_in_dim(table, s, 0, keepdims=False)
    lens, src_len = row[:-1], row[-1]
    docs = lens.shape[0]
    ends = jnp.cumsum(lens)[:-1]
    i = jnp.arange(2 * C, dtype=jnp.int32)
    slot = i // C

    def place(which):
        chunk = pick(which == 0, slot * 3, slot + 1)
        return chunk * C + i % C

    lanes = jnp.arange(128, dtype=jnp.int32) % 64

    def doc_hot(pos):
        doc = jnp.sum((pos[:, None] >= ends[None, :]).astype(jnp.int32), axis=-1)
        return doc[:, None] == lanes[None, :]

    own_pos, peer_pos = place(core), place(1 - core)
    k_aug = [doc_hot(own_pos).astype(BF), doc_hot(peer_pos).astype(BF)]
    q_aug = jnp.where(doc_hot(own_pos) | (lanes >= docs)[None, :], 0.0, NEG).astype(BF)
    ck_aug = [((pos[:, None] >= src_len) & (lanes == 0)[None, :]).astype(BF) for pos in (own_pos, peer_pos)]
    cq_aug = jnp.broadcast_to(jnp.where(lanes == 0, NEG, 0.0).astype(BF)[None, :], (2 * C, 128))

    scale = 0.125 * LOG2E
    branch_scale = (step_index[0] + 1).astype(F32) / 5.0
    q = (product(x, w_query) * scale).astype(BF)
    k = product(x, w_key).astype(BF)
    v = product(x, w_value).astype(BF)
    k_peer, v_peer = flip(k, 1), flip(v, 1)
    ck = product(src, c_key).astype(BF)
    cv = product(src, c_value).astype(BF)
    ck_peer, cv_peer = flip(ck, 1), flip(cv, 1)
    attended, p_self = attend(SELF_PLANS, info, q, k, k_peer, v, v_peer, q_aug, *k_aug)
    first_sum = x.astype(F32) + product(attended, w_out)
    first_norm = normalize(first_sum)
    cq = (product(first_norm.astype(BF), c_query) * scale).astype(BF)
    cross_attended, p_cross = attend(CROSS_PLANS, info, cq, ck, ck_peer, cv, cv_peer, cq_aug, *ck_aug)
    second_sum = first_norm + product(cross_attended, c_out)
    second_norm = normalize(second_sum)
    second_low = second_norm.astype(BF)
    hidden_pre = product(second_low, w_expand)
    hidden = smooth(hidden_pre).astype(BF)
    narrow = product(second_low, adapter_down)
    squeezed = smooth(narrow).astype(BF)
    third_sum = second_norm + product(hidden, w_contract) + branch_scale * product(squeezed, adapter_up)
    output = normalize(third_sum).astype(BF)
    output = reshard_out(output, d, s)
    grad_third = normalize_back(third_sum, g_out.astype(F32))
    grad_ffn = grad_third.astype(BF)
    grad_adapt = (branch_scale * grad_third).astype(BF)
    grad_up = product(squeezed.T, grad_adapt)
    grad_narrow = smooth_back(narrow, product(grad_adapt, adapter_up.T)).astype(BF)
    grad_down = product(second_low.T, grad_narrow)
    last = [("seq", 2), ("seq", 1)] + [("dp", 1 << j) for j in range(low.bit_length() - 1)]
    grad_up = reduce_all(grad_up, d, s, [("dp", low), ("dp", 2 * low), ("dp", 4 * low)] + last)
    grad_down = reduce_all(grad_down, d, s, [("dp", low), ("dp", 4 * low), ("dp", 2 * low)] + last)
    grad_hidden = smooth_back(hidden_pre, product(grad_ffn, w_contract.T)).astype(BF)
    grad_second = grad_third + product(grad_hidden, w_expand.T) + product(grad_narrow, adapter_down.T)
    grad_second_sum = normalize_back(second_sum, grad_second)
    grad_cross = product(grad_second_sum.astype(BF), c_out.T).astype(BF)
    gq, gk, gv, gk_peer, gv_peer = attend_back(
        CROSS_PLANS, info, cq, ck, ck_peer, cv, cv_peer, grad_cross, cross_attended, p_cross
    )
    gk = (gk + flip(gk_peer, 1).astype(F32)).astype(BF)
    gv = (gv + flip(gv_peer, 1).astype(F32)).astype(BF)
    grad_source = (product(gk, c_key.T) + product(gv, c_value.T)).astype(BF)
    grad_source = reshard_out(grad_source, d, s)
    grad_first = grad_second_sum + 0.125 * product(gq, c_query.T)
    grad_first_sum = normalize_back(first_sum, grad_first)
    grad_self = product(grad_first_sum.astype(BF), w_out.T).astype(BF)
    gq, gk, gv, gk_peer, gv_peer = attend_back(
        SELF_PLANS, info, q, k, k_peer, v, v_peer, grad_self, attended, p_self
    )
    gk = (gk + flip(gk_peer, 1).astype(F32)).astype(BF)
    gv = (gv + flip(gv_peer, 1).astype(F32)).astype(BF)
    grad_tokens = grad_first_sum + 0.125 * product(gq, w_query.T) + product(gk, w_key.T) + product(gv, w_value.T)
    grad_tokens = reshard_out(grad_tokens.astype(BF), d, s)
    return (output, grad_tokens, grad_source, grad_down, grad_up)


def solution(mesh):
    rows = P("dp", "seq", None)
    weight = P("dp", None)
    return jax.shard_map(
        local,
        mesh=mesh,
        in_specs=(rows, rows, weight, P("dp"), P()) + (weight,) * 10 + (P(), P(), rows),
        out_specs=(rows, rows, rows, P(), P()),
        check_vma=False,
    )
```

```python
import functools
import jax
import jax.numpy as jnp
from jax.sharding import PartitionSpec as P
from jax import lax
from jax.experimental import pallas as pl
from jax.experimental.pallas import tpu as pltpu
BF=jnp.bfloat16; F32=jnp.float32
NEG=-1e30
LOG2E=1.4426950408889634
VM=56*1024*1024

SELF_PLANS=(((((0,True),)), ((0,False),(2,False),(3,False),(1,True))),
            (((2,False),(0,True)), ((2,False),(0,False),(1,True))))
CROSS_PLANS=((((0,False),(1,False),(2,False),(3,False)),)*2,)

def nt(a,b): return lax.dot_general(a,b,(((1,),(1,)),((),())),preferred_element_type=F32)
def nn(a,b): return lax.dot_general(a,b,(((1,),(0,)),((),())),preferred_element_type=F32)

def half_mask(shape, h):
    l=lax.broadcasted_iota(jnp.int32, shape, 1)
    return (l<64) if h==0 else (l>=64)

def fwd_body(plan, C, q, ks, vs, qa, kas, o_ref, p_ref):
    n=0
    kaug=[[jnp.where(half_mask(k.shape,h),k,a) for k,a in zip(ks,kas)] for h in range(2)]
    vts=[v.T for v in vs]
    for slot,blocks in enumerate(plan):
        halves=[]
        for h in range(2):
            qs=q[slot*C:(slot+1)*C]; qas=qa[slot*C:(slot+1)*C]
            qh=jnp.where(half_mask(qs.shape,h),qs,qas)
            ss=[]
            for (kb,diag) in blocks:
                s=nt(kaug[h][kb],qh)
                if diag:
                    ki=lax.broadcasted_iota(jnp.int32,s.shape,0); qi=lax.broadcasted_iota(jnp.int32,s.shape,1)
                    s=jnp.where(ki<=qi,s,NEG)
                ss.append(s)
            m=functools.reduce(jnp.maximum,[jnp.max(s,axis=0,keepdims=True) for s in ss])
            ps=[jnp.exp2(s-m) for s in ss]
            l=functools.reduce(jnp.add,[jnp.sum(p,axis=0,keepdims=True) for p in ps])
            inv=1.0/l
            acc=None
            for i,((kb,_),p) in enumerate(zip(blocks,ps)):
                pb=(p*inv).astype(BF)
                p_ref[0,h,n+i]=pb
                t=nn(vts[kb][64*h:64*h+64],pb)
                acc=t if acc is None else acc+t
            halves.append(acc)
        n+=len(blocks)
        ot=jnp.concatenate(halves,axis=0)
        o_ref[slot*C:(slot+1)*C]=ot.T.astype(BF)

def fwd_kernel(plans, C, info, q_ref, ko, kp, vo, vp, qa, kao, kap, o_ref, p_ref):
    def run(plan):
        ks=[ko[0:C],ko[C:2*C],kp[0:C],kp[C:2*C]]
        vs=[vo[0:C],vo[C:2*C],vp[0:C],vp[C:2*C]]
        kas=[kao[0:C],kao[C:2*C],kap[0:C],kap[C:2*C]]
        fwd_body(plan,C,q_ref[...],ks,vs,qa[...],kas,o_ref,p_ref)
    if len(plans)==1: run(plans[0])
    else:
        for v,plan in enumerate(plans):
            pl.when(info[0]==v)(functools.partial(run,plan))

def attend(plans, info, q, ko, kp, vo, vp, qa, kao, kap):
    T,D=q.shape; C=T//2; pairs=D//128
    nb=sum(len(b) for b in plans[0])
    col=pl.BlockSpec((T,128),lambda h,*_:(0,h))
    fix=pl.BlockSpec((T,128),lambda h,*_:(0,0))
    return pl.pallas_call(
        functools.partial(fwd_kernel,plans,C),
        grid_spec=pltpu.PrefetchScalarGridSpec(num_scalar_prefetch=1,grid=(pairs,),
            in_specs=[col]*5+[fix]*3,
            out_specs=[col,pl.BlockSpec((1,2,nb,C,C),lambda h,*_:(h,0,0,0,0))]),
        out_shape=[jax.ShapeDtypeStruct((T,D),BF),jax.ShapeDtypeStruct((pairs,2,nb,C,C),BF)],
        compiler_params=pltpu.CompilerParams(vmem_limit_bytes=VM),
        cost_estimate=pl.CostEstimate(flops=2*2*nb*C*C*64*2*pairs*4,bytes_accessed=pairs*2*nb*C*C*2,transcendentals=0),
        name="attend")(info,q,ko,kp,vo,vp,qa,kao,kap)

def bwd_body(plan, C, q, ks, vs, do, o, p_ref, gq_ref, gko, gvo, gkp, gvp):
    lane=lax.broadcasted_iota(jnp.int32,(C,128),1)
    l64=lax.rem(lane,64)
    ones=jnp.where(l64<2,1.0,0.0).astype(BF)
    vaug=[[jnp.where(half_mask(v.shape,h),v,ones) for v in vs] for h in range(2)]
    kts=[k.T for k in ks]
    gk=[None]*4; gv=[None]*4
    n=0
    zero=jnp.zeros((C,128),BF)
    for slot,blocks in enumerate(plan):
        halves=[]
        for h in range(2):
            hm=lane<64 if h==0 else lane>=64
            dos=do[slot*C:(slot+1)*C]; os=o[slot*C:(slot+1)*C]; qs=q[slot*C:(slot+1)*C]
            prod=jnp.where(hm,dos.astype(F32)*os.astype(F32),0.0)
            d=-jnp.sum(prod,axis=1,keepdims=True)
            hi=d.astype(BF); lo=(d-hi.astype(F32)).astype(BF)
            doa=jnp.where(hm,dos,jnp.where(l64==0,jnp.broadcast_to(hi,(C,128)),jnp.where(l64==1,jnp.broadcast_to(lo,(C,128)),zero)))
            dom=jnp.where(hm,dos,zero)
            qm=jnp.where(hm,qs,zero)
            acc=None
            for i,(kb,_) in enumerate(blocks):
                pb=p_ref[0,h,n+i]
                dp=nt(vaug[h][kb],doa)
                ds=(pb.astype(F32)*dp).astype(BF)
                a=nn(pb,dom); gv[kb]=a if gv[kb] is None else gv[kb]+a
                b=nn(ds,qm); gk[kb]=b if gk[kb] is None else gk[kb]+b
                t=nn(kts[kb][64*h:64*h+64],ds)
                acc=t if acc is None else acc+t
            halves.append(acc)
        n+=len(blocks)
        gq_ref[slot*C:(slot+1)*C]=jnp.concatenate(halves,axis=0).T.astype(BF)
    for kb in range(4):
        rk,rv=(gko,gvo) if kb<2 else (gkp,gvp)
        sl=slice((kb%2)*C,(kb%2)*C+C)
        z=jnp.zeros((C,128),F32)
        rk[sl]=((gk[kb] if gk[kb] is not None else z)*(1.0/LOG2E)).astype(rk.dtype)
        rv[sl]=(gv[kb] if gv[kb] is not None else z).astype(rv.dtype)

def bwd_kernel(plans, C, info, q_ref, ko, kp, vo, vp, do, o, p_ref, gq, gko, gvo, gkp, gvp):
    def run(plan):
        ks=[ko[0:C],ko[C:2*C],kp[0:C],kp[C:2*C]]
        vs=[vo[0:C],vo[C:2*C],vp[0:C],vp[C:2*C]]
        bwd_body(plan,C,q_ref[...],ks,vs,do[...],o[...],p_ref,gq,gko,gvo,gkp,gvp)
    if len(plans)==1: run(plans[0])
    else:
        for v,plan in enumerate(plans):
            pl.when(info[0]==v)(functools.partial(run,plan))

def attend_back(plans, info, q, ko, kp, vo, vp, do, o, p):
    T,D=q.shape; C=T//2; pairs=D//128
    nb=p.shape[2]
    col=pl.BlockSpec((T,128),lambda h,*_:(0,h))
    return pl.pallas_call(
        functools.partial(bwd_kernel,plans,C),
        grid_spec=pltpu.PrefetchScalarGridSpec(num_scalar_prefetch=1,grid=(pairs,),
            in_specs=[col]*7+[pl.BlockSpec((1,2,nb,C,C),lambda h,*_:(h,0,0,0,0))],
            out_specs=[col]*5),
        out_shape=[jax.ShapeDtypeStruct((T,D),BF),jax.ShapeDtypeStruct((T,D),F32),jax.ShapeDtypeStruct((T,D),F32),
                   jax.ShapeDtypeStruct((T,D),BF),jax.ShapeDtypeStruct((T,D),BF)],
        compiler_params=pltpu.CompilerParams(vmem_limit_bytes=VM),
        cost_estimate=pl.CostEstimate(flops=2*4*nb*C*C*64*2*pairs*4,bytes_accessed=pairs*2*nb*C*C*2,transcendentals=0),
        name="attend_back")(info,q,ko,kp,vo,vp,do,o,p)


def vmem(mib):
    return pltpu.CompilerParams(vmem_limit_bytes=mib * 1024 * 1024)


class Piece:
    def __init__(self, parts, at, rows):
        self.parts, self.at, self.rows = parts, at, rows


def fused(name, info, body, loads, outs, mib=48, flops=0):
    flat, plan, scratch = [], [], []
    seen = {}

    def arg(a):
        if id(a) not in seen:
            seen[id(a)] = len(flat)
            flat.append(a)
        return seen[id(a)]

    count = 0
    for load in loads:
        if isinstance(load, Piece):
            plan.append((count, load.at, load.rows, [arg(p) for p in load.parts]))
            scratch.append(pltpu.VMEM((8 * load.rows, load.parts[0].shape[1]), load.parts[0].dtype))
            count += 8
        else:
            plan.append((count, None, None, [arg(load)]))
            scratch.append(pltpu.VMEM(load.shape, load.dtype))
            count += 1
    nout = len(outs)

    def kernel(info_ref, *refs):
        ins, out_refs = refs[: len(flat)], refs[len(flat) : len(flat) + nout]
        bufs, sem = refs[len(flat) + nout : -1], refs[-1]
        started = []
        for (first, at, rows, args), buf in zip(plan, bufs):
            copies = []
            if at is None:
                copies.append(pltpu.make_async_copy(ins[args[0]], buf, sem.at[first]))
            else:
                for m in range(8):
                    owner = info_ref[1] ^ m
                    to = pl.multiple_of(owner * rows, 16)
                    copies.append(
                        pltpu.make_async_copy(
                            ins[args[m]].at[pl.ds(at, rows)], buf.at[pl.ds(to, rows)], sem.at[first + m]
                        )
                    )
            for c in copies:
                c.start()
            started.append(copies)
        ready = set()

        def get(i):
            if i not in ready:
                for c in started[i]:
                    c.wait()
                ready.add(i)
            return bufs[i]

        body(info_ref, get, *out_refs)

    return pl.pallas_call(
        kernel,
        grid_spec=pltpu.PrefetchScalarGridSpec(
            num_scalar_prefetch=1,
            grid=(1,),
            in_specs=[pl.BlockSpec(memory_space=pl.ANY)] * len(flat),
            out_specs=[pl.BlockSpec(o.shape, lambda i, *_: (0, 0)) for o in outs],
            scratch_shapes=scratch + [pltpu.SemaphoreType.DMA((count,))],
        ),
        out_shape=list(outs),
        compiler_params=vmem(mib),
        cost_estimate=pl.CostEstimate(flops=flops, bytes_accessed=sum(a.size * a.dtype.itemsize for a in flat), transcendentals=0),
        name=name,
    )(info, *flat)


def gather_pieces(info, piece):
    def body(info_ref, get, out):
        out[...] = get(0)[...]

    rows = 8 * piece.rows
    return fused("whole", info, body, [piece], [shape(rows, piece.parts[0].shape[1], piece.parts[0].dtype)])[0]


def shape(rows, cols, dtype):
    return jax.ShapeDtypeStruct((rows, cols), dtype)


def norm_parts(v):
    mean = jnp.mean(v, axis=-1, keepdims=True)
    c = v - mean
    inv = lax.rsqrt(jnp.mean(c * c, axis=-1, keepdims=True) + 1e-05)
    return c * inv, inv


def norm_back(y, inv, g):
    return inv * (g - jnp.mean(g, axis=-1, keepdims=True) - y * jnp.mean(g * y, axis=-1, keepdims=True))


def gelu_pair(v):
    phi = 0.5 + 0.5 * lax.erf(v * 0.7071067811865476)
    pdf = jnp.exp(v * v * -0.5) * 0.3989422804014327
    return v * phi, phi + v * pdf


def tn(a, b):
    return lax.dot_general(a, b, (((0,), (0,)), ((), ())), preferred_element_type=F32)


GMAC = 512 * 1024 * 1024 * 2


def project_qkv(info, x, a1, b1, n):
    T, D = x.shape

    def body(info_ref, get, q, k, v):
        xv = get(0)[...]
        q[...] = (nn(xv, get(1)[...]) * (0.125 * LOG2E)).astype(BF)
        k[...] = nn(xv, get(2)[...]).astype(BF)
        v[...] = nn(xv, get(3)[...]).astype(BF)

    return fused("qkv", info, body, [x, Piece(a1, 0, n), Piece(b1, 0, n), Piece(b1, n, n)],
                 [shape(T, D, BF)] * 3, flops=3 * GMAC)


def project_source(info, x, key, value):
    T, D = x.shape

    def body(info_ref, get, k, v):
        xv = get(0)[...]
        k[...] = nn(xv, get(1)[...]).astype(BF)
        v[...] = nn(xv, get(2)[...]).astype(BF)

    return fused("source_kv", info, body, [x, key, value], [shape(T, D, BF)] * 2, flops=2 * GMAC)


def after_self(info, x, att, w_out, c_query):
    T, D = x.shape

    def body(info_ref, get, y_ref, inv_ref, cq_ref):
        y, inv = norm_parts(get(0)[...].astype(F32) + nn(get(1)[...], get(2)[...]))
        y_ref[...] = y
        inv_ref[...] = jnp.broadcast_to(inv, inv_ref.shape)
        cq_ref[...] = (nn(y.astype(BF), get(3)[...]) * (0.125 * LOG2E)).astype(BF)

    return fused("after_self", info, body, [x, att, w_out, c_query],
                 [shape(T, D, F32), shape(T, 128, F32), shape(T, D, BF)], flops=2 * GMAC)


def after_cross(info, y1, att, c_out, down, up, scale):
    T, D = y1.shape
    A = down.shape[1]

    def body(info_ref, get, y_ref, inv_ref, low_ref, sq_ref, gn_ref, base_ref):
        y, inv = norm_parts(get(0)[...] + nn(get(1)[...], get(2)[...]))
        y_ref[...] = y
        inv_ref[...] = jnp.broadcast_to(inv, inv_ref.shape)
        low = y.astype(BF)
        low_ref[...] = low
        h, g = gelu_pair(nn(low, get(3)[...]))
        hb = h.astype(BF)
        sq_ref[...] = hb
        gn_ref[...] = g.astype(BF)
        base_ref[...] = y + get(5)[0:1, 0:1] * nn(hb, get(4)[...])

    return fused("after_cross", info, body, [y1, att, c_out, down, up, scale],
                 [shape(T, D, F32), shape(T, 128, F32), shape(T, D, BF), shape(T, A, BF), shape(T, A, BF),
                  shape(T, D, F32)], flops=2 * GMAC)


def expand_kernel(x, e, h_ref, g_ref):
    h, g = gelu_pair(nn(x[...], e[...]))
    h_ref[...] = h.astype(BF)
    g_ref[...] = g.astype(BF)


def expand(x, e, block=1024):
    T, D = x.shape
    F = e.shape[1]
    out = pl.BlockSpec((T, block), lambda i: (0, i))
    return pl.pallas_call(
        expand_kernel,
        grid=(F // block,),
        in_specs=[pl.BlockSpec((T, D), lambda i: (0, 0)), pl.BlockSpec((D, block), lambda i: (0, i))],
        out_specs=[out, out],
        out_shape=[shape(T, F, BF)] * 2,
        compiler_params=vmem(40),
        cost_estimate=pl.CostEstimate(flops=4 * GMAC, bytes_accessed=D * F * 2, transcendentals=0),
        name="expand",
    )(x, e)


def contract_kernel(h, c, base, low, sq, gn, up, g_out, scale, out_ref, g3_ref, gup_ref, gdown_ref, gnar_ref, acc):
    i = pl.program_id(0)

    @pl.when(i == 0)
    def _():
        acc[...] = base[...]

    acc[...] += nn(h[...], c[...])

    @pl.when(i == pl.num_programs(0) - 1)
    def _():
        y, inv = norm_parts(acc[...])
        out_ref[...] = y.astype(BF)
        g3 = norm_back(y, inv, g_out[...].astype(F32))
        g3_ref[...] = g3
        ga = (scale[0:1, 0:1] * g3).astype(BF)
        gup_ref[...] = tn(sq[...], ga)
        gnar = (gn[...].astype(F32) * nt(ga, up[...])).astype(BF)
        gnar_ref[...] = gnar
        gdown_ref[...] = tn(low[...], gnar)


def contract(h, c, base, low, sq, gn, up, g_out, scale, block=1024):
    T, D = base.shape
    F = c.shape[0]
    A = sq.shape[1]

    def whole(a):
        return pl.BlockSpec(a.shape, lambda i: (0, 0), pipeline_mode=pl.Buffered(1))

    outs = [shape(T, D, BF), shape(T, D, F32), shape(A, D, F32), shape(D, A, F32), shape(T, A, BF)]
    return pl.pallas_call(
        contract_kernel,
        grid=(F // block,),
        in_specs=[pl.BlockSpec((T, block), lambda i: (0, i)), pl.BlockSpec((block, D), lambda i: (i, 0))]
        + [whole(a) for a in (base, low, sq, gn, up, g_out, scale)],
        out_specs=[pl.BlockSpec(o.shape, lambda i: (0, 0)) for o in outs],
        out_shape=outs,
        scratch_shapes=[pltpu.VMEM((T, D), F32)],
        compiler_params=vmem(48),
        cost_estimate=pl.CostEstimate(flops=6 * GMAC, bytes_accessed=D * F * 2, transcendentals=0),
        name="contract",
    )(h, c, base, low, sq, gn, up, g_out, scale)


def ffn_back_kernel(g3, c, e, gp, gnar, down, y2, inv2, co, g2_ref, ga_ref, acc):
    i = pl.program_id(0)

    @pl.when(i == 0)
    def _():
        acc[...] = g3[...] + nt(gnar[...], down[...])

    gh = (nt(g3[...].astype(BF), c[...]) * gp[...].astype(F32)).astype(BF)
    acc[...] += nt(gh, e[...])

    @pl.when(i == pl.num_programs(0) - 1)
    def _():
        g2 = norm_back(y2[...], inv2[:, 0:1], acc[...])
        g2_ref[...] = g2
        ga_ref[...] = nt(g2.astype(BF), co[...]).astype(BF)


def ffn_back(g3, c, e, gp, gnar, down, y2, inv2, co, block=1024):
    T, D = g3.shape
    F = c.shape[0]

    def whole(a):
        return pl.BlockSpec(a.shape, lambda i: (0, 0), pipeline_mode=pl.Buffered(1))

    outs = [shape(T, D, F32), shape(T, D, BF)]
    return pl.pallas_call(
        ffn_back_kernel,
        grid=(F // block,),
        in_specs=[whole(g3), pl.BlockSpec((block, D), lambda i: (i, 0)), pl.BlockSpec((D, block), lambda i: (0, i)),
                  pl.BlockSpec((T, block), lambda i: (0, i))] + [whole(a) for a in (gnar, down, y2, inv2, co)],
        out_specs=[pl.BlockSpec(o.shape, lambda i: (0, 0)) for o in outs],
        out_shape=outs,
        scratch_shapes=[pltpu.VMEM((T, D), F32)],
        compiler_params=vmem(52),
        cost_estimate=pl.CostEstimate(flops=9 * GMAC, bytes_accessed=2 * D * F * 2, transcendentals=0),
        name="ffn_back",
    )(g3, c, e, gp, gnar, down, y2, inv2, co)


def before_self(info, g2, gq, y1, inv1, c_query, w_out):
    T, D = g2.shape

    def body(info_ref, get, g1_ref, ga_ref):
        g = get(0)[...] + 0.125 * nt(get(1)[...], get(2)[...])
        g1 = norm_back(get(3)[...], get(4)[:, 0:1], g)
        g1_ref[...] = g1
        ga_ref[...] = nt(g1.astype(BF), get(5)[...]).astype(BF)

    return fused("before_self", info, body, [g2, gq, c_query, y1, inv1, w_out],
                 [shape(T, D, F32), shape(T, D, BF)], flops=2 * GMAC)


def source_grad(info, gk, gk_got, gv, gv_got, key, value):
    T, D = gk.shape

    def body(info_ref, get, out):
        k = (get(0)[...] + get(1)[...].astype(F32)).astype(BF)
        v = (get(3)[...] + get(4)[...].astype(F32)).astype(BF)
        out[...] = (nt(k, get(2)[...]) + nt(v, get(5)[...])).astype(BF)

    return fused("source_grad", info, body, [gk, gk_got, key, gv, gv_got, value], [shape(T, D, BF)], flops=2 * GMAC)[0]


def token_grad(info, g1, gq, gk, gk_got, gv, gv_got, a1, b1, n):
    T, D = g1.shape

    def body(info_ref, get, out):
        acc = get(0)[...] + 0.125 * nt(get(1)[...], get(2)[...])
        k = (get(3)[...] + get(4)[...].astype(F32)).astype(BF)
        acc += nt(k, get(5)[...])
        v = (get(6)[...] + get(7)[...].astype(F32)).astype(BF)
        out[...] = (acc + nt(v, get(8)[...])).astype(BF)

    return fused("token_grad", info, body,
                 [g1, gq, Piece(a1, 0, n), gk, gk_got, Piece(b1, 0, n), gv, gv_got, Piece(b1, n, n)],
                 [shape(T, D, BF)], flops=3 * GMAC)[0]


def move(value, target):
    dp, seq = lax.axis_size("dp"), lax.axis_size("seq")
    pairs = []
    for d in range(dp):
        for s in range(seq):
            a, b = target(d, s)
            pairs.append((d * seq + s, a * seq + b))
    return lax.ppermute(value, ("dp", "seq"), pairs)


def flip(value, bit):
    return move(value, lambda d, s: (d ^ bit, s))


def core_of(chunk):
    return (0, 1, 1, 0)[chunk]


def pick(flag, first, second):
    return jnp.where(flag, first, second)


def reshard_in(value, d, s):
    got = []
    for k in range(2):
        piece = lax.dynamic_index_in_dim(value, (s + k) % 2, 0, keepdims=False)
        got.append(
            move(piece, lambda a, q: (2 * (a // 2) + core_of(q), 2 * (a % 2) + (q + k) % 2))
        )
    even = (s + d) % 2 == 0
    return jnp.concatenate([pick(even, got[0], got[1]), pick(even, got[1], got[0])], axis=0)


def reshard_out(value, d, s):
    C = value.shape[0] // 2
    dp, seq = lax.axis_size("dp"), lax.axis_size("seq")
    got = []
    for k in range(2):
        slot = (s + k + d) % 2
        piece = lax.dynamic_slice_in_dim(value, slot * C, C, 0)
        back = {}
        for a in range(dp):
            for q in range(seq):
                back[(2 * (a // 2) + core_of(q), 2 * (a % 2) + (q + k) % 2)] = (a, q)
        got.append(move(piece, lambda a, b: back[(a, b)]))
    even = s % 2 == 0
    return jnp.stack([pick(even, got[0], got[1]), pick(even, got[1], got[0])])


def spread_pieces(shard, low, order):
    b1, b2 = order
    pieces = {0: shard}
    pieces[b1] = flip(shard, b1 * low)
    for m in (0, b1):
        pieces[m ^ b2] = flip(pieces[m], b2 * low)
    for m in (0, b1, b2, b1 ^ b2):
        pieces[m ^ 1] = flip(pieces[m], low)
    return [pieces[m] for m in range(8)]


def reduce_all(value, d, s, steps):
    def other(v, step):
        axis, bit = step
        if axis == "dp":
            return move(v, lambda a, b: (a ^ bit, b))
        return move(v, lambda a, b: (a, b ^ bit))

    def high(step):
        axis, bit = step
        return ((d if axis == "dp" else s) // bit) % 2 == 1

    for step in steps:
        half = value.shape[0] // 2
        up = high(step)
        lo, hi = value[:half], value[half:]
        sent = pick(up, lo, hi).astype(BF)
        kept = pick(up, hi, lo)
        value = kept.astype(F32) + other(sent, step).astype(F32)
    value = value.astype(BF)
    for step in reversed(steps):
        up = high(step)
        got = other(value, step)
        value = jnp.concatenate([pick(up, got, value), pick(up, value, got)], axis=0)
    return value.astype(F32)


def local(tokens, source, target_lengths, source_lengths, step_index, self_query, self_key, self_value,
          self_out, cross_query, cross_key, cross_value, cross_out, ffn_expand, ffn_contract, adapter_down,
          adapter_up, grad_output):
    rows, C, D = tokens.shape
    dp, seq = lax.axis_size("dp"), lax.axis_size("seq")
    assert rows == 2 and seq == 4 and dp % 8 == 0
    low = dp // 8
    d, s = lax.axis_index("dp"), lax.axis_index("seq")
    core = d % 2
    info = jnp.stack([core, d // low]).astype(jnp.int32)

    x = reshard_in(tokens, d, s)

    def widen(shard):
        if low == 1:
            return shard
        groups = [[g * low + i for i in range(low)] for g in range(8)]
        return lax.all_gather(shard, "dp", axis=0, tiled=True, axis_index_groups=groups)

    def two(a, b):
        return jnp.concatenate([a, b], axis=0)

    wide = [widen(w) for w in (self_query, self_key, self_value, self_out, cross_query, cross_key,
                               cross_value, cross_out)]
    sq, sk, sv, so, cq_, ck_, cv_, co_ = wide
    n = sq.shape[0]
    XY, YX = (2, 4), (4, 2)
    a1 = spread_pieces(two(sq, ck_), low, XY)
    b1 = spread_pieces(two(sk, sv), low, YX)
    a2 = spread_pieces(two(so, cv_), low, XY)
    b2 = spread_pieces(two(cq_, co_), low, YX)
    w_expand = lax.all_gather(ffn_expand, "dp", axis=0, tiled=True)
    w_contract = lax.all_gather(ffn_contract, "dp", axis=0, tiled=True)
    src = reshard_in(source, d, s)
    g_out = reshard_in(grad_output, d, s)

    mine = jnp.concatenate([target_lengths, source_lengths[:, None]], axis=1)
    other = flip(mine, 1)
    table = jnp.concatenate([pick(core == 0, mine, other), pick(core == 0, other, mine)], axis=0)
    row = lax.dynamic_index_in_dim(table, s, 0, keepdims=False)
    lens, src_len = row[:-1], row[-1]
    docs = lens.shape[0]
    ends = jnp.cumsum(lens)[:-1]
    i = jnp.arange(2 * C, dtype=jnp.int32)
    slot = i // C

    def place(which):
        chunk = pick(which == 0, slot * 3, slot + 1)
        return chunk * C + i % C

    lanes = jnp.arange(128, dtype=jnp.int32) % 64

    def doc_hot(pos):
        doc = jnp.sum((pos[:, None] >= ends[None, :]).astype(jnp.int32), axis=-1)
        return doc[:, None] == lanes[None, :]

    own_pos, peer_pos = place(core), place(1 - core)
    k_aug = [doc_hot(own_pos).astype(BF), doc_hot(peer_pos).astype(BF)]
    q_aug = jnp.where(doc_hot(own_pos) | (lanes >= docs)[None, :], 0.0, NEG).astype(BF)
    ck_aug = [((pos[:, None] >= src_len) & (lanes == 0)[None, :]).astype(BF) for pos in (own_pos, peer_pos)]
    cq_aug = jnp.broadcast_to(jnp.where(lanes == 0, NEG, 0.0).astype(BF)[None, :], (2 * C, 128))

    scale = jnp.full((8, 128), (step_index[0] + 1).astype(F32) / 5.0, F32)
    q, k, v = project_qkv(info, x, a1, b1, n)
    k_peer, v_peer = flip(k, 1), flip(v, 1)
    attended, p_self = attend(SELF_PLANS, info, q, k, k_peer, v, v_peer, q_aug, *k_aug)
    ck, cv = project_source(info, src, Piece(a1, n, n), Piece(a2, n, n))
    ck_peer, cv_peer = flip(ck, 1), flip(cv, 1)
    y1, inv1, cq = after_self(info, x, attended, Piece(a2, 0, n), Piece(b2, 0, n))
    cross_attended, p_cross = attend(CROSS_PLANS, info, cq, ck, ck_peer, cv, cv_peer, cq_aug, *ck_aug)
    y2, inv2, second_low, squeezed, gn, base = after_cross(
        info, y1, cross_attended, Piece(b2, n, n), adapter_down, adapter_up, scale
    )
    hidden, gp = expand(second_low, w_expand)
    output, g3, grad_up, grad_down, gnar = contract(
        hidden, w_contract, base, second_low, squeezed, gn, adapter_up, g_out, scale
    )
    output = reshard_out(output, d, s)
    last = [("seq", 2), ("seq", 1)] + [("dp", 1 << j) for j in range(low.bit_length() - 1)]
    grad_up = reduce_all(grad_up, d, s, [("dp", low), ("dp", 2 * low), ("dp", 4 * low)] + last)
    grad_down = reduce_all(grad_down, d, s, [("dp", low), ("dp", 4 * low), ("dp", 2 * low)] + last)
    c_out = gather_pieces(info, Piece(b2, n, n))
    g2, grad_cross = ffn_back(g3, w_contract, w_expand, gp, gnar, adapter_down, y2, inv2, c_out)
    gq, gk, gv, gk_peer, gv_peer = attend_back(
        CROSS_PLANS, info, cq, ck, ck_peer, cv, cv_peer, grad_cross, cross_attended, p_cross
    )
    gk_got, gv_got = flip(gk_peer, 1), flip(gv_peer, 1)
    g1, grad_self = before_self(info, g2, gq, y1, inv1, Piece(b2, 0, n), Piece(a2, 0, n))
    grad_source = source_grad(info, gk, gk_got, gv, gv_got, Piece(a1, n, n), Piece(a2, n, n))
    grad_source = reshard_out(grad_source, d, s)
    gq, gk, gv, gk_peer, gv_peer = attend_back(
        SELF_PLANS, info, q, k, k_peer, v, v_peer, grad_self, attended, p_self
    )
    gk_got, gv_got = flip(gk_peer, 1), flip(gv_peer, 1)
    grad_tokens = token_grad(info, g1, gq, gk, gk_got, gv, gv_got, a1, b1, n)
    grad_tokens = reshard_out(grad_tokens, d, s)
    return (output, grad_tokens, grad_source, grad_down, grad_up)


def solution(mesh):
    rows = P("dp", "seq", None)
    weight = P("dp", None)
    return jax.shard_map(
        local,
        mesh=mesh,
        in_specs=(rows, rows, weight, P("dp"), P()) + (weight,) * 10 + (P(), P(), rows),
        out_specs=(rows, rows, rows, P(), P()),
        check_vma=False,
    )
```

```python
import functools
import jax
import jax.numpy as jnp
from jax.sharding import PartitionSpec as P
from jax import lax
from jax.experimental import pallas as pl
from jax.experimental.pallas import tpu as pltpu
BF=jnp.bfloat16; F32=jnp.float32
NEG=-1e30
LOG2E=1.4426950408889634

def cost(us):
    return pl.CostEstimate(flops=int(us * 1e9), bytes_accessed=1024, transcendentals=0)

VM=60*1024*1024

SELF_PLANS=(((((0,True),)), ((0,False),(2,False),(3,False),(1,True))),
            (((2,False),(0,True)), ((2,False),(0,False),(1,True))))
CROSS_PLANS=((((0,False),(1,False),(2,False),(3,False)),)*2,)

def nt(a,b): return lax.dot_general(a,b,(((1,),(1,)),((),())),preferred_element_type=F32)
def nn(a,b): return lax.dot_general(a,b,(((1,),(0,)),((),())),preferred_element_type=F32)

def half_mask(shape, h):
    l=lax.broadcasted_iota(jnp.int32, shape, 1)
    return (l<64) if h==0 else (l>=64)

def fwd_body(plan, C, q, ks, vs, qa, kas, o_ref, p_ref):
    n=0
    kaug=[[jnp.where(half_mask(k.shape,h),k,a) for k,a in zip(ks,kas)] for h in range(2)]
    vts=[v.T for v in vs]
    for slot,blocks in enumerate(plan):
        halves=[]
        for h in range(2):
            qs=q[slot*C:(slot+1)*C]; qas=qa[slot*C:(slot+1)*C]
            qh=jnp.where(half_mask(qs.shape,h),qs,qas)
            ss=[]
            for (kb,diag) in blocks:
                s=nt(kaug[h][kb],qh)
                if diag:
                    ki=lax.broadcasted_iota(jnp.int32,s.shape,0); qi=lax.broadcasted_iota(jnp.int32,s.shape,1)
                    s=jnp.where(ki<=qi,s,NEG)
                ss.append(s)
            m=functools.reduce(jnp.maximum,[jnp.max(s,axis=0,keepdims=True) for s in ss])
            ps=[jnp.exp2(s-m) for s in ss]
            l=functools.reduce(jnp.add,[jnp.sum(p,axis=0,keepdims=True) for p in ps])
            inv=1.0/l
            acc=None
            for i,((kb,_),p) in enumerate(zip(blocks,ps)):
                pb=(p*inv).astype(BF)
                p_ref[0,h,n+i]=pb
                t=nn(vts[kb][64*h:64*h+64],pb)
                acc=t if acc is None else acc+t
            halves.append(acc)
        n+=len(blocks)
        ot=jnp.concatenate(halves,axis=0)
        o_ref[slot*C:(slot+1)*C]=ot.T.astype(BF)

def fwd_kernel(plans, C, info, q_ref, ko, vo, kp, vp, qa, kao, kap, o_ref, p_ref):
    def run(plan):
        ks=[r[i*C:(i+1)*C] for r in (ko,kp) for i in range(2)]
        vs=[r[i*C:(i+1)*C] for r in (vo,vp) for i in range(2)]
        kas=[kao[0:C],kao[C:2*C],kap[0:C],kap[C:2*C]]
        fwd_body(plan,C,q_ref[...],ks,vs,qa[...],kas,o_ref,p_ref)
    if len(plans)==1: run(plans[0])
    else:
        for v,plan in enumerate(plans):
            pl.when(info[0]==v)(functools.partial(run,plan))

def attend(plans, info, q, own, peer, qa, kao, kap):
    T,D=q.shape; C=T//2; pairs=D//128
    nb=sum(len(b) for b in plans[0])
    col=pl.BlockSpec((T,128),lambda h,*_:(0,h))
    val=pl.BlockSpec((T,128),lambda h,*_:(0,pairs+h))
    fix=pl.BlockSpec((T,128),lambda h,*_:(0,0))
    return pl.pallas_call(
        functools.partial(fwd_kernel,plans,C),
        grid_spec=pltpu.PrefetchScalarGridSpec(num_scalar_prefetch=1,grid=(pairs,),
            in_specs=[col]+[col,val]*2+[fix]*3,
            out_specs=[col,pl.BlockSpec((1,2,nb,C,C),lambda h,*_:(h,0,0,0,0))]),
        out_shape=[jax.ShapeDtypeStruct((T,D),BF),jax.ShapeDtypeStruct((pairs,2,nb,C,C),BF)],
        compiler_params=pltpu.CompilerParams(vmem_limit_bytes=VM),
        cost_estimate=cost(20),
        name="attend")(info,q,own,own,peer,peer,qa,kao,kap)

def bwd_body(plan, C, q, ks, vs, do, o, p_ref, gq_ref, gown, gpeer):
    lane=lax.broadcasted_iota(jnp.int32,(C,128),1)
    l64=lax.rem(lane,64)
    ones=jnp.where(l64<2,1.0,0.0).astype(BF)
    vaug=[[jnp.where(half_mask(v.shape,h),v,ones) for v in vs] for h in range(2)]
    kts=[k.T for k in ks]
    gk=[None]*4; gv=[None]*4
    n=0
    zero=jnp.zeros((C,128),BF)
    for slot,blocks in enumerate(plan):
        halves=[]
        for h in range(2):
            hm=lane<64 if h==0 else lane>=64
            dos=do[slot*C:(slot+1)*C]; os=o[slot*C:(slot+1)*C]; qs=q[slot*C:(slot+1)*C]
            prod=jnp.where(hm,dos.astype(F32)*os.astype(F32),0.0)
            d=-jnp.sum(prod,axis=1,keepdims=True)
            hi=d.astype(BF); lo=(d-hi.astype(F32)).astype(BF)
            doa=jnp.where(hm,dos,jnp.where(l64==0,jnp.broadcast_to(hi,(C,128)),jnp.where(l64==1,jnp.broadcast_to(lo,(C,128)),zero)))
            dom=jnp.where(hm,dos,zero)
            qm=jnp.where(hm,qs,zero)
            acc=None
            for i,(kb,_) in enumerate(blocks):
                pb=p_ref[0,h,n+i]
                dp=nt(vaug[h][kb],doa)
                ds=(pb.astype(F32)*dp).astype(BF)
                a=nn(pb,dom); gv[kb]=a if gv[kb] is None else gv[kb]+a
                b=nn(ds,qm); gk[kb]=b if gk[kb] is None else gk[kb]+b
                t=nn(kts[kb][64*h:64*h+64],ds)
                acc=t if acc is None else acc+t
            halves.append(acc)
        n+=len(blocks)
        gq_ref[slot*C:(slot+1)*C]=jnp.concatenate(halves,axis=0).T.astype(BF)
    for kb in range(4):
        ref=gown if kb<2 else gpeer
        sl=slice((kb%2)*C,(kb%2)*C+C)
        z=jnp.zeros((C,128),F32)
        ref[sl,0:128]=((gk[kb] if gk[kb] is not None else z)*(1.0/LOG2E)).astype(ref.dtype)
        ref[sl,128:256]=(gv[kb] if gv[kb] is not None else z).astype(ref.dtype)

def bwd_kernel(plans, C, info, q_ref, ko, vo, kp, vp, do, o, p_ref, *refs):
    gq, gown, gpeer = refs[-3:]
    def run(plan):
        ks=[r[i*C:(i+1)*C] for r in (ko,kp) for i in range(2)]
        vs=[r[i*C:(i+1)*C] for r in (vo,vp) for i in range(2)]
        bwd_body(plan,C,q_ref[...],ks,vs,do[...],o[...],p_ref,gq,gown,gpeer)
    if len(plans)==1: run(plans[0])
    else:
        for v,plan in enumerate(plans):
            pl.when(info[0]==v)(functools.partial(run,plan))

def attend_back(plans, info, q, own, peer, do, o, p, deps=()):
    T,D=q.shape; C=T//2; pairs=D//128
    nb=p.shape[2]
    col=pl.BlockSpec((T,128),lambda h,*_:(0,h))
    wide=pl.BlockSpec((T,256),lambda h,*_:(0,h))
    val=pl.BlockSpec((T,128),lambda h,*_:(0,pairs+h))
    return pl.pallas_call(
        functools.partial(bwd_kernel,plans,C),
        grid_spec=pltpu.PrefetchScalarGridSpec(num_scalar_prefetch=1,grid=(pairs,),
            in_specs=[col]+[col,val]*2+[col]*2+[pl.BlockSpec((1,2,nb,C,C),lambda h,*_:(h,0,0,0,0))]+[pl.BlockSpec(memory_space=pl.ANY)]*len(deps),
            out_specs=[col]+[wide]*2),
        out_shape=[jax.ShapeDtypeStruct((T,D),BF),jax.ShapeDtypeStruct((T,2*D),F32),jax.ShapeDtypeStruct((T,2*D),BF)],
        compiler_params=pltpu.CompilerParams(vmem_limit_bytes=VM),
        cost_estimate=cost(22),
        name="attend_back")(info,q,own,own,peer,peer,do,o,p,*deps)


def vmem(mib):
    return pltpu.CompilerParams(vmem_limit_bytes=mib * 1024 * 1024)


class Piece:
    def __init__(self, parts, at, rows, stride=None, base=0):
        self.parts, self.at, self.rows, self.stride, self.base = parts, at, rows, stride or rows, base
        self.cols, self.dtype = parts[0][0].shape[1], parts[0][0].dtype


def shape_of(load):
    if not isinstance(load, list):
        return load.shape, load.dtype
    return (8 * load[0].stride, load[0].cols), load[0].dtype


def copies_of(load, refs, buf, owner, sem, first):
    if not isinstance(load, list):
        return [pltpu.make_async_copy(refs[0], buf, sem.at[first])]
    out = []
    for j, piece in enumerate(load):
        for m in range(8):
            to = pl.multiple_of((owner ^ m) * piece.stride + piece.base, 16)
            out.append(
                pltpu.make_async_copy(
                    refs[8 * j + m].at[pl.ds(piece.parts[m][1] + piece.at, piece.rows)],
                    buf.at[pl.ds(to, piece.rows)],
                    sem.at[first + 8 * j + m],
                )
            )
    return out


def arrays_of(load):
    return [a for piece in load for a, _ in piece.parts] if isinstance(load, list) else [load]


def gate(values, deps):
    def kernel(*refs):
        del refs

    n = len(values)
    anywhere = pl.BlockSpec(memory_space=pl.ANY)
    return pl.pallas_call(
        kernel,
        in_specs=[anywhere] * (n + len(deps)),
        out_specs=[anywhere] * n,
        out_shape=[jax.ShapeDtypeStruct(v.shape, v.dtype) for v in values],
        input_output_aliases={i: i for i in range(n)},
        cost_estimate=cost(0.1),
        name="gate",
    )(*values, *deps)


def barrier(*values):
    return gate(values, ())


def stage(expand_shard, contract_shard, deps):
    rows, cols = expand_shard.shape
    half = cols // 2

    def kernel(e_ref, c_ref, *refs):
        e1, e2, c = refs[-3:]
        e1[...] = e_ref[:, :half]
        e2[...] = e_ref[:, half:]
        c[...] = c_ref[...]

    full = pl.BlockSpec(memory_space=pltpu.VMEM)
    return pl.pallas_call(
        kernel,
        in_specs=[full, full] + [pl.BlockSpec(memory_space=pl.ANY)] * len(deps),
        out_specs=[full] * 3,
        out_shape=[jax.ShapeDtypeStruct((rows, half), BF)] * 2
        + [jax.ShapeDtypeStruct(contract_shard.shape, BF)],
        cost_estimate=cost(2),
        compiler_params=vmem(60),
        name="stage",
    )(expand_shard, contract_shard, *deps)


def fused(name, info, body, loads, outs, mib=60, deps=()):
    flat, places = [], []
    for load in loads:
        arrays = arrays_of(load)
        places.append((len(flat), len(arrays)))
        flat += arrays
    total, nout = len(flat), len(outs)

    def kernel(info_ref, *refs):
        out_refs = refs[total + len(deps) :][:nout]
        bufs, sem = refs[total + len(deps) + nout : -1], refs[-1]
        started = []
        for load, (first, count), buf in zip(loads, places, bufs):
            started.append(copies_of(load, refs[first : first + count], buf, info_ref[1], sem, first))
            for c in started[-1]:
                c.start()
        ready = set()

        def get(i):
            if i not in ready:
                for c in started[i]:
                    c.wait()
                ready.add(i)
            return bufs[i]

        body(info_ref, get, *out_refs)

    return pl.pallas_call(
        kernel,
        grid_spec=pltpu.PrefetchScalarGridSpec(
            num_scalar_prefetch=1,
            grid=(1,),
            in_specs=[pl.BlockSpec(memory_space=pl.ANY)] * (total + len(deps)),
            out_specs=[pl.BlockSpec(o.shape, lambda i, *_: (0, 0)) for o in outs],
            scratch_shapes=[pltpu.VMEM(*shape_of(load)) for load in loads] + [pltpu.SemaphoreType.DMA((total,))],
        ),
        out_shape=list(outs),
        compiler_params=vmem(mib),
        cost_estimate=cost(6),
        name=name,
    )(info, *flat, *deps)


def shape(rows, cols, dtype):
    return jax.ShapeDtypeStruct((rows, cols), dtype)


def norm_parts(v):
    mean = jnp.mean(v, axis=-1, keepdims=True)
    c = v - mean
    inv = lax.rsqrt(jnp.mean(c * c, axis=-1, keepdims=True) + 1e-05)
    return c * inv, inv


def norm_back(y, inv, g):
    return inv * (g - jnp.mean(g, axis=-1, keepdims=True) - y * jnp.mean(g * y, axis=-1, keepdims=True))


def gelu_pair(v):
    phi = 0.5 + 0.5 * lax.erf(v * 0.7071067811865476)
    pdf = jnp.exp(v * v * -0.5) * 0.3989422804014327
    return v * phi, phi + v * pdf


def tn(a, b):
    return lax.dot_general(a, b, (((0,), (0,)), ((), ())), preferred_element_type=F32)


def project_qkv(info, x, w_query, w_key, w_value, deps):
    T, D = x.shape

    def body(info_ref, get, q, kv):
        xv = get(0)[...]
        q[...] = (nn(xv, get(1)[...]) * (0.125 * LOG2E)).astype(BF)
        kv[:, :D] = nn(xv, get(2)[...]).astype(BF)
        kv[:, D:] = nn(xv, get(3)[...]).astype(BF)

    return fused("qkv", info, body, [x, w_query, w_key, w_value], [shape(T, D, BF), shape(T, 2 * D, BF)], deps=deps)


def project_source(info, x, w_key, w_value):
    T, D = x.shape

    def body(info_ref, get, kv):
        xv = get(0)[...]
        kv[:, :D] = nn(xv, get(1)[...]).astype(BF)
        kv[:, D:] = nn(xv, get(2)[...]).astype(BF)

    return fused("source_kv", info, body, [x, w_key, w_value], [shape(T, 2 * D, BF)])[0]


def after_self(info, x, att, w_out, c_query):
    T, D = x.shape

    def body(info_ref, get, y_ref, inv_ref, cq_ref):
        y, inv = norm_parts(get(0)[...].astype(F32) + nn(get(1)[...], get(2)[...]))
        y_ref[...] = y
        inv_ref[...] = jnp.broadcast_to(inv, inv_ref.shape)
        cq_ref[...] = (nn(y.astype(BF), get(3)[...]) * (0.125 * LOG2E)).astype(BF)

    return fused("after_self", info, body, [x, att, w_out, c_query],
                 [shape(T, D, F32), shape(T, 128, F32), shape(T, D, BF)])


def after_cross(info, y1, att, c_out, down, up, scale):
    T, D = y1.shape
    A = down.shape[1]

    def body(info_ref, get, y_ref, inv_ref, low_ref, sq_ref, gn_ref, base_ref):
        y, inv = norm_parts(get(0)[...] + nn(get(1)[...], get(2)[...]))
        y_ref[...] = y
        inv_ref[...] = jnp.broadcast_to(inv, inv_ref.shape)
        low = y.astype(BF)
        low_ref[...] = low
        h, g = gelu_pair(nn(low, get(3)[...]))
        hb = h.astype(BF)
        sq_ref[...] = hb
        gn_ref[...] = g.astype(BF)
        base_ref[...] = y + get(5)[0:1, 0:1] * nn(hb, get(4)[...])

    return fused("after_cross", info, body, [y1, att, c_out, down, up, scale],
                 [shape(T, D, F32), shape(T, 128, F32), shape(T, D, BF), shape(T, A, BF), shape(T, A, BF),
                  shape(T, D, F32)])


def expand(info, x, first, second, block=1024):
    T, D = x.shape
    width = first.cols
    F = 2 * width
    per = width // block

    def kernel(info_ref, x_ref, *refs):
        ins, (h_ref, g_ref, e, sem) = refs[:16], refs[16:]
        i = pl.program_id(0)
        copies = [copies_of([p], ins[8 * v : 8 * v + 8], e.at[v], info_ref[1], sem, 8 * v)
                  for v, p in enumerate((first, second))]

        @pl.when(i == 0)
        def _():
            for group in copies:
                for c in group:
                    c.start()

        for v in range(2):
            @pl.when(i == v * per)
            def _():
                for c in copies[v]:
                    c.wait()

        w = e[i // per, :, pl.ds(pl.multiple_of(lax.rem(i, per) * block, 128), block)]
        h, g = gelu_pair(nn(x_ref[...], w))
        h_ref[...] = h.astype(BF)
        g_ref[...] = g.astype(BF)

    out = pl.BlockSpec((T, block), lambda i, *_: (0, i))
    return pl.pallas_call(
        kernel,
        grid_spec=pltpu.PrefetchScalarGridSpec(
            num_scalar_prefetch=1,
            grid=(F // block,),
            in_specs=[pl.BlockSpec((T, D), lambda i, *_: (0, 0))] + [pl.BlockSpec(memory_space=pl.ANY)] * 16,
            out_specs=[out, out],
            scratch_shapes=[pltpu.VMEM((2, D, width), BF), pltpu.SemaphoreType.DMA((16,))],
        ),
        out_shape=[shape(T, F, BF)] * 2,
        compiler_params=vmem(60),
        cost_estimate=cost(12),
        name="expand",
    )(info, x, *[a for a, _ in first.parts], *[a for a, _ in second.parts])


def contract_kernel(h, c, base, low, sq, gn, up, g_out, scale, out_ref, g3_ref, gup_ref, gdown_ref, gnar_ref, acc):
    i = pl.program_id(0)

    @pl.when(i == 0)
    def _():
        acc[...] = base[...]

    acc[...] += nn(h[...], c[...])

    @pl.when(i == pl.num_programs(0) - 1)
    def _():
        y, inv = norm_parts(acc[...])
        out_ref[...] = y.astype(BF)
        g3 = norm_back(y, inv, g_out[...].astype(F32))
        g3_ref[...] = g3
        ga = (scale[0:1, 0:1] * g3).astype(BF)
        gup_ref[...] = tn(sq[...], ga).astype(BF)
        gnar = (gn[...].astype(F32) * nt(ga, up[...])).astype(BF)
        gnar_ref[...] = gnar
        gdown_ref[...] = tn(gnar, low[...]).astype(BF)


def contract(h, c, base, low, sq, gn, up, g_out, scale, block=1024):
    T, D = base.shape
    F = c.shape[0]
    A = sq.shape[1]

    def whole(a):
        return pl.BlockSpec(a.shape, lambda i: (0, 0), pipeline_mode=pl.Buffered(1))

    outs = [shape(T, D, BF), shape(T, D, F32), shape(A, D, BF), shape(A, D, BF), shape(T, A, BF)]
    return pl.pallas_call(
        contract_kernel,
        grid=(F // block,),
        in_specs=[pl.BlockSpec((T, block), lambda i: (0, i)), pl.BlockSpec((block, D), lambda i: (i, 0))]
        + [whole(a) for a in (base, low, sq, gn, up, g_out, scale)],
        out_specs=[pl.BlockSpec(o.shape, lambda i: (0, 0)) for o in outs],
        out_shape=outs,
        scratch_shapes=[pltpu.VMEM((T, D), F32)],
        compiler_params=vmem(60),
        cost_estimate=cost(14),
        name="contract",
    )(h, c, base, low, sq, gn, up, g_out, scale)


def ffn_back(info, g3, c, first, second, gp, gnar, down, y2, inv2, c_out, deps, block=1024):
    T, D = g3.shape
    F = c.shape[0]
    width = first.cols
    per = width // block
    loads = ([first], [second], c_out)
    extra = [a for load in loads for a in arrays_of(load)]
    count = len(extra)

    def kernel(info_ref, g3_ref, c_ref, gp_ref, gnar_ref, down_ref, y2_ref, inv2_ref, *refs):
        g2_ref, ga_ref, acc, ea, eb, co, sem = refs[-7:]
        i = pl.program_id(0)
        copies = [copies_of(load, refs[8 * v : count], buf, info_ref[1], sem, 8 * v)
                  for v, (load, buf) in enumerate(zip(loads, (ea, eb, co)))]

        @pl.when(i == 0)
        def _():
            for group in copies:
                for c in group:
                    c.start()
            acc[...] = g3_ref[...] + nt(gnar_ref[...], down_ref[...])

        gh = (nt(g3_ref[...].astype(BF), c_ref[...]) * gp_ref[...].astype(F32)).astype(BF)
        for v, e in enumerate((ea, eb)):
            @pl.when(i == v * per)
            def _():
                for c in copies[v]:
                    c.wait()

            @pl.when(i // per == v)
            def _():
                acc[...] += nt(gh, e[:, pl.ds(pl.multiple_of(lax.rem(i, per) * block, 128), block)])

        @pl.when(i == F // block - 1)
        def _():
            for c in copies[2]:
                c.wait()
            g2 = norm_back(y2_ref[...], inv2_ref[:, 0:1], acc[...])
            g2_ref[...] = g2
            ga_ref[...] = nt(g2.astype(BF), co[...]).astype(BF)

    def whole(a):
        return pl.BlockSpec(a.shape, lambda i, *_: (0, 0), pipeline_mode=pl.Buffered(1))

    outs = [shape(T, D, F32), shape(T, D, BF)]
    extra += list(deps)
    return pl.pallas_call(
        kernel,
        grid_spec=pltpu.PrefetchScalarGridSpec(
            num_scalar_prefetch=1,
            grid=(F // block,),
            in_specs=[whole(g3), pl.BlockSpec((block, D), lambda i, *_: (i, 0)),
                      pl.BlockSpec((T, block), lambda i, *_: (0, i))]
            + [whole(a) for a in (gnar, down, y2, inv2)] + [pl.BlockSpec(memory_space=pl.ANY)] * len(extra),
            out_specs=[pl.BlockSpec(o.shape, lambda i, *_: (0, 0)) for o in outs],
            scratch_shapes=[pltpu.VMEM((T, D), F32), pltpu.VMEM((D, width), BF), pltpu.VMEM((D, width), BF),
                            pltpu.VMEM(*shape_of(c_out)), pltpu.SemaphoreType.DMA((count,))],
        ),
        out_shape=outs,
        compiler_params=vmem(60),
        cost_estimate=cost(18),
        name="ffn_back",
    )(info, g3, c, gp, gnar, down, y2, inv2, *extra)


def before_self(info, g2, gq, y1, inv1, c_query, w_out, deps):
    T, D = g2.shape

    def body(info_ref, get, g1_ref, ga_ref):
        g = get(0)[...] + 0.125 * nt(get(1)[...], get(2)[...])
        g1 = norm_back(get(3)[...], get(4)[:, 0:1], g)
        g1_ref[...] = g1
        ga_ref[...] = nt(g1.astype(BF), get(5)[...]).astype(BF)

    return fused("before_self", info, body, [g2, gq, c_query, y1, inv1, w_out],
                 [shape(T, D, F32), shape(T, D, BF)], deps=deps)


def add_pairs(mine, got, buf):
    D = mine.shape[1] // 2
    for v in range(2):
        for h in range(D // 128):
            at = slice(256 * h + 128 * v, 256 * h + 128 * v + 128)
            buf[:, D * v + 128 * h : D * v + 128 * h + 128] = (mine[:, at] + got[:, at].astype(F32)).astype(BF)


def source_grad(info, gkv, got, w_key, w_value, deps):
    T, D = gkv.shape[0], gkv.shape[1] // 2

    def body(info_ref, get, out):
        buf = get(4)
        add_pairs(get(0), get(1), buf)
        out[...] = (nt(buf[:, :D], get(2)[...]) + nt(buf[:, D:], get(3)[...])).astype(BF)

    return fused("source_grad", info, body, [gkv, got, w_key, w_value, got], [shape(T, D, BF)], deps=deps)[0]


def token_grad(info, g1, gq, gkv, got, w_query, w_key, w_value, deps):
    T, D = g1.shape

    def body(info_ref, get, out):
        acc = get(0)[...] + 0.125 * nt(get(1)[...], get(2)[...])
        buf = get(7)
        add_pairs(get(3), get(4), buf)
        out[...] = (acc + nt(buf[:, :D], get(5)[...]) + nt(buf[:, D:], get(6)[...])).astype(BF)

    return fused("token_grad", info, body, [g1, gq, w_query, gkv, got, w_key, w_value, got],
                 [shape(T, D, BF)], deps=deps)[0]


def move(value, target):
    dp, seq = lax.axis_size("dp"), lax.axis_size("seq")
    pairs = []
    for d in range(dp):
        for s in range(seq):
            a, b = target(d, s)
            pairs.append((d * seq + s, a * seq + b))
    return lax.ppermute(value, ("dp", "seq"), pairs)


def flip(value, bit):
    return move(value, lambda d, s: (d ^ bit, s))


def core_of(chunk):
    return (0, 1, 1, 0)[chunk]


def pick(flag, first, second):
    return jnp.where(flag, first, second)


def take_pieces(value, s):
    return [lax.dynamic_index_in_dim(value, (s + k) % 2, 0, keepdims=False) for k in range(2)]


def send_pieces(pieces):
    return [
        move(piece, lambda a, q, k=k: (2 * (a // 2) + core_of(q), 2 * (a % 2) + (q + k) % 2))
        for k, piece in enumerate(pieces)
    ]


def join_pieces(got, d, s):
    even = (s + d) % 2 == 0
    return jnp.concatenate([pick(even, got[0], got[1]), pick(even, got[1], got[0])], axis=0)


def send_back(value, d, s):
    C = value.shape[0] // 2
    dp, seq = lax.axis_size("dp"), lax.axis_size("seq")
    got = []
    for k in range(2):
        slot = (s + k + d) % 2
        piece = lax.dynamic_slice_in_dim(value, slot * C, C, 0)
        back = {}
        for a in range(dp):
            for q in range(seq):
                back[(2 * (a // 2) + core_of(q), 2 * (a % 2) + (q + k) % 2)] = (a, q)
        got.append(move(piece, lambda a, b: back[(a, b)]))
    return got


def join_rows(got, s):
    even = s % 2 == 0
    return jnp.stack([pick(even, got[0], got[1]), pick(even, got[1], got[0])])


def first_hop(pair, low):
    return [flip(pair[0], 2 * low), flip(pair[1], 4 * low)]


def beside(pair, got):
    return [jnp.concatenate([own, other], axis=0) for own, other in zip(pair, got)]


def second_hop(near, low):
    return [flip(near[0], 4 * low), flip(near[1], 2 * low)]


def all_parts(near, far, low):
    out = []
    for v in range(2):
        half = near[v].shape[0] // 2
        b1, b2 = ((2, 4), (4, 2))[v]
        arrays = [near[v], far[v], flip(near[v], low), flip(far[v], low)]
        parts = {}
        for a, m in zip(arrays, (0, b2, 1, b2 ^ 1)):
            parts[m] = (a, 0)
            parts[m ^ b1] = (a, half)
        out.append([parts[m] for m in range(8)])
    return out


class Reduce:
    def __init__(self, value, d, s, low):
        self.d, self.s, self.low, self.value = d, s, low, value
        self.high = (d // low) % 2 == 1

    def plane(self, v, m):
        return flip(v, 2 * self.low * m)

    def line(self, v, m):
        return move(v, lambda a, b: (a, b ^ m))

    def send_pair(self):
        half = self.value.shape[0] // 2
        lo, hi = self.value[:half], self.value[half:]
        self.kept, self.got = pick(self.high, hi, lo), [flip(pick(self.high, lo, hi), self.low)]

    def send_parts(self, me, n, send):
        parts = self.value.reshape(n, -1, self.value.shape[1])
        take = [lax.dynamic_index_in_dim(parts, me ^ m, 0, keepdims=False) for m in range(n)]
        self.kept, self.got = take[0], [send(take[m], m) for m in range(1, n)]

    def add(self):
        total = self.kept.astype(F32)
        for got in self.got:
            total += got.astype(F32)
        self.value = total.astype(BF)

    def scatter_plane(self):
        self.send_parts(self.d // (2 * self.low), 4, self.plane)

    def scatter_line(self):
        self.send_parts(self.s, lax.axis_size("seq"), self.line)

    def low_bits(self):
        bit = 1
        while bit < self.low:
            got = flip(self.value, bit)
            self.value = (self.value.astype(F32) + got.astype(F32)).astype(BF)
            bit *= 2

    def spread(self, me, n, send):
        self.me, self.got = me, [self.value] + [send(self.value, m) for m in range(1, n)]

    def gather_line(self):
        self.spread(self.s, lax.axis_size("seq"), self.line)

    def gather_plane(self):
        self.spread(self.d // (2 * self.low), 4, self.plane)

    def gather_pair(self):
        self.spread((self.d // self.low) % 2, 2, lambda v, m: flip(v, self.low * m))

    def put(self):
        got = self.got
        n, rows = len(got), []
        for j in range(n):
            part = got[n - 1]
            for m in range(n - 1):
                part = pick((self.me ^ j) == m, got[m], part)
            rows.append(part)
        self.value = jnp.concatenate(rows, axis=0)


def local(tokens, source, target_lengths, source_lengths, step_index, self_query, self_key, self_value,
          self_out, cross_query, cross_key, cross_value, cross_out, ffn_expand, ffn_contract, adapter_down,
          adapter_up, grad_output):
    rows, C, D = tokens.shape
    dp, seq = lax.axis_size("dp"), lax.axis_size("seq")
    assert rows == 2 and seq == 4 and dp % 8 == 0
    low = dp // 8
    d, s = lax.axis_index("dp"), lax.axis_index("seq")
    core = d % 2
    info = jnp.stack([core, d // low]).astype(jnp.int32)

    x = join_pieces(send_pieces(take_pieces(tokens, s)), d, s)

    def widen(shard):
        if low == 1:
            return shard
        groups = [[g * low + i for i in range(low)] for g in range(8)]
        return lax.all_gather(shard, "dp", axis=0, tiled=True, axis_index_groups=groups)

    def two(a, b):
        return jnp.concatenate([a, b], axis=0)

    wide = [widen(w) for w in (self_query, self_key, self_value, self_out, cross_query, cross_key,
                               cross_value, cross_out, ffn_expand)]
    sq, sk, sv, so, cq_, ck_, cv_, co_, ex = wide
    n = sq.shape[0]
    def rows_of(*weights):
        return jnp.concatenate(weights, axis=0)

    h = n // 2
    pair = [rows_of(sk, sv[:h]), rows_of(sq, sv[h:])]
    hop = first_hop(pair, low)
    near = beside(pair, hop)
    a1, b1 = all_parts(near, second_hop(near, low), low)
    w_key, w_query = [Piece(a1, 0, n)], [Piece(b1, 0, n)]
    w_value = [Piece(a1, n, h, n, 0), Piece(b1, n, h, n, h)]
    pair2 = gate([rows_of(ck_, cv_, co_[:h]), rows_of(so, cq_, co_[h:])], hop)
    hop2 = first_hop(pair2, low)

    mine = jnp.concatenate([target_lengths, source_lengths[:, None]], axis=1)
    other = flip(mine, 1)
    table = jnp.concatenate([pick(core == 0, mine, other), pick(core == 0, other, mine)], axis=0)
    row = lax.dynamic_index_in_dim(table, s, 0, keepdims=False)
    lens, src_len = row[:-1], row[-1]
    docs = lens.shape[0]
    ends = jnp.cumsum(lens)[:-1]
    i = jnp.arange(2 * C, dtype=jnp.int32)
    slot = i // C

    def place(which):
        chunk = pick(which == 0, slot * 3, slot + 1)
        return chunk * C + i % C

    lanes = jnp.arange(128, dtype=jnp.int32) % 64

    def doc_hot(pos):
        doc = jnp.sum((pos[:, None] >= ends[None, :]).astype(jnp.int32), axis=-1)
        return doc[:, None] == lanes[None, :]

    own_pos, peer_pos = place(core), place(1 - core)
    k_aug = [doc_hot(own_pos).astype(BF), doc_hot(peer_pos).astype(BF)]
    q_aug = jnp.where(doc_hot(own_pos) | (lanes >= docs)[None, :], 0.0, NEG).astype(BF)
    ck_aug = [((pos[:, None] >= src_len) & (lanes == 0)[None, :]).astype(BF) for pos in (own_pos, peer_pos)]
    cq_aug = jnp.broadcast_to(jnp.where(lanes == 0, NEG, 0.0).astype(BF)[None, :], (2 * C, 128))

    scale = jnp.full((8, 128), (step_index[0] + 1).astype(F32) / 5.0, F32)
    e1, e2, c_shard = stage(ex, ffn_contract, hop)
    q, kv = project_qkv(info, x, w_query, w_key, w_value, (e1,))
    *hop2, q, kv = barrier(*hop2, q, kv)
    near2 = beside(pair2, hop2)
    kv_peer = flip(kv, 1)
    far2, got = second_hop(near2, low), send_pieces(gate(take_pieces(source, s), (q,)))
    attended, p_self = attend(SELF_PLANS, info, q, kv, kv_peer, q_aug, *k_aug)
    *far2, s0, s1, attended, e1, e2, c_shard = barrier(*far2, *got, attended, e1, e2, c_shard)
    w_contract = lax.all_gather(c_shard, "dp", axis=0, tiled=True)
    hop3 = first_hop([e1, e2], low)
    a2, b2 = all_parts(near2, far2, low)
    c_key, c_value = [Piece(a2, 0, n)], [Piece(a2, n, n)]
    w_out, c_query = [Piece(b2, 0, n)], [Piece(b2, n, n)]
    c_out = [Piece(a2, 2 * n, h, n, 0), Piece(b2, 2 * n, h, n, h)]
    src = join_pieces([s0, s1], d, s)
    skv = project_source(info, src, c_key, c_value)
    skv_peer = flip(skv, 1)
    y1, inv1, cq = after_self(info, x, attended, w_out, c_query)
    *hop3, skv_peer, cq = barrier(*hop3, skv_peer, cq)
    near3 = beside([e1, e2], hop3)
    far3, got = second_hop(near3, low), send_pieces(gate(take_pieces(grad_output, s), (cq,)))
    cross_attended, p_cross = attend(CROSS_PLANS, info, cq, skv, skv_peer, cq_aug, *ck_aug)
    *far3, s0, s1, cross_attended = barrier(*far3, *got, cross_attended)
    a3, b3 = all_parts(near3, far3, low)
    g_out = join_pieces([s0, s1], d, s)
    y2, inv2, second_low, squeezed, gn, base = after_cross(
        info, y1, cross_attended, c_out, adapter_down, adapter_up, scale
    )
    ea, eb = Piece(a3, 0, n), Piece(b3, 0, n)
    hidden, gp = expand(info, second_low, ea, eb)
    output, g3, grad_up, grad_down, gnar = contract(
        hidden, w_contract, base, second_low, squeezed, gn, adapter_up, g_out, scale
    )
    output = send_back(output, d, s)
    total = Reduce(two(grad_up, grad_down), d, s, low)
    total.send_pair()
    g2, grad_cross = ffn_back(info, g3, w_contract, ea, eb, gp, gnar, adapter_down, y2, inv2, c_out, ())
    *total.got, g2, grad_cross = barrier(*total.got, g2, grad_cross)
    total.add()
    total.scatter_plane()
    gq, gkv, gkv_peer = attend_back(
        CROSS_PLANS, info, cq, skv, skv_peer, grad_cross, cross_attended, p_cross, (total.kept,)
    )
    *total.got, o0, o1, gq, gkv_peer = barrier(*total.got, *output, gq, gkv_peer)
    output = [o0, o1]
    total.add()
    total.scatter_line()
    got = flip(gkv_peer, 1)
    g1, grad_self = before_self(info, g2, gq, y1, inv1, c_query, w_out, (total.kept,))
    *total.got, got, grad_self = barrier(*total.got, got, grad_self)
    total.add()
    total.low_bits()
    total.gather_line()
    grad_source = source_grad(info, gkv, got, c_key, c_value, (grad_self, total.value))
    *line, grad_source = barrier(*total.got[1:], grad_source)
    total.got[1:] = line
    total.put()
    total.gather_plane()
    pieces = send_back(grad_source, d, s)
    gq, gkv, gkv_peer = attend_back(
        SELF_PLANS, info, q, kv, kv_peer, grad_self, attended, p_self, (total.value,)
    )
    *total.got, o0, o1, gq, gkv_peer = barrier(*total.got, *pieces, gq, gkv_peer)
    got = flip(gkv_peer, 1)
    total.put()
    total.gather_pair()
    grad_tokens = token_grad(info, g1, gq, gkv, got, w_query, w_key, w_value, (total.value,))
    *total.got, grad_tokens = barrier(*total.got, grad_tokens)
    grad_tokens = send_back(grad_tokens, d, s)
    output, grad_source, grad_tokens = [join_rows(v, s) for v in (output, [o0, o1], grad_tokens)]
    total.put()
    grads = total.value.astype(F32)
    A = adapter_down.shape[1]
    grad_up, grad_down = grads[:A], grads[A:].T
    return (output, grad_tokens, grad_source, grad_down, grad_up)


def solution(mesh):
    rows = P("dp", "seq", None)
    weight = P("dp", None)
    return jax.shard_map(
        local,
        mesh=mesh,
        in_specs=(rows, rows, weight, P("dp"), P()) + (weight,) * 10 + (P(), P(), rows),
        out_specs=(rows, rows, rows, P(), P()),
        check_vma=False,
    )
```

```python
import functools

import jax
import jax.numpy as jnp
from jax import lax
from jax.experimental import pallas as pl
from jax.experimental.pallas import tpu as pltpu
from jax.sharding import PartitionSpec as P

BF, F32 = jnp.bfloat16, jnp.float32
NEG = -1e30
LOG2E = 1.4426950408889634
PER = 2

SELF_PLANS = (
    (((0, True),), ((0, False), (2, False), (3, False), (1, True))),
    (((2, False), (0, True)), ((2, False), (0, False), (1, True))),
)
CROSS_PLANS = ((((0, False), (1, False), (2, False), (3, False)),) * 2,)


def nt(a, b):
    return lax.dot_general(a, b, (((1,), (1,)), ((), ())), preferred_element_type=F32)


def nn(a, b):
    return lax.dot_general(a, b, (((1,), (0,)), ((), ())), preferred_element_type=F32)


def tn(a, b):
    return lax.dot_general(a, b, (((0,), (0,)), ((), ())), preferred_element_type=F32)


def cost(us):
    return pl.CostEstimate(flops=int(us * 3e8), bytes_accessed=1024, transcendentals=0)


def params():
    return pltpu.CompilerParams(vmem_limit_bytes=64 * 1024 * 1024)


def shape(rows, cols, dtype):
    return jax.ShapeDtypeStruct((rows, cols), dtype)


class Whole:
    def __init__(self, array):
        self.arrays, self.shape, self.dtype, self.count = [array], array.shape, array.dtype, 1

    def copies(self, info, refs, buf, sem, first):
        return [pltpu.make_async_copy(refs[0], buf, sem.at[first])]


class Pieces:
    def __init__(self, stride, *pieces):
        self.stride, self.pieces = stride, pieces
        self.arrays = [a for parts, *_ in pieces for a, _ in parts]
        self.shape, self.dtype = (8 * stride, self.arrays[0].shape[1]), self.arrays[0].dtype
        self.count = len(self.arrays)

    def copies(self, info, refs, buf, sem, first):
        out = []
        for parts, at, rows, base in self.pieces:
            for m, (_, start) in enumerate(parts):
                to = pl.multiple_of((info[1] ^ m) * self.stride + base, 16)
                i = len(out)
                out.append(
                    pltpu.make_async_copy(
                        refs[i].at[pl.ds(start + at, rows)], buf.at[pl.ds(to, rows)], sem.at[first + i]
                    )
                )
        return out


class Shards:
    def __init__(self, array, owners, at, rows):
        self.arrays, self.count, self.at, self.rows = [array], owners, at, rows
        self.each = array.shape[0] // owners
        self.shape, self.dtype = (owners * rows, array.shape[1]), array.dtype

    def copies(self, info, refs, buf, sem, first):
        return [
            pltpu.make_async_copy(
                refs[0].at[pl.ds(j * self.each + self.at, self.rows)],
                buf.at[pl.ds(j * self.rows, self.rows)],
                sem.at[first + j],
            )
            for j in range(self.count)
        ]


class Slots:
    def __init__(self, arrays, at, rows):
        self.arrays, self.at, self.rows, self.count = list(arrays), at, rows, 2
        self.shape, self.dtype = (2 * rows, arrays[0].shape[1]), arrays[0].dtype

    def copies(self, info, refs, buf, sem, first):
        return [
            pltpu.make_async_copy(
                refs[k].at[pl.ds(self.at, self.rows)],
                buf.at[pl.ds(pl.multiple_of((info[2] ^ k) * self.rows, 16), self.rows)],
                sem.at[first + k],
            )
            for k in range(2)
        ]


class Chunk:
    def __init__(self, array, k):
        self.arrays, self.k, self.count = [array], k, 1
        self.shape, self.dtype = (array.shape[0] // 2, array.shape[1]), array.dtype

    def copies(self, info, refs, buf, sem, first):
        rows = self.shape[0]
        at = pl.multiple_of((info[2] ^ self.k) * rows, 16)
        return [pltpu.make_async_copy(refs[0].at[pl.ds(at, rows)], buf, sem.at[first])]


class Loads:
    def __init__(self, loads):
        self.loads = [v if hasattr(v, "copies") else Whole(v) for v in loads]
        self.arrays = [a for v in self.loads for a in v.arrays]
        self.specs = [pl.BlockSpec(memory_space=pl.ANY)] * len(self.arrays)
        self.scratch = [pltpu.VMEM(v.shape, v.dtype) for v in self.loads]
        self.scratch.append(pltpu.SemaphoreType.DMA((sum(v.count for v in self.loads),)))

    def bind(self, info, refs, scratch):
        bufs, sem = scratch[:-1], scratch[-1]
        at = first = 0
        out = []
        for v, buf in zip(self.loads, bufs):
            out.append((v.copies(info, refs[at : at + len(v.arrays)], buf, sem, first), buf))
            at += len(v.arrays)
            first += v.count
        return out


def start_all(bound):
    for copies, _ in bound:
        for c in copies:
            c.start()


def getter(bound):
    ready = set()

    def get(i):
        copies, buf = bound[i]
        if i not in ready:
            for c in copies:
                c.wait()
            ready.add(i)
        return buf

    return get


ANYWHERE = pl.BlockSpec(memory_space=pl.ANY)


def half_mask(shape, h):
    lane = lax.broadcasted_iota(jnp.int32, shape, 1)
    return (lane < 64) if h == 0 else (lane >= 64)


def top(parts):
    rows = 64
    pieces = [p[i : i + rows] for p in parts for i in range(0, p.shape[0], rows)]
    while len(pieces) > 1:
        pieces = [jnp.maximum(*pieces[i : i + 2]) if i + 1 < len(pieces) else pieces[i] for i in range(0, len(pieces), 2)]
    return jnp.max(pieces[0], axis=0, keepdims=True)


def forward_pair(plan, C, q, ks, vs, qa, kas, put, p_ref):
    kaug = [[jnp.where(half_mask(k.shape, h), k, a) for k, a in zip(ks, kas)] for h in range(2)]
    vts = [v.T for v in vs]
    ones = jnp.ones((16, C), BF)
    units, n = [], 0
    for slot, blocks in enumerate(plan):
        units += [(slot, h, n, blocks) for h in range(2)]
        n += len(blocks)

    def scores_of(unit):
        slot, h, _, blocks = unit
        rows = slice(slot * C, (slot + 1) * C)
        qh = jnp.where(half_mask((C, 128), h), q[rows], qa[rows])
        scores = []
        for kb, diagonal in blocks:
            s = nt(kaug[h][kb], qh)
            if diagonal:
                ki = lax.broadcasted_iota(jnp.int32, s.shape, 0)
                qi = lax.broadcasted_iota(jnp.int32, s.shape, 1)
                s = jnp.where(ki <= qi, s, NEG)
            scores.append(s)
        return scores, top(scores)

    def rest(unit, scores, m):
        _, h, n, blocks = unit
        ps = [jnp.exp2(s - m).astype(BF) for s in scores]
        for i, p in enumerate(ps):
            p_ref[h, n + i] = p
        values = [jnp.concatenate([vts[kb][64 * h : 64 * h + 64], ones], axis=0) for kb, _ in blocks]
        both = nn(jnp.concatenate(values, axis=1), jnp.concatenate(ps, axis=0))
        inv = 1.0 / both[64:65]
        return both[:64] * inv, jnp.broadcast_to(inv, (64, C))

    done = []
    AHEAD = 2
    pending = [scores_of(u) for u in units[:AHEAD]]
    for i, unit in enumerate(units):
        if i + AHEAD < len(units):
            pending.append(scores_of(units[i + AHEAD]))
        done.append(rest(unit, *pending[i]))
        if i % 2:
            halves, inverses = zip(*done[-2:])
            put(unit[0], jnp.concatenate(halves, axis=0).T.astype(BF), jnp.concatenate(inverses, axis=0).T)


def by_plan(plans, info, run):
    if len(plans) == 1:
        run(plans[0])
    else:
        for v, plan in enumerate(plans):
            pl.when(info[0] == v)(functools.partial(run, plan))


def attend(plans, info, q, own, peer, qa, kao, kap, loads, outs, finish, deps=()):
    T, D = q.shape
    C, pairs = T // 2, D // 128
    steps = pairs // PER
    nb = sum(len(b) for b in plans[0])
    held = Loads(loads)

    def kernel(info_ref, q_ref, ko, vo, kp, vp, qa_ref, kao_ref, kap_ref, *refs):
        ins = refs[: len(held.arrays)]
        o_ref, p_ref, r_ref, *out_refs = refs[len(held.arrays) + len(deps) :][: 3 + len(outs)]
        att, *scratch = refs[len(held.arrays) + len(deps) + 3 + len(outs) :]
        step = pl.program_id(0)
        bound = held.bind(info_ref, ins, scratch)
        pl.when(step == 0)(lambda: start_all(bound))

        def run(plan):
            for j in range(PER):
                at = slice(128 * j, 128 * j + 128)
                cols = pl.ds(pl.multiple_of((step * PER + j) * 128, 128), 128)

                def put(slot, value, inverse):
                    o_ref[slot * C : (slot + 1) * C, at] = value
                    r_ref[slot * C : (slot + 1) * C, at] = inverse
                    att[slot * C : (slot + 1) * C, cols] = value

                def chunks(*rs):
                    return [r[i * C : (i + 1) * C, at] for r in rs for i in range(2)]

                masks = [m[i * C : (i + 1) * C] for m in (kao_ref, kap_ref) for i in range(2)]
                forward_pair(plan, C, q_ref[:, at], chunks(ko, kp), chunks(vo, vp), qa_ref[...], masks, put, p_ref.at[j])

        by_plan(plans, info_ref, run)

        @pl.when(step == steps - 1)
        def _():
            finish(getter(bound), att, *out_refs)

    col = pl.BlockSpec((T, 128 * PER), lambda h, *_: (0, h))
    val = pl.BlockSpec((T, 128 * PER), lambda h, *_: (0, steps + h))
    fix = pl.BlockSpec((T, 128), lambda h, *_: (0, 0))
    return pl.pallas_call(
        kernel,
        grid_spec=pltpu.PrefetchScalarGridSpec(
            num_scalar_prefetch=1,
            grid=(steps,),
            in_specs=[col] + [col, val] * 2 + [fix] * 3 + held.specs + [ANYWHERE] * len(deps),
            out_specs=[col, pl.BlockSpec((PER, 2, nb, C, C), lambda h, *_: (h, 0, 0, 0, 0)), col]
            + [pl.BlockSpec(o.shape, lambda h, *_: (0, 0)) for o in outs],
            scratch_shapes=[pltpu.VMEM((T, D), BF)] + held.scratch,
        ),
        out_shape=[shape(T, D, BF), jax.ShapeDtypeStruct((pairs, 2, nb, C, C), BF), shape(T, D, F32)] + list(outs),
        compiler_params=params(),
        cost_estimate=cost(25),
        name="attend",
    )(info, q, own, own, peer, peer, qa, kao, kap, *held.arrays, *deps)


def backward_pair(plan, C, q, ks, vs, do, o, r, p_ref, put, gown, gpeer):
    lane = lax.broadcasted_iota(jnp.int32, (C, 128), 1)
    l64 = lax.rem(lane, 64)
    ones = jnp.where(l64 < 2, 1.0, 0.0).astype(BF)
    vaug = [[jnp.where(half_mask(v.shape, h), v, ones) for v in vs] for h in range(2)]
    kts = [k.T for k in ks]
    by_key = [[] for _ in range(4)]
    zero = jnp.zeros((C, 128), BF)
    units, n = [], 0
    for slot, blocks in enumerate(plan):
        units += [(slot, h, n, blocks) for h in range(2)]
        n += len(blocks)

    def probs_back(unit):
        slot, h, n, blocks = unit
        rows = slice(slot * C, (slot + 1) * C)
        scaled = do[rows].astype(F32) * r[rows]
        dos = scaled.astype(BF)
        hm = lane < 64 if h == 0 else lane >= 64
        d = -jnp.sum(jnp.where(hm, scaled * o[rows].astype(F32), 0.0), axis=1, keepdims=True)
        hi = d.astype(BF)
        lo = (d - hi.astype(F32)).astype(BF)
        tail = jnp.where(l64 == 0, jnp.broadcast_to(hi, (C, 128)), jnp.where(l64 == 1, jnp.broadcast_to(lo, (C, 128)), zero))
        doa = jnp.where(hm, dos, tail)
        return [nt(vaug[h][kb], doa) for kb, _ in blocks], jnp.where(hm, dos, zero), jnp.where(hm, q[rows], zero)

    def rest(unit, dps, dom, qm):
        slot, h, n, blocks = unit
        grads = []
        for i, ((kb, _), dp) in enumerate(zip(blocks, dps)):
            pb = p_ref[h, n + i]
            ds = (pb.astype(F32) * dp).astype(BF)
            grads.append(ds)
            by_key[kb].append((pb, ds, dom, qm))
        wide = jnp.concatenate([kts[kb][64 * h : 64 * h + 64] for kb, _ in blocks], axis=1)
        return nn(wide, jnp.concatenate(grads, axis=0))

    done = []
    BACK = 2
    pending = [probs_back(u) for u in units[:BACK]]
    for i, unit in enumerate(units):
        if i + BACK < len(units):
            pending.append(probs_back(units[i + BACK]))
        done.append(rest(unit, *pending[i]))
        if i % 2:
            put(unit[0], jnp.concatenate(done[-2:], axis=0).T.astype(BF))
    for kb in range(4):
        ref = gown if kb < 2 else gpeer
        rows = slice((kb % 2) * C, (kb % 2) * C + C)
        if by_key[kb]:
            pbs, dss, doms, qms = zip(*by_key[kb])
            gk = nn(jnp.concatenate(dss, axis=1), jnp.concatenate(qms, axis=0))
            gv = nn(jnp.concatenate(pbs, axis=1), jnp.concatenate(doms, axis=0))
        else:
            gk = gv = jnp.zeros((C, 128), F32)
        ref[rows, 0:128] = (gk * (1.0 / LOG2E)).astype(BF)
        ref[rows, 128:256] = gv.astype(BF)


def attend_back(plans, info, q, own, peer, do, o, r, p, loads, outs, finish, deps=()):
    T, D = q.shape
    C, pairs, nb = T // 2, D // 128, p.shape[2]
    steps = pairs // PER
    held = Loads(loads)

    def kernel(info_ref, q_ref, ko, vo, kp, vp, do_ref, o_ref, r_ref, p_ref, *refs):
        ins = refs[: len(held.arrays)]
        gown, gpeer, *out_refs = refs[len(held.arrays) + len(deps) :][: 2 + len(outs)]
        gq, *scratch = refs[len(held.arrays) + len(deps) + 2 + len(outs) :]
        step = pl.program_id(0)
        bound = held.bind(info_ref, ins, scratch)
        pl.when(step == 0)(lambda: start_all(bound))

        def run(plan):
            for j in range(PER):
                at = slice(128 * j, 128 * j + 128)
                wide = slice(256 * j, 256 * j + 256)
                cols = pl.ds(pl.multiple_of((step * PER + j) * 128, 128), 128)

                def put(slot, value):
                    gq[slot * C : (slot + 1) * C, cols] = value

                def chunks(*rs):
                    return [r[i * C : (i + 1) * C, at] for r in rs for i in range(2)]

                backward_pair(plan, C, q_ref[:, at], chunks(ko, kp), chunks(vo, vp), do_ref[:, at], o_ref[:, at],
                              r_ref[:, at], p_ref.at[j], put, gown.at[:, wide], gpeer.at[:, wide])

        by_plan(plans, info_ref, run)

        @pl.when(step == steps - 1)
        def _():
            finish(getter(bound), gq, *out_refs)

    col = pl.BlockSpec((T, 128 * PER), lambda h, *_: (0, h))
    val = pl.BlockSpec((T, 128 * PER), lambda h, *_: (0, steps + h))
    wide = pl.BlockSpec((T, 256 * PER), lambda h, *_: (0, h))
    return pl.pallas_call(
        kernel,
        grid_spec=pltpu.PrefetchScalarGridSpec(
            num_scalar_prefetch=1,
            grid=(steps,),
            in_specs=[col] + [col, val] * 2 + [col] * 3
            + [pl.BlockSpec((PER, 2, nb, C, C), lambda h, *_: (h, 0, 0, 0, 0))] + held.specs + [ANYWHERE] * len(deps),
            out_specs=[wide] * 2 + [pl.BlockSpec(v.shape, lambda h, *_: (0, 0)) for v in outs],
            scratch_shapes=[pltpu.VMEM((T, D), BF)] + held.scratch,
        ),
        out_shape=[shape(T, 2 * D, BF)] * 2 + list(outs),
        compiler_params=params(),
        cost_estimate=cost(25),
        name="attend_back",
    )(info, q, own, own, peer, peer, do, o, r, p, *held.arrays, *deps)


def gate(values, deps):
    def kernel(*refs):
        del refs

    n = len(values)
    return pl.pallas_call(
        kernel,
        in_specs=[ANYWHERE] * (n + len(deps)),
        out_specs=[ANYWHERE] * n,
        out_shape=[jax.ShapeDtypeStruct(v.shape, v.dtype) for v in values],
        input_output_aliases={i: i for i in range(n)},
        cost_estimate=cost(0.1),
        name="gate",
    )(*values, *deps)


def barrier(*values):
    return gate(values, ())


def beside(pair, got, deps=()):
    def kernel(a, b, c, d, *refs):
        ab, cd = refs[-2:]
        n, m = a.shape[0], c.shape[0]
        ab[:n] = a[...]
        ab[n:] = b[...]
        cd[:m] = c[...]
        cd[m:] = d[...]

    full = pl.BlockSpec(memory_space=pltpu.VMEM)
    return pl.pallas_call(
        kernel,
        in_specs=[full] * 4 + [ANYWHERE] * len(deps),
        out_specs=[full] * 2,
        out_shape=[shape(2 * v.shape[0], v.shape[1], BF) for v in pair],
        cost_estimate=cost(2),
        compiler_params=params(),
        name="beside",
    )(pair[0], got[0], pair[1], got[1], *deps)


def stage(expand_shard, contract_shard, others, deps):
    rows, cols = expand_shard.shape
    half = cols // 2
    n = len(others)

    def kernel(e_ref, c_ref, *refs):
        e1, e2, c, rest = refs[-4:]
        e1[...] = e_ref[:, :half]
        e2[...] = e_ref[:, half:]
        c[...] = c_ref[...]
        at = 0
        for r in refs[:n]:
            rest[at : at + r.shape[0]] = r[...]
            at += r.shape[0]

    full = pl.BlockSpec(memory_space=pltpu.VMEM)
    return pl.pallas_call(
        kernel,
        in_specs=[full] * (2 + n) + [ANYWHERE] * len(deps),
        out_specs=[full] * 4,
        out_shape=[shape(rows, half, BF)] * 2
        + [shape(*contract_shard.shape, BF), shape(sum(o.shape[0] for o in others), others[0].shape[1], BF)],
        cost_estimate=cost(3),
        compiler_params=params(),
        name="stage",
    )(expand_shard, contract_shard, *others, *deps)


def halves(array, deps):
    rows, half = array.shape[0], array.shape[1] // 2

    def kernel(a, *refs):
        refs[-2][...] = a[:, :half]
        refs[-1][...] = a[:, half:]

    full = pl.BlockSpec(memory_space=pltpu.VMEM)
    return pl.pallas_call(
        kernel,
        in_specs=[full] + [ANYWHERE] * len(deps),
        out_specs=[full] * 2,
        out_shape=[shape(rows, half, BF)] * 2,
        cost_estimate=cost(2),
        compiler_params=params(),
        name="halves",
    )(array, *deps)


def fused(name, info, body, loads, outs, deps=(), extra=()):
    held = Loads(loads)
    total, nout = len(held.arrays), len(outs)

    def kernel(info_ref, *refs):
        out_refs = refs[total + len(deps) :][:nout]
        scratch = refs[total + len(deps) + nout :]
        bound = held.bind(info_ref, refs[:total], scratch[len(extra) :])
        start_all(bound)
        body(info_ref, getter(bound), *out_refs, *scratch[: len(extra)])

    return pl.pallas_call(
        kernel,
        grid_spec=pltpu.PrefetchScalarGridSpec(
            num_scalar_prefetch=1,
            grid=(1,),
            in_specs=held.specs + [ANYWHERE] * len(deps),
            out_specs=[pl.BlockSpec(o.shape, lambda i, *_: (0, 0)) for o in outs],
            scratch_shapes=list(extra) + held.scratch,
        ),
        out_shape=list(outs),
        compiler_params=params(),
        cost_estimate=cost(6),
        name=name,
    )(info, *held.arrays, *deps)


def norm_parts(v):
    mean = jnp.mean(v, axis=-1, keepdims=True)
    c = v - mean
    inv = lax.rsqrt(jnp.mean(c * c, axis=-1, keepdims=True) + 1e-05)
    return c * inv, inv


def norm_back(y, inv, g):
    return inv * (g - jnp.mean(g, axis=-1, keepdims=True) - y * jnp.mean(g * y, axis=-1, keepdims=True))


def gelu_pair(v):
    phi = 0.5 + 0.5 * lax.erf(v * 0.7071067811865476)
    pdf = jnp.exp(v * v * -0.5) * 0.3989422804014327
    return v * phi, phi + v * pdf


def put_slots(info_ref, value, first, second):
    C = value.shape[0] // 2
    for k, ref in enumerate((first, second)):
        ref[...] = value[pl.ds(pl.multiple_of((info_ref[2] ^ k) * C, 16), C)].astype(BF)


def project_qkv(info, x, w_query, w_key, w_value, deps):
    T, D = x.shape

    def body(info_ref, get, q, kv):
        xv = get(0)[...]
        kv[:, :D] = nn(xv, get(1)[...]).astype(BF)
        kv[:, D:] = nn(xv, get(2)[...]).astype(BF)
        q[...] = (nn(xv, get(3)[...]) * (0.125 * LOG2E)).astype(BF)

    return fused("qkv", info, body, [x, w_key, w_value, w_query], [shape(T, D, BF), shape(T, 2 * D, BF)], deps=deps)


def project_source(info, x, w_key, w_value, deps):
    T, D = x.shape

    def body(info_ref, get, kv):
        xv = get(0)[...]
        kv[:, :D] = nn(xv, get(1)[...]).astype(BF)
        kv[:, D:] = nn(xv, get(2)[...]).astype(BF)

    return fused("source_kv", info, body, [x, w_key, w_value], [shape(T, 2 * D, BF)], deps=deps)[0]


def attend_self(info, q, kv, kv_peer, masks, deps):
    return attend(SELF_PLANS, info, q, kv, kv_peer, *masks, [], [], lambda get, att: None, deps)


def between(info, x, att, w_out, c_query, src, c_key, c_value, deps):
    T, D = x.shape

    def body(info_ref, get, kv, y_ref, low_ref, inv_ref, cq_ref):
        xv = get(0)[...]
        kv[:, :D] = nn(xv, get(1)[...]).astype(BF)
        kv[:, D:] = nn(xv, get(2)[...]).astype(BF)
        y, inv = norm_parts(get(5)[...].astype(F32) + nn(get(3)[...], get(4)[...]))
        low = y.astype(BF)
        y_ref[...] = y
        low_ref[...] = low
        inv_ref[...] = jnp.broadcast_to(inv, inv_ref.shape)
        cq_ref[...] = (nn(low, get(6)[...]) * (0.125 * LOG2E)).astype(BF)

    outs = [shape(T, 2 * D, BF), shape(T, D, F32), shape(T, D, BF), shape(T, 128, F32), shape(T, D, BF)]
    return fused("between", info, body, [src, c_key, c_value, att, w_out, x, c_query], outs, deps=deps)


def attend_cross(info, q, kv, kv_peer, masks, y1, c_out, down, up, scale):
    T, D = q.shape
    A = down.shape[1]

    def finish(get, att, low_ref, inv_ref, sq_ref, gn_ref, base_ref):
        y, inv = norm_parts(get(1)[...] + nn(att[...], get(0)[...]))
        inv_ref[...] = jnp.broadcast_to(inv, inv_ref.shape)
        low = y.astype(BF)
        low_ref[...] = low
        h, g = gelu_pair(nn(low, get(2)[...]))
        hb = h.astype(BF)
        sq_ref[...] = hb
        gn_ref[...] = g.astype(BF)
        base_ref[...] = y + get(4)[0:1, 0:1] * nn(hb, get(3)[...])

    outs = [shape(T, D, BF), shape(T, 128, F32), shape(T, A, BF), shape(T, A, BF), shape(T, D, F32)]
    return attend(CROSS_PLANS, info, q, kv, kv_peer, *masks, [c_out, y1, down, up, scale], outs, finish)


def expand(info, x, first, second, block=1024):
    T, D = x.shape
    width = first.shape[1]
    F = 2 * width
    per = width // block
    held = Loads([first, second])

    def kernel(info_ref, x_ref, *refs):
        ins, (h_ref, g_ref, *scratch) = refs[: len(held.arrays)], refs[len(held.arrays) :]
        i = pl.program_id(0)
        bound = held.bind(info_ref, ins, scratch)
        pl.when(i == 0)(lambda: start_all(bound))
        cols = pl.ds(pl.multiple_of(lax.rem(i, per) * block, 128), block)
        for v, (copies, buf) in enumerate(bound):
            @pl.when(i == v * per)
            def _():
                for c in copies:
                    c.wait()

            @pl.when(i // per == v)
            def _():
                h, g = gelu_pair(nn(x_ref[...], buf[:, cols]))
                h_ref[...] = h.astype(BF)
                g_ref[...] = g.astype(BF)

    out = pl.BlockSpec((T, block), lambda i, *_: (0, i))
    return pl.pallas_call(
        kernel,
        grid_spec=pltpu.PrefetchScalarGridSpec(
            num_scalar_prefetch=1,
            grid=(F // block,),
            in_specs=[pl.BlockSpec((T, D), lambda i, *_: (0, 0))] + held.specs,
            out_specs=[out, out],
            scratch_shapes=held.scratch,
        ),
        out_shape=[shape(T, F, BF)] * 2,
        compiler_params=params(),
        cost_estimate=cost(12),
        name="expand",
    )(info, x, *held.arrays)


def contract(info, h, c, base, low, sq, gn, up, g_out, scale, block=1024):
    T, D = base.shape
    F = c.shape[0]
    A = sq.shape[1]
    held = Loads([base, g_out, scale, sq, up, gn, low])

    def kernel(info_ref, h_ref, c_ref, *refs):
        ins = refs[: len(held.arrays)]
        out0, out1, g3_ref, kept_ref, sent_ref, gnar_ref, acc, *scratch = refs[len(held.arrays) :]
        i = pl.program_id(0)
        bound = held.bind(info_ref, ins, scratch)
        pl.when(i == 0)(lambda: start_all(bound))

        @pl.when(i == 0)
        def _():
            acc[...] = nn(h_ref[...], c_ref[...])

        @pl.when(i > 0)
        def _():
            acc[...] += nn(h_ref[...], c_ref[...])

        @pl.when(i == F // block - 1)
        def _():
            get = getter(bound)
            y, inv = norm_parts(acc[...] + get(0)[...])
            g3 = norm_back(y, inv, get(1)[...].astype(F32))
            g3_ref[...] = g3
            acc[...] = y
            put_slots(info_ref, acc, out0, out1)
            ga = (get(2)[0:1, 0:1] * g3).astype(BF)
            gup = tn(get(3)[...], ga).astype(BF)
            gnar = (get(5)[...].astype(F32) * nt(ga, get(4)[...])).astype(BF)
            gnar_ref[...] = gnar
            gdown = tn(gnar, get(6)[...]).astype(BF)
            for side, keep, send in ((0, gup, gdown), (1, gdown, gup)):
                @pl.when(info_ref[3] == side)
                def _():
                    kept_ref[...] = keep
                    sent_ref[...] = send

    outs = [shape(T // 2, D, BF)] * 2 + [shape(T, D, F32), shape(A, D, BF), shape(A, D, BF), shape(T, A, BF)]
    return pl.pallas_call(
        kernel,
        grid_spec=pltpu.PrefetchScalarGridSpec(
            num_scalar_prefetch=1,
            grid=(F // block,),
            in_specs=[pl.BlockSpec((T, block), lambda i, *_: (0, i)), pl.BlockSpec((block, D), lambda i, *_: (i, 0))]
            + held.specs,
            out_specs=[pl.BlockSpec(o.shape, lambda i, *_: (0, 0)) for o in outs],
            scratch_shapes=[pltpu.VMEM((T, D), F32)] + held.scratch,
        ),
        out_shape=outs,
        compiler_params=params(),
        cost_estimate=cost(14),
        name="contract",
    )(info, h, c, *held.arrays)


def ffn_back(info, g3, c, first, second, gp, gnar, down, low, inv, c_out, deps, block=1024):
    T, D = g3.shape
    F = c.shape[0]
    width = first.shape[1]
    per = width // block
    held = Loads([first, second, gnar, down, c_out, low, inv])

    def kernel(info_ref, g3_ref, c_ref, gp_ref, *refs):
        ins = refs[: len(held.arrays)]
        g2_ref, ga_ref, acc, *scratch = refs[len(held.arrays) + len(deps) :]
        i = pl.program_id(0)
        bound = held.bind(info_ref, ins, scratch)
        pl.when(i == 0)(lambda: start_all(bound))
        gh = (nt(g3_ref[...].astype(BF), c_ref[...]) * gp_ref[...].astype(F32)).astype(BF)

        @pl.when(i == 0)
        def _():
            acc[...] = g3_ref[...]

        for v in range(2):
            copies, e = bound[v]

            @pl.when(i == v * per)
            def _():
                for copy in copies:
                    copy.wait()

            @pl.when(i // per == v)
            def _():
                acc[...] += nt(gh, e[:, pl.ds(pl.multiple_of(lax.rem(i, per) * block, 128), block)])

        @pl.when(i == F // block - 1)
        def _():
            get = getter(bound)
            g2 = norm_back(get(5)[...].astype(F32), get(6)[:, 0:1], acc[...] + nt(get(2)[...], get(3)[...]))
            g2_ref[...] = g2
            ga_ref[...] = nt(g2.astype(BF), get(4)[...]).astype(BF)

    outs = [shape(T, D, F32), shape(T, D, BF)]
    return pl.pallas_call(
        kernel,
        grid_spec=pltpu.PrefetchScalarGridSpec(
            num_scalar_prefetch=1,
            grid=(F // block,),
            in_specs=[pl.BlockSpec((T, D), lambda i, *_: (0, 0)), pl.BlockSpec((block, D), lambda i, *_: (i, 0)),
                      pl.BlockSpec((T, block), lambda i, *_: (0, i))] + held.specs + [ANYWHERE] * len(deps),
            out_specs=[pl.BlockSpec(o.shape, lambda i, *_: (0, 0)) for o in outs],
            scratch_shapes=[pltpu.VMEM((T, D), F32)] + held.scratch,
        ),
        out_shape=outs,
        compiler_params=params(),
        cost_estimate=cost(18),
        name="ffn_back",
    )(info, g3, c, gp, *held.arrays, *deps)


def attend_cross_back(info, q, kv, kv_peer, do, o, r, p, g2, y1, inv1, c_query, w_out, deps):
    T, D = q.shape

    def finish(get, gq, g1_ref, ga_ref):
        g = get(1)[...] + 0.125 * nt(gq[...], get(0)[...])
        g1 = norm_back(get(2)[...].astype(F32), get(3)[:, 0:1], g)
        g1_ref[...] = g1
        ga_ref[...] = nt(g1.astype(BF), get(4)[...]).astype(BF)

    return attend_back(CROSS_PLANS, info, q, kv, kv_peer, do, o, r, p, [c_query, g2, y1, inv1, w_out],
                       [shape(T, D, F32), shape(T, D, BF)], finish, deps)


def attend_self_back(info, q, kv, kv_peer, do, o, r, p, g1, w_query, deps):
    T, D = q.shape

    def finish(get, gq, acc_ref):
        acc_ref[...] = get(1)[...] + 0.125 * nt(gq[...], get(0)[...])

    return attend_back(SELF_PLANS, info, q, kv, kv_peer, do, o, r, p, [w_query, g1], [shape(T, D, F32)], finish, deps)


def add_pairs(mine, got, part):
    D = mine.shape[1] // 2
    out = []
    for h in range(D // 128):
        at = slice(256 * h + 128 * part, 256 * h + 128 * part + 128)
        out.append((mine[:, at].astype(F32) + got[:, at].astype(F32)).astype(BF))
    return jnp.concatenate(out, axis=1)


def source_grad(info, gkv, got, w_key, w_value, deps):
    T, D = gkv.shape[0], gkv.shape[1] // 2

    def body(info_ref, get, out0, out1, total):
        mine, other = get(0), get(1)
        acc = nt(add_pairs(mine, other, 0), get(2)[...])
        total[...] = acc + nt(add_pairs(mine, other, 1), get(3)[...])
        put_slots(info_ref, total, out0, out1)

    return fused("source_grad", info, body, [gkv, got, w_key, w_value], [shape(T // 2, D, BF)] * 2, deps=deps,
                 extra=[pltpu.VMEM((T, D), F32)])


def token_grad(info, acc, gkv, got, w_key, w_value, deps):
    T, D = acc.shape

    def body(info_ref, get, out0, out1):
        mine, other = get(0), get(1)
        g = get(4)
        g[...] += nt(add_pairs(mine, other, 0), get(2)[...])
        g[...] += nt(add_pairs(mine, other, 1), get(3)[...])
        put_slots(info_ref, g, out0, out1)

    return fused("token_grad", info, body, [gkv, got, w_key, w_value, acc], [shape(T // 2, D, BF)] * 2, deps=deps)


def move(value, target):
    dp, seq = lax.axis_size("dp"), lax.axis_size("seq")
    pairs = []
    for d in range(dp):
        for s in range(seq):
            a, b = target(d, s)
            pairs.append((d * seq + s, a * seq + b))
    return lax.ppermute(value, ("dp", "seq"), pairs)


def flip(value, bit):
    return move(value, lambda d, s: (d ^ bit, s))


def core_of(chunk):
    return (0, 1, 1, 0)[chunk]


def pick(flag, first, second):
    return jnp.where(flag, first, second)


def send_pieces(pieces):
    return [
        move(piece, lambda a, q, k=k: (2 * (a // 2) + core_of(q), 2 * (a % 2) + (q + k) % 2))
        for k, piece in enumerate(pieces)
    ]


def take_pieces(value, s):
    return [lax.dynamic_index_in_dim(value, (s + k) % 2, 0, keepdims=False) for k in range(2)]


def send_back(pieces):
    dp, seq = lax.axis_size("dp"), lax.axis_size("seq")
    got = []
    for k, piece in enumerate(pieces):
        back = {}
        for a in range(dp):
            for q in range(seq):
                back[(2 * (a // 2) + core_of(q), 2 * (a % 2) + (q + k) % 2)] = (a, q)
        got.append(move(piece, lambda a, b: back[(a, b)]))
    return got


def join_rows(got, s):
    even = s % 2 == 0
    return jnp.stack([pick(even, got[0], got[1]), pick(even, got[1], got[0])])


def first_hop(pair, low):
    return [flip(pair[0], 2 * low), flip(pair[1], 4 * low)]


def second_hop(near, low):
    return [flip(near[0], 4 * low), flip(near[1], 2 * low)]


def all_parts(near, far, low):
    out = []
    for v in range(2):
        half = near[v].shape[0] // 2
        b1, b2 = ((2, 4), (4, 2))[v]
        arrays = [near[v], far[v], flip(near[v], low), flip(far[v], low)]
        parts = {}
        for a, m in zip(arrays, (0, b2, 1, b2 ^ 1)):
            parts[m] = (a, 0)
            parts[m ^ b1] = (a, half)
        out.append([parts[m] for m in range(8)])
    return out


class Reduce:
    def __init__(self, kept, sent, d, s, low):
        self.d, self.s, self.low = d, s, low
        self.kept, self.got = kept, [flip(sent, low)]

    def plane(self, v, m):
        return flip(v, 2 * self.low * m)

    def scatter_plane(self):
        me = self.d // (2 * self.low)
        parts = self.value.reshape(4, -1, self.value.shape[1])
        take = [lax.dynamic_index_in_dim(parts, me ^ m, 0, keepdims=False) for m in range(4)]
        self.kept, self.got = take[0], [self.plane(take[m], m) for m in range(1, 4)]

    def line(self, bit):
        self.kept, self.got = self.value, [move(self.value, lambda a, b: (a, b ^ bit))]

    def add(self):
        total = self.kept.astype(F32)
        for got in self.got:
            total += got.astype(F32)
        self.value = total.astype(BF)

    def low_bits(self):
        bit = 1
        while bit < self.low:
            got = flip(self.value, bit)
            self.value = (self.value.astype(F32) + got.astype(F32)).astype(BF)
            bit *= 2

    def gather_plane(self):
        self.me = self.d // (2 * self.low)
        self.got = [self.value] + [self.plane(self.value, m) for m in range(1, 4)]

    def put(self):
        got = self.got
        n, rows = len(got), []
        for j in range(n):
            part = got[n - 1]
            for m in range(n - 1):
                part = pick((self.me ^ j) == m, got[m], part)
            rows.append(part)
        self.value = jnp.concatenate(rows, axis=0)


def local(tokens, source, target_lengths, source_lengths, step_index, self_query, self_key, self_value,
          self_out, cross_query, cross_key, cross_value, cross_out, ffn_expand, ffn_contract, adapter_down,
          adapter_up, grad_output):
    rows, C, D = tokens.shape
    dp, seq = lax.axis_size("dp"), lax.axis_size("seq")
    assert rows == 2 and seq == 4 and dp % 8 == 0
    low = dp // 8
    d, s = lax.axis_index("dp"), lax.axis_index("seq")
    core = d % 2
    info = jnp.stack([core, d // low, (s + d) % 2, (d // low) % 2]).astype(jnp.int32)

    def widen(shard):
        if low == 1:
            return shard
        groups = [[g * low + i for i in range(low)] for g in range(8)]
        return lax.all_gather(shard, "dp", axis=0, tiled=True, axis_index_groups=groups)

    def rows_of(*weights):
        return jnp.concatenate(weights, axis=0)

    t = send_pieces(take_pieces(tokens, s))
    sq, sk, sv, ex = [widen(w) for w in (self_query, self_key, self_value, ffn_expand)]
    n = sq.shape[0]
    h = n // 2
    pair = [rows_of(sk, sv[:h]), rows_of(sq, sv[h:])]
    e1, e2, c_shard, rest = stage(ex, ffn_contract, [self_out, cross_key, cross_value, cross_query, cross_out], ())
    near = beside(pair, first_hop(pair, low), (t[0], rest))
    rest = lax.all_gather(rest, "dp", axis=0, tiled=True)
    each = self_out.shape[0]
    w_out, c_key, c_value, c_query, c_out = [Shards(rest, dp, j * each, each) for j in range(5)]

    mine = jnp.concatenate([target_lengths, source_lengths[:, None]], axis=1)
    other = flip(mine, 1)
    table = jnp.concatenate([pick(core == 0, mine, other), pick(core == 0, other, mine)], axis=0)
    row = lax.dynamic_index_in_dim(table, s, 0, keepdims=False)
    lens, src_len = row[:-1], row[-1]
    docs = lens.shape[0]
    ends = jnp.cumsum(lens)[:-1]
    i = jnp.arange(2 * C, dtype=jnp.int32)
    slot = i // C

    def place(which):
        chunk = pick(which == 0, slot * 3, slot + 1)
        return chunk * C + i % C

    lanes = jnp.arange(128, dtype=jnp.int32) % 64

    def doc_hot(pos):
        doc = jnp.sum((pos[:, None] >= ends[None, :]).astype(jnp.int32), axis=-1)
        return doc[:, None] == lanes[None, :]

    own_pos, peer_pos = place(core), place(1 - core)
    k_aug = [doc_hot(own_pos).astype(BF), doc_hot(peer_pos).astype(BF)]
    q_aug = jnp.where(doc_hot(own_pos) | (lanes >= docs)[None, :], 0.0, NEG).astype(BF)
    ck_aug = [((pos[:, None] >= src_len) & (lanes == 0)[None, :]).astype(BF) for pos in (own_pos, peer_pos)]
    cq_aug = jnp.broadcast_to(jnp.where(lanes == 0, NEG, 0.0).astype(BF)[None, :], (2 * C, 128))

    scale = jnp.full((8, 128), (step_index[0] + 1).astype(F32) / 5.0, F32)
    src = send_pieces(gate(take_pieces(source, s), t))
    *far, c_shard = gate(
        [*second_hop(near, low), c_shard], (*src, info, q_aug, *k_aug, cq_aug, *ck_aug, scale, e1, e2)
    )
    w_contract = lax.all_gather(c_shard, "dp", axis=0, tiled=True)
    a1, b1 = all_parts(near, far, low)
    w_key, w_query = Pieces(n, (a1, 0, n, 0)), Pieces(n, (b1, 0, n, 0))
    w_value = Pieces(n, (a1, n, h, 0), (b1, n, h, h))
    x = Slots(t, 0, C)
    q, kv = project_qkv(info, x, w_query, w_key, w_value, ())
    q, kv, e1, e2 = barrier(q, kv, e1, e2)
    kv_peer = flip(kv, 1)
    hop3 = first_hop([e1, e2], low)
    attended, p_self, r_self = attend_self(info, q, kv, kv_peer, (q_aug, *k_aug), ())
    *hop3, attended = barrier(*hop3, attended)
    near3 = beside([e1, e2], hop3)
    far3 = second_hop(near3, low)
    skv, y1, y1_low, inv1, cq = between(info, x, attended, w_out, c_query, Slots(src, 0, C), c_key, c_value, near3)
    skv, cq, *pieces = barrier(skv, cq, *take_pieces(grad_output, s))
    g_out = send_pieces(pieces)
    skv_peer = flip(skv, 1)
    cross_attended, p_cross, r_cross, second_low, inv2, squeezed, gn, base = attend_cross(
        info, cq, skv, skv_peer, (cq_aug, *ck_aug), y1, c_out, adapter_down, adapter_up, scale
    )
    *far3, g0, g1, second_low = barrier(*far3, *g_out, second_low)
    g_out = [g0, g1]
    a3, b3 = all_parts(near3, far3, low)
    ea, eb = Pieces(n, (a3, 0, n, 0)), Pieces(n, (b3, 0, n, 0))
    hidden, gp = expand(info, second_low, ea, eb)
    o0, o1, g3, kept, sent, gnar = contract(
        info, hidden, w_contract, base, second_low, squeezed, gn, adapter_up, Slots(g_out, 0, C), scale
    )
    output = send_back([o0, o1])
    total = Reduce(kept, sent, d, s, low)
    g2, grad_cross = ffn_back(info, g3, w_contract, ea, eb, gp, gnar, adapter_down, second_low, inv2, c_out, ())
    *total.got, g2, grad_cross = barrier(*total.got, g2, grad_cross)
    total.add()
    total.scatter_plane()
    gkv, gkv_peer, g1, grad_self = attend_cross_back(
        info, cq, skv, skv_peer, grad_cross, cross_attended, r_cross, p_cross, g2, y1_low, inv1, c_query, w_out, (total.kept,)
    )
    *total.got, o0, o1, grad_self, gkv_peer = barrier(*total.got, *output, grad_self, gkv_peer)
    output = [o0, o1]
    total.add()
    total.line(2)
    got = flip(gkv_peer, 1)
    pieces = source_grad(info, gkv, got, c_key, c_value, (grad_self, total.kept))
    pieces = send_back(pieces)
    gkv, gkv_peer, acc = attend_self_back(
        info, q, kv, kv_peer, grad_self, attended, r_self, p_self, g1, w_query, pieces[:0]
    )
    *total.got, s0, s1, gkv_peer = barrier(*total.got, *pieces, gkv_peer)
    got = flip(gkv_peer, 1)
    total.add()
    total.line(1)
    pieces = token_grad(info, acc, gkv, got, w_key, w_value, (total.kept,))
    *total.got, o0, o1, s0, s1, t0, t1 = barrier(*total.got, *output, s0, s1, *pieces)
    tokens_back = send_back([t0, t1])
    output = [o0, o1]
    total.add()
    total.low_bits()
    total.gather_plane()
    total.put()
    grads, other = total.value, flip(total.value, low)
    high = (d // low) % 2 == 1
    grad_up = pick(high, other, grads).astype(F32)
    grad_down = pick(high, grads, other).astype(F32).T
    output, grad_source, grad_tokens = [join_rows(v, s) for v in (output, [s0, s1], tokens_back)]
    return (output, grad_tokens, grad_source, grad_down, grad_up)


def solution(mesh):
    rows = P("dp", "seq", None)
    weight = P("dp", None)
    return jax.shard_map(
        local,
        mesh=mesh,
        in_specs=(rows, rows, weight, P("dp"), P()) + (weight,) * 10 + (P(), P(), rows),
        out_specs=(rows, rows, rows, P(), P()),
        check_vma=False,
    )
```

```python
import functools

import jax
import jax.numpy as jnp
from jax import lax
from jax.experimental import pallas as pl
from jax.experimental.pallas import tpu as pltpu
from jax.sharding import PartitionSpec as P

BF, F32 = jnp.bfloat16, jnp.float32
NEG = -1e30
LOG2E = 1.4426950408889634
PER = 2

SELF_PLANS = (
    (((0, True),), ((0, False), (2, False), (3, False), (1, True))),
    (((2, False), (0, True)), ((2, False), (0, False), (1, True))),
)
CROSS_PLANS = ((((0, False), (1, False), (2, False), (3, False)),) * 2,)


def nt(a, b):
    return lax.dot_general(a, b, (((1,), (1,)), ((), ())), preferred_element_type=F32)


def nn(a, b):
    return lax.dot_general(a, b, (((1,), (0,)), ((), ())), preferred_element_type=F32)


def tn(a, b):
    return lax.dot_general(a, b, (((0,), (0,)), ((), ())), preferred_element_type=F32)


def cost(us):
    return pl.CostEstimate(flops=int(us * 3e8), bytes_accessed=1024, transcendentals=0)


def params():
    return pltpu.CompilerParams(vmem_limit_bytes=64 * 1024 * 1024)


def shape(rows, cols, dtype):
    return jax.ShapeDtypeStruct((rows, cols), dtype)


class Whole:
    def __init__(self, array):
        self.arrays, self.shape, self.dtype, self.count = [array], array.shape, array.dtype, 1

    def copies(self, info, refs, buf, sem, first):
        return [pltpu.make_async_copy(refs[0], buf, sem.at[first])]


class Pieces:
    def __init__(self, stride, *pieces):
        self.stride, self.pieces = stride, pieces
        self.arrays = [a for parts, *_ in pieces for a, _ in parts]
        self.shape, self.dtype = (8 * stride, self.arrays[0].shape[1]), self.arrays[0].dtype
        self.count = len(self.arrays)

    def copies(self, info, refs, buf, sem, first):
        out = []
        for parts, at, rows, base in self.pieces:
            for m, (_, start) in enumerate(parts):
                to = pl.multiple_of((info[1] ^ m) * self.stride + base, 16)
                i = len(out)
                out.append(
                    pltpu.make_async_copy(
                        refs[i].at[pl.ds(start + at, rows)], buf.at[pl.ds(to, rows)], sem.at[first + i]
                    )
                )
        return out


class Shards:
    def __init__(self, array, owners, at, rows):
        self.arrays, self.count, self.at, self.rows = [array], owners, at, rows
        self.each = array.shape[0] // owners
        self.shape, self.dtype = (owners * rows, array.shape[1]), array.dtype

    def copies(self, info, refs, buf, sem, first):
        return [
            pltpu.make_async_copy(
                refs[0].at[pl.ds(j * self.each + self.at, self.rows)],
                buf.at[pl.ds(j * self.rows, self.rows)],
                sem.at[first + j],
            )
            for j in range(self.count)
        ]


class Slots:
    def __init__(self, arrays, at, rows):
        self.arrays, self.at, self.rows, self.count = list(arrays), at, rows, 2
        self.shape, self.dtype = (2 * rows, arrays[0].shape[1]), arrays[0].dtype

    def copies(self, info, refs, buf, sem, first):
        return [
            pltpu.make_async_copy(
                refs[k].at[pl.ds(self.at, self.rows)],
                buf.at[pl.ds(pl.multiple_of((info[2] ^ k) * self.rows, 16), self.rows)],
                sem.at[first + k],
            )
            for k in range(2)
        ]


class Chunk:
    def __init__(self, array, k):
        self.arrays, self.k, self.count = [array], k, 1
        self.shape, self.dtype = (array.shape[0] // 2, array.shape[1]), array.dtype

    def copies(self, info, refs, buf, sem, first):
        rows = self.shape[0]
        at = pl.multiple_of((info[2] ^ self.k) * rows, 16)
        return [pltpu.make_async_copy(refs[0].at[pl.ds(at, rows)], buf, sem.at[first])]


class Loads:
    def __init__(self, loads):
        self.loads = [v if hasattr(v, "copies") else Whole(v) for v in loads]
        self.arrays = [a for v in self.loads for a in v.arrays]
        self.specs = [pl.BlockSpec(memory_space=pl.ANY)] * len(self.arrays)
        self.scratch = [pltpu.VMEM(v.shape, v.dtype) for v in self.loads]
        self.scratch.append(pltpu.SemaphoreType.DMA((sum(v.count for v in self.loads),)))

    def bind(self, info, refs, scratch):
        bufs, sem = scratch[:-1], scratch[-1]
        at = first = 0
        out = []
        for v, buf in zip(self.loads, bufs):
            out.append((v.copies(info, refs[at : at + len(v.arrays)], buf, sem, first), buf))
            at += len(v.arrays)
            first += v.count
        return out


def start_all(bound):
    for copies, _ in bound:
        for c in copies:
            c.start()


def getter(bound):
    ready = set()

    def get(i):
        copies, buf = bound[i]
        if i not in ready:
            for c in copies:
                c.wait()
            ready.add(i)
        return buf

    return get


ANYWHERE = pl.BlockSpec(memory_space=pl.ANY)


def half_mask(shape, h):
    lane = lax.broadcasted_iota(jnp.int32, shape, 1)
    return (lane < 64) if h == 0 else (lane >= 64)


def top(parts):
    rows = 64
    pieces = [p[i : i + rows] for p in parts for i in range(0, p.shape[0], rows)]
    while len(pieces) > 1:
        pieces = [jnp.maximum(*pieces[i : i + 2]) if i + 1 < len(pieces) else pieces[i] for i in range(0, len(pieces), 2)]
    return jnp.max(pieces[0], axis=0, keepdims=True)


def forward_pair(plan, C, q, ks, vs, qa, kas, put, p_ref):
    kaug = [[jnp.where(half_mask(k.shape, h), k, a) for k, a in zip(ks, kas)] for h in range(2)]
    vts = [v.T for v in vs]
    ones = jnp.ones((16, C), BF)
    units, n = [], 0
    for slot, blocks in enumerate(plan):
        units += [(slot, h, n, blocks) for h in range(2)]
        n += len(blocks)

    def scores_of(unit):
        slot, h, _, blocks = unit
        rows = slice(slot * C, (slot + 1) * C)
        qh = jnp.where(half_mask((C, 128), h), q[rows], qa[rows])
        scores = []
        for kb, diagonal in blocks:
            s = nt(kaug[h][kb], qh)
            if diagonal:
                ki = lax.broadcasted_iota(jnp.int32, s.shape, 0)
                qi = lax.broadcasted_iota(jnp.int32, s.shape, 1)
                s = jnp.where(ki <= qi, s, NEG)
            scores.append(s)
        return scores, top(scores)

    def rest(unit, scores, m):
        _, h, n, blocks = unit
        ps = [jnp.exp2(s - m).astype(BF) for s in scores]
        for i, p in enumerate(ps):
            p_ref[h, n + i] = p
        values = [jnp.concatenate([vts[kb][64 * h : 64 * h + 64], ones], axis=0) for kb, _ in blocks]
        both = nn(jnp.concatenate(values, axis=1), jnp.concatenate(ps, axis=0))
        inv = 1.0 / both[64:65]
        return both[:64] * inv, jnp.broadcast_to(inv, (64, C))

    done = []
    AHEAD = 2
    pending = [scores_of(u) for u in units[:AHEAD]]
    for i, unit in enumerate(units):
        if i + AHEAD < len(units):
            pending.append(scores_of(units[i + AHEAD]))
        done.append(rest(unit, *pending[i]))
        if i % 2:
            halves, inverses = zip(*done[-2:])
            put(unit[0], jnp.concatenate(halves, axis=0).T.astype(BF), jnp.concatenate(inverses, axis=0).T)


def by_plan(plans, info, run):
    if len(plans) == 1:
        run(plans[0])
    else:
        for v, plan in enumerate(plans):
            pl.when(info[0] == v)(functools.partial(run, plan))


def attend(plans, info, q, own, peer, qa, kao, kap, loads, outs, finish, deps=()):
    T, D = q.shape
    C, pairs = T // 2, D // 128
    steps = pairs // PER
    nb = sum(len(b) for b in plans[0])
    held = Loads(loads)

    def kernel(info_ref, q_ref, ko, vo, kp, vp, qa_ref, kao_ref, kap_ref, *refs):
        ins = refs[: len(held.arrays)]
        o_ref, p_ref, r_ref, *out_refs = refs[len(held.arrays) + len(deps) :][: 3 + len(outs)]
        att, *scratch = refs[len(held.arrays) + len(deps) + 3 + len(outs) :]
        step = pl.program_id(0)
        bound = held.bind(info_ref, ins, scratch)
        pl.when(step == 0)(lambda: start_all(bound))

        def run(plan):
            for j in range(PER):
                at = slice(128 * j, 128 * j + 128)
                cols = pl.ds(pl.multiple_of((step * PER + j) * 128, 128), 128)

                def put(slot, value, inverse):
                    o_ref[slot * C : (slot + 1) * C, at] = value
                    r_ref[slot * C : (slot + 1) * C, at] = inverse
                    att[slot * C : (slot + 1) * C, cols] = value

                def chunks(*rs):
                    return [r[i * C : (i + 1) * C, at] for r in rs for i in range(2)]

                masks = [m[i * C : (i + 1) * C] for m in (kao_ref, kap_ref) for i in range(2)]
                forward_pair(plan, C, q_ref[:, at], chunks(ko, kp), chunks(vo, vp), qa_ref[...], masks, put, p_ref.at[j])

        by_plan(plans, info_ref, run)

        @pl.when(step == steps - 1)
        def _():
            finish(getter(bound), att, *out_refs)

    col = pl.BlockSpec((T, 128 * PER), lambda h, *_: (0, h))
    val = pl.BlockSpec((T, 128 * PER), lambda h, *_: (0, steps + h))
    fix = pl.BlockSpec((T, 128), lambda h, *_: (0, 0))
    return pl.pallas_call(
        kernel,
        grid_spec=pltpu.PrefetchScalarGridSpec(
            num_scalar_prefetch=1,
            grid=(steps,),
            in_specs=[col] + [col, val] * 2 + [fix] * 3 + held.specs + [ANYWHERE] * len(deps),
            out_specs=[col, pl.BlockSpec((PER, 2, nb, C, C), lambda h, *_: (h, 0, 0, 0, 0)), col]
            + [pl.BlockSpec(o.shape, lambda h, *_: (0, 0)) for o in outs],
            scratch_shapes=[pltpu.VMEM((T, D), BF)] + held.scratch,
        ),
        out_shape=[shape(T, D, BF), jax.ShapeDtypeStruct((pairs, 2, nb, C, C), BF), shape(T, D, F32)] + list(outs),
        compiler_params=params(),
        cost_estimate=cost(25),
        name="attend",
    )(info, q, own, own, peer, peer, qa, kao, kap, *held.arrays, *deps)


def backward_pair(plan, C, q, ks, vs, do, o, r, p_ref, put, gown, gpeer):
    lane = lax.broadcasted_iota(jnp.int32, (C, 128), 1)
    l64 = lax.rem(lane, 64)
    ones = jnp.where(l64 < 2, 1.0, 0.0).astype(BF)
    vaug = [[jnp.where(half_mask(v.shape, h), v, ones) for v in vs] for h in range(2)]
    kts = [k.T for k in ks]
    by_key = [[] for _ in range(4)]
    zero = jnp.zeros((C, 128), BF)
    units, n = [], 0
    for slot, blocks in enumerate(plan):
        units += [(slot, h, n, blocks) for h in range(2)]
        n += len(blocks)

    def probs_back(unit):
        slot, h, n, blocks = unit
        rows = slice(slot * C, (slot + 1) * C)
        scaled = do[rows].astype(F32) * r[rows]
        dos = scaled.astype(BF)
        hm = lane < 64 if h == 0 else lane >= 64
        d = -jnp.sum(jnp.where(hm, scaled * o[rows].astype(F32), 0.0), axis=1, keepdims=True)
        hi = d.astype(BF)
        lo = (d - hi.astype(F32)).astype(BF)
        tail = jnp.where(l64 == 0, jnp.broadcast_to(hi, (C, 128)), jnp.where(l64 == 1, jnp.broadcast_to(lo, (C, 128)), zero))
        doa = jnp.where(hm, dos, tail)
        return [nt(vaug[h][kb], doa) for kb, _ in blocks], jnp.where(hm, dos, zero), jnp.where(hm, q[rows], zero)

    def rest(unit, dps, dom, qm):
        slot, h, n, blocks = unit
        grads = []
        for i, ((kb, _), dp) in enumerate(zip(blocks, dps)):
            pb = p_ref[h, n + i]
            ds = (pb.astype(F32) * dp).astype(BF)
            grads.append(ds)
            by_key[kb].append((pb, ds, dom, qm))
        wide = jnp.concatenate([kts[kb][64 * h : 64 * h + 64] for kb, _ in blocks], axis=1)
        return nn(wide, jnp.concatenate(grads, axis=0))

    done = []
    BACK = 2
    pending = [probs_back(u) for u in units[:BACK]]
    for i, unit in enumerate(units):
        if i + BACK < len(units):
            pending.append(probs_back(units[i + BACK]))
        done.append(rest(unit, *pending[i]))
        if i % 2:
            put(unit[0], jnp.concatenate(done[-2:], axis=0).T.astype(BF))
    for kb in range(4):
        ref = gown if kb < 2 else gpeer
        rows = slice((kb % 2) * C, (kb % 2) * C + C)
        if by_key[kb]:
            pbs, dss, doms, qms = zip(*by_key[kb])
            gk = nn(jnp.concatenate(dss, axis=1), jnp.concatenate(qms, axis=0))
            gv = nn(jnp.concatenate(pbs, axis=1), jnp.concatenate(doms, axis=0))
        else:
            gk = gv = jnp.zeros((C, 128), F32)
        ref[rows, 0:128] = (gk * (1.0 / LOG2E)).astype(BF)
        ref[rows, 128:256] = gv.astype(BF)


def attend_back(plans, info, q, own, peer, do, o, r, p, loads, outs, finish, deps=()):
    T, D = q.shape
    C, pairs, nb = T // 2, D // 128, p.shape[2]
    steps = pairs // PER
    held = Loads(loads)

    def kernel(info_ref, q_ref, ko, vo, kp, vp, do_ref, o_ref, r_ref, p_ref, *refs):
        ins = refs[: len(held.arrays)]
        gown, gpeer, *out_refs = refs[len(held.arrays) + len(deps) :][: 2 + len(outs)]
        gq, *scratch = refs[len(held.arrays) + len(deps) + 2 + len(outs) :]
        step = pl.program_id(0)
        bound = held.bind(info_ref, ins, scratch)
        pl.when(step == 0)(lambda: start_all(bound))

        def run(plan):
            for j in range(PER):
                at = slice(128 * j, 128 * j + 128)
                wide = slice(256 * j, 256 * j + 256)
                cols = pl.ds(pl.multiple_of((step * PER + j) * 128, 128), 128)

                def put(slot, value):
                    gq[slot * C : (slot + 1) * C, cols] = value

                def chunks(*rs):
                    return [r[i * C : (i + 1) * C, at] for r in rs for i in range(2)]

                backward_pair(plan, C, q_ref[:, at], chunks(ko, kp), chunks(vo, vp), do_ref[:, at], o_ref[:, at],
                              r_ref[:, at], p_ref.at[j], put, gown.at[:, wide], gpeer.at[:, wide])

        by_plan(plans, info_ref, run)

        @pl.when(step == steps - 1)
        def _():
            finish(getter(bound), gq, *out_refs)

    col = pl.BlockSpec((T, 128 * PER), lambda h, *_: (0, h))
    val = pl.BlockSpec((T, 128 * PER), lambda h, *_: (0, steps + h))
    wide = pl.BlockSpec((T, 256 * PER), lambda h, *_: (0, h))
    return pl.pallas_call(
        kernel,
        grid_spec=pltpu.PrefetchScalarGridSpec(
            num_scalar_prefetch=1,
            grid=(steps,),
            in_specs=[col] + [col, val] * 2 + [col] * 3
            + [pl.BlockSpec((PER, 2, nb, C, C), lambda h, *_: (h, 0, 0, 0, 0))] + held.specs + [ANYWHERE] * len(deps),
            out_specs=[wide] * 2 + [pl.BlockSpec(v.shape, lambda h, *_: (0, 0)) for v in outs],
            scratch_shapes=[pltpu.VMEM((T, D), BF)] + held.scratch,
        ),
        out_shape=[shape(T, 2 * D, BF)] * 2 + list(outs),
        compiler_params=params(),
        cost_estimate=cost(25),
        name="attend_back",
    )(info, q, own, own, peer, peer, do, o, r, p, *held.arrays, *deps)


def gate(values, deps):
    def kernel(*refs):
        del refs

    n = len(values)
    return pl.pallas_call(
        kernel,
        in_specs=[ANYWHERE] * (n + len(deps)),
        out_specs=[ANYWHERE] * n,
        out_shape=[jax.ShapeDtypeStruct(v.shape, v.dtype) for v in values],
        input_output_aliases={i: i for i in range(n)},
        cost_estimate=cost(0.1),
        name="gate",
    )(*values, *deps)


def barrier(*values):
    return gate(values, ())


def beside(pair, got, deps=()):
    def kernel(a, b, c, d, *refs):
        ab, cd = refs[-2:]
        n, m = a.shape[0], c.shape[0]
        ab[:n] = a[...]
        ab[n:] = b[...]
        cd[:m] = c[...]
        cd[m:] = d[...]

    full = pl.BlockSpec(memory_space=pltpu.VMEM)
    return pl.pallas_call(
        kernel,
        in_specs=[full] * 4 + [ANYWHERE] * len(deps),
        out_specs=[full] * 2,
        out_shape=[shape(2 * v.shape[0], v.shape[1], BF) for v in pair],
        cost_estimate=cost(2),
        compiler_params=params(),
        name="beside",
    )(pair[0], got[0], pair[1], got[1], *deps)


def stage(expand_shard, contract_shard, deps):
    rows, cols = expand_shard.shape
    half = cols // 2

    def kernel(e_ref, c_ref, *refs):
        e1, e2, c = refs[-3:]
        e1[...] = e_ref[:, :half]
        e2[...] = e_ref[:, half:]
        c[...] = c_ref[...]

    full = pl.BlockSpec(memory_space=pltpu.VMEM)
    return pl.pallas_call(
        kernel,
        in_specs=[full, full] + [ANYWHERE] * len(deps),
        out_specs=[full] * 3,
        out_shape=[shape(rows, half, BF)] * 2 + [shape(*contract_shard.shape, BF)],
        cost_estimate=cost(3),
        compiler_params=params(),
        name="stage",
    )(expand_shard, contract_shard, *deps)


def fused(name, info, body, loads, outs, deps=(), extra=()):
    held = Loads(loads)
    total, nout = len(held.arrays), len(outs)

    def kernel(info_ref, *refs):
        out_refs = refs[total + len(deps) :][:nout]
        scratch = refs[total + len(deps) + nout :]
        bound = held.bind(info_ref, refs[:total], scratch[len(extra) :])
        start_all(bound)
        body(info_ref, getter(bound), *out_refs, *scratch[: len(extra)])

    return pl.pallas_call(
        kernel,
        grid_spec=pltpu.PrefetchScalarGridSpec(
            num_scalar_prefetch=1,
            grid=(1,),
            in_specs=held.specs + [ANYWHERE] * len(deps),
            out_specs=[pl.BlockSpec(o.shape, lambda i, *_: (0, 0)) for o in outs],
            scratch_shapes=list(extra) + held.scratch,
        ),
        out_shape=list(outs),
        compiler_params=params(),
        cost_estimate=cost(6),
        name=name,
    )(info, *held.arrays, *deps)


def norm_parts(v):
    mean = jnp.mean(v, axis=-1, keepdims=True)
    c = v - mean
    inv = lax.rsqrt(jnp.mean(c * c, axis=-1, keepdims=True) + 1e-05)
    return c * inv, inv


def norm_back(y, inv, g):
    return inv * (g - jnp.mean(g, axis=-1, keepdims=True) - y * jnp.mean(g * y, axis=-1, keepdims=True))


def gelu_pair(v):
    phi = 0.5 + 0.5 * lax.erf(v * 0.7071067811865476)
    pdf = jnp.exp(v * v * -0.5) * 0.3989422804014327
    return v * phi, phi + v * pdf


def put_slots(info_ref, value, first, second):
    C = value.shape[0] // 2
    for k, ref in enumerate((first, second)):
        ref[...] = value[pl.ds(pl.multiple_of((info_ref[2] ^ k) * C, 16), C)].astype(BF)


def project_qkv(info, x, w_query, w_key, w_value, deps):
    T, D = x.shape

    def body(info_ref, get, q, kv):
        xv = get(0)[...]
        kv[:, :D] = nn(xv, get(1)[...]).astype(BF)
        kv[:, D:] = nn(xv, get(2)[...]).astype(BF)
        q[...] = (nn(xv, get(3)[...]) * (0.125 * LOG2E)).astype(BF)

    return fused("qkv", info, body, [x, w_key, w_value, w_query], [shape(T, D, BF), shape(T, 2 * D, BF)], deps=deps)


def project_source(info, x, w_key, w_value, deps):
    T, D = x.shape

    def body(info_ref, get, kv):
        xv = get(0)[...]
        kv[:, :D] = nn(xv, get(1)[...]).astype(BF)
        kv[:, D:] = nn(xv, get(2)[...]).astype(BF)

    return fused("source_kv", info, body, [x, w_key, w_value], [shape(T, 2 * D, BF)], deps=deps)[0]


def attend_self(info, q, kv, kv_peer, masks, deps):
    return attend(SELF_PLANS, info, q, kv, kv_peer, *masks, [], [], lambda get, att: None, deps)


def between(info, x, att, w_out, c_query, src, c_key, c_value, deps):
    T, D = x.shape

    def body(info_ref, get, kv, y_ref, low_ref, inv_ref, cq_ref):
        xv = get(0)[...]
        kv[:, :D] = nn(xv, get(1)[...]).astype(BF)
        kv[:, D:] = nn(xv, get(2)[...]).astype(BF)
        y, inv = norm_parts(get(5)[...].astype(F32) + nn(get(3)[...], get(4)[...]))
        low = y.astype(BF)
        y_ref[...] = y
        low_ref[...] = low
        inv_ref[...] = jnp.broadcast_to(inv, inv_ref.shape)
        cq_ref[...] = (nn(low, get(6)[...]) * (0.125 * LOG2E)).astype(BF)

    outs = [shape(T, 2 * D, BF), shape(T, D, F32), shape(T, D, BF), shape(T, 128, F32), shape(T, D, BF)]
    return fused("between", info, body, [src, c_key, c_value, att, w_out, x, c_query], outs, deps=deps)


def attend_cross(info, q, kv, kv_peer, masks, y1, c_out, down, up, scale):
    T, D = q.shape
    A = down.shape[1]

    def finish(get, att, low_ref, inv_ref, sq_ref, gn_ref, base_ref):
        y, inv = norm_parts(get(1)[...] + nn(att[...], get(0)[...]))
        inv_ref[...] = jnp.broadcast_to(inv, inv_ref.shape)
        low = y.astype(BF)
        low_ref[...] = low
        h, g = gelu_pair(nn(low, get(2)[...]))
        hb = h.astype(BF)
        sq_ref[...] = hb
        gn_ref[...] = g.astype(BF)
        base_ref[...] = y + get(4)[0:1, 0:1] * nn(hb, get(3)[...])

    outs = [shape(T, D, BF), shape(T, 128, F32), shape(T, A, BF), shape(T, A, BF), shape(T, D, F32)]
    return attend(CROSS_PLANS, info, q, kv, kv_peer, *masks, [c_out, y1, down, up, scale], outs, finish)


def expand(info, x, first, second, block=1024):
    T, D = x.shape
    width = first.shape[1]
    F = 2 * width
    per = width // block
    held = Loads([first, second])

    def kernel(info_ref, x_ref, *refs):
        ins, (h_ref, g_ref, *scratch) = refs[: len(held.arrays)], refs[len(held.arrays) :]
        i = pl.program_id(0)
        bound = held.bind(info_ref, ins, scratch)
        pl.when(i == 0)(lambda: start_all(bound))
        cols = pl.ds(pl.multiple_of(lax.rem(i, per) * block, 128), block)
        for v, (copies, buf) in enumerate(bound):
            @pl.when(i == v * per)
            def _():
                for c in copies:
                    c.wait()

            @pl.when(i // per == v)
            def _():
                h, g = gelu_pair(nn(x_ref[...], buf[:, cols]))
                h_ref[...] = h.astype(BF)
                g_ref[...] = g.astype(BF)

    out = pl.BlockSpec((T, block), lambda i, *_: (0, i))
    return pl.pallas_call(
        kernel,
        grid_spec=pltpu.PrefetchScalarGridSpec(
            num_scalar_prefetch=1,
            grid=(F // block,),
            in_specs=[pl.BlockSpec((T, D), lambda i, *_: (0, 0))] + held.specs,
            out_specs=[out, out],
            scratch_shapes=held.scratch,
        ),
        out_shape=[shape(T, F, BF)] * 2,
        compiler_params=params(),
        cost_estimate=cost(12),
        name="expand",
    )(info, x, *held.arrays)


def contract(info, h, c, base, low, sq, gn, up, g_out, scale, block=2048):
    T, D = base.shape
    F = c.shape[0]
    A = sq.shape[1]
    held = Loads([base, g_out, scale, sq, up, gn, low])

    def kernel(info_ref, h_ref, c_ref, *refs):
        ins = refs[: len(held.arrays)]
        out0, out1, g3_ref, kept_ref, sent_ref, gnar_ref, acc, *scratch = refs[len(held.arrays) :]
        i = pl.program_id(0)
        bound = held.bind(info_ref, ins, scratch)
        pl.when(i == 0)(lambda: start_all(bound))

        @pl.when(i == 0)
        def _():
            acc[...] = nn(h_ref[...], c_ref[...])

        @pl.when(i > 0)
        def _():
            acc[...] += nn(h_ref[...], c_ref[...])

        @pl.when(i == F // block - 1)
        def _():
            get = getter(bound)
            y, inv = norm_parts(acc[...] + get(0)[...])
            g3 = norm_back(y, inv, get(1)[...].astype(F32))
            g3_ref[...] = g3
            acc[...] = y
            put_slots(info_ref, acc, out0, out1)
            ga = (get(2)[0:1, 0:1] * g3).astype(BF)
            gup = tn(get(3)[...], ga).astype(BF)
            gnar = (get(5)[...].astype(F32) * nt(ga, get(4)[...])).astype(BF)
            gnar_ref[...] = gnar
            gdown = tn(gnar, get(6)[...]).astype(BF)
            for side, keep, send in ((0, gup, gdown), (1, gdown, gup)):
                @pl.when(info_ref[3] == side)
                def _():
                    kept_ref[...] = keep
                    sent_ref[...] = send

    outs = [shape(T // 2, D, BF)] * 2 + [shape(T, D, F32), shape(A, D, BF), shape(A, D, BF), shape(T, A, BF)]
    return pl.pallas_call(
        kernel,
        grid_spec=pltpu.PrefetchScalarGridSpec(
            num_scalar_prefetch=1,
            grid=(F // block,),
            in_specs=[pl.BlockSpec((T, block), lambda i, *_: (0, i)), pl.BlockSpec((block, D), lambda i, *_: (i, 0))]
            + held.specs,
            out_specs=[pl.BlockSpec(o.shape, lambda i, *_: (0, 0)) for o in outs],
            scratch_shapes=[pltpu.VMEM((T, D), F32)] + held.scratch,
        ),
        out_shape=outs,
        compiler_params=params(),
        cost_estimate=cost(14),
        name="contract",
    )(info, h, c, *held.arrays)


def ffn_back(info, g3, c, first, second, gp, gnar, down, low, inv, c_out, deps, block=1024):
    T, D = g3.shape
    F = c.shape[0]
    width = first.shape[1]
    per = width // block
    held = Loads([first, second, gnar, down, c_out, low, inv])

    def kernel(info_ref, g3_ref, c_ref, gp_ref, *refs):
        ins = refs[: len(held.arrays)]
        g2_ref, ga_ref, acc, *scratch = refs[len(held.arrays) + len(deps) :]
        i = pl.program_id(0)
        bound = held.bind(info_ref, ins, scratch)
        pl.when(i == 0)(lambda: start_all(bound))
        gh = (nt(g3_ref[...].astype(BF), c_ref[...]) * gp_ref[...].astype(F32)).astype(BF)

        @pl.when(i == 0)
        def _():
            acc[...] = g3_ref[...]

        for v in range(2):
            copies, e = bound[v]

            @pl.when(i == v * per)
            def _():
                for copy in copies:
                    copy.wait()

            @pl.when(i // per == v)
            def _():
                acc[...] += nt(gh, e[:, pl.ds(pl.multiple_of(lax.rem(i, per) * block, 128), block)])

        @pl.when(i == F // block - 1)
        def _():
            get = getter(bound)
            g2 = norm_back(get(5)[...].astype(F32), get(6)[:, 0:1], acc[...] + nt(get(2)[...], get(3)[...]))
            g2_ref[...] = g2
            ga_ref[...] = nt(g2.astype(BF), get(4)[...]).astype(BF)

    outs = [shape(T, D, F32), shape(T, D, BF)]
    return pl.pallas_call(
        kernel,
        grid_spec=pltpu.PrefetchScalarGridSpec(
            num_scalar_prefetch=1,
            grid=(F // block,),
            in_specs=[pl.BlockSpec((T, D), lambda i, *_: (0, 0)), pl.BlockSpec((block, D), lambda i, *_: (i, 0)),
                      pl.BlockSpec((T, block), lambda i, *_: (0, i))] + held.specs + [ANYWHERE] * len(deps),
            out_specs=[pl.BlockSpec(o.shape, lambda i, *_: (0, 0)) for o in outs],
            scratch_shapes=[pltpu.VMEM((T, D), F32)] + held.scratch,
        ),
        out_shape=outs,
        compiler_params=params(),
        cost_estimate=cost(18),
        name="ffn_back",
    )(info, g3, c, gp, *held.arrays, *deps)


def attend_cross_back(info, q, kv, kv_peer, do, o, r, p, g2, y1, inv1, c_query, w_out, deps):
    T, D = q.shape

    def finish(get, gq, g1_ref, ga_ref):
        g = get(1)[...] + 0.125 * nt(gq[...], get(0)[...])
        g1 = norm_back(get(2)[...].astype(F32), get(3)[:, 0:1], g)
        g1_ref[...] = g1
        ga_ref[...] = nt(g1.astype(BF), get(4)[...]).astype(BF)

    return attend_back(CROSS_PLANS, info, q, kv, kv_peer, do, o, r, p, [c_query, g2, y1, inv1, w_out],
                       [shape(T, D, F32), shape(T, D, BF)], finish, deps)


def attend_self_back(info, q, kv, kv_peer, do, o, r, p, g1, w_query, deps):
    T, D = q.shape

    def finish(get, gq, acc_ref):
        acc_ref[...] = get(1)[...] + 0.125 * nt(gq[...], get(0)[...])

    return attend_back(SELF_PLANS, info, q, kv, kv_peer, do, o, r, p, [w_query, g1], [shape(T, D, F32)], finish, deps)


def add_pairs(mine, got, part):
    D = mine.shape[1] // 2
    out = []
    for h in range(D // 128):
        at = slice(256 * h + 128 * part, 256 * h + 128 * part + 128)
        out.append((mine[:, at].astype(F32) + got[:, at].astype(F32)).astype(BF))
    return jnp.concatenate(out, axis=1)


def source_grad(info, gkv, got, w_key, w_value, deps):
    T, D = gkv.shape[0], gkv.shape[1] // 2

    def body(info_ref, get, out0, out1, total):
        mine, other = get(0), get(1)
        acc = nt(add_pairs(mine, other, 0), get(2)[...])
        total[...] = acc + nt(add_pairs(mine, other, 1), get(3)[...])
        put_slots(info_ref, total, out0, out1)

    return fused("source_grad", info, body, [gkv, got, w_key, w_value], [shape(T // 2, D, BF)] * 2, deps=deps,
                 extra=[pltpu.VMEM((T, D), F32)])


def token_grad(info, acc, gkv, got, w_key, w_value, deps):
    T, D = acc.shape

    def body(info_ref, get, out0, out1):
        mine, other = get(0), get(1)
        total = nt(add_pairs(mine, other, 0), get(2)[...])
        total += nt(add_pairs(mine, other, 1), get(3)[...])
        g = get(4)
        g[...] += total
        put_slots(info_ref, g, out0, out1)

    return fused("token_grad", info, body, [gkv, got, w_key, w_value, acc], [shape(T // 2, D, BF)] * 2, deps=deps)


def move(value, target):
    dp, seq = lax.axis_size("dp"), lax.axis_size("seq")
    pairs = []
    for d in range(dp):
        for s in range(seq):
            a, b = target(d, s)
            pairs.append((d * seq + s, a * seq + b))
    return lax.ppermute(value, ("dp", "seq"), pairs)


def flip(value, bit):
    return move(value, lambda d, s: (d ^ bit, s))


def core_of(chunk):
    return (0, 1, 1, 0)[chunk]


def pick(flag, first, second):
    return jnp.where(flag, first, second)


def send_pieces(pieces):
    return [
        move(piece, lambda a, q, k=k: (2 * (a // 2) + core_of(q), 2 * (a % 2) + (q + k) % 2))
        for k, piece in enumerate(pieces)
    ]


def take_pieces(value, s):
    return [lax.dynamic_index_in_dim(value, (s + k) % 2, 0, keepdims=False) for k in range(2)]


def send_back(pieces):
    dp, seq = lax.axis_size("dp"), lax.axis_size("seq")
    got = []
    for k, piece in enumerate(pieces):
        back = {}
        for a in range(dp):
            for q in range(seq):
                back[(2 * (a // 2) + core_of(q), 2 * (a % 2) + (q + k) % 2)] = (a, q)
        got.append(move(piece, lambda a, b: back[(a, b)]))
    return got


def join_rows(got, s):
    even = s % 2 == 0
    return jnp.stack([pick(even, got[0], got[1]), pick(even, got[1], got[0])])


def first_hop(pair, low):
    return [flip(pair[0], 2 * low), flip(pair[1], 4 * low)]


def second_hop(near, low):
    return [flip(near[0], 4 * low), flip(near[1], 2 * low)]


def all_parts(near, far, low):
    out = []
    for v in range(2):
        half = near[v].shape[0] // 2
        b1, b2 = ((2, 4), (4, 2))[v]
        arrays = [near[v], far[v], flip(near[v], low), flip(far[v], low)]
        parts = {}
        for a, m in zip(arrays, (0, b2, 1, b2 ^ 1)):
            parts[m] = (a, 0)
            parts[m ^ b1] = (a, half)
        out.append([parts[m] for m in range(8)])
    return out


class Reduce:
    def __init__(self, kept, sent, d, s, low):
        self.d, self.s, self.low = d, s, low
        self.kept, self.got = kept, [flip(sent, low)]

    def plane(self, v, m):
        return flip(v, 2 * self.low * m)

    def scatter_plane(self):
        me = self.d // (2 * self.low)
        parts = self.value.reshape(4, -1, self.value.shape[1])
        take = [lax.dynamic_index_in_dim(parts, me ^ m, 0, keepdims=False) for m in range(4)]
        self.kept, self.got = take[0], [self.plane(take[m], m) for m in range(1, 4)]

    def line(self, bit):
        self.kept, self.got = self.value, [move(self.value, lambda a, b: (a, b ^ bit))]

    def add(self):
        total = self.kept.astype(F32)
        for got in self.got:
            total += got.astype(F32)
        self.value = total.astype(BF)

    def low_bits(self):
        bit = 1
        while bit < self.low:
            got = flip(self.value, bit)
            self.value = (self.value.astype(F32) + got.astype(F32)).astype(BF)
            bit *= 2

    def gather_plane(self):
        self.me = self.d // (2 * self.low)
        self.got = [self.value] + [self.plane(self.value, m) for m in range(1, 4)]

    def put(self):
        got = self.got
        n, rows = len(got), []
        for j in range(n):
            part = got[n - 1]
            for m in range(n - 1):
                part = pick((self.me ^ j) == m, got[m], part)
            rows.append(part)
        self.value = jnp.concatenate(rows, axis=0)


def local(tokens, source, target_lengths, source_lengths, step_index, self_query, self_key, self_value,
          self_out, cross_query, cross_key, cross_value, cross_out, ffn_expand, ffn_contract, adapter_down,
          adapter_up, grad_output):
    rows, C, D = tokens.shape
    dp, seq = lax.axis_size("dp"), lax.axis_size("seq")
    assert rows == 2 and seq == 4 and dp % 8 == 0
    low = dp // 8
    d, s = lax.axis_index("dp"), lax.axis_index("seq")
    core = d % 2
    info = jnp.stack([core, d // low, (s + d) % 2, (d // low) % 2]).astype(jnp.int32)

    def widen(shard):
        if low == 1:
            return shard
        groups = [[g * low + i for i in range(low)] for g in range(8)]
        return lax.all_gather(shard, "dp", axis=0, tiled=True, axis_index_groups=groups)

    def rows_of(*weights):
        return jnp.concatenate(weights, axis=0)

    t = send_pieces(take_pieces(tokens, s))
    sq, sk, sv, ex = [widen(w) for w in (self_query, self_key, self_value, ffn_expand)]
    n = sq.shape[0]
    h = n // 2
    pair = [rows_of(sk, sv[:h]), rows_of(sq, sv[h:])]
    rest = rows_of(self_out, cross_key, cross_value, cross_query, cross_out)
    near = beside(pair, first_hop(pair, low), (t[0],))
    e1, e2, c_shard = stage(ex, ffn_contract, near)
    rest = lax.all_gather(rest, "dp", axis=0, tiled=True)
    each = self_out.shape[0]
    w_out, c_key, c_value, c_query, c_out = [Shards(rest, dp, j * each, each) for j in range(5)]

    mine = jnp.concatenate([target_lengths, source_lengths[:, None]], axis=1)
    other = flip(mine, 1)
    table = jnp.concatenate([pick(core == 0, mine, other), pick(core == 0, other, mine)], axis=0)
    row = lax.dynamic_index_in_dim(table, s, 0, keepdims=False)
    lens, src_len = row[:-1], row[-1]
    docs = lens.shape[0]
    ends = jnp.cumsum(lens)[:-1]
    i = jnp.arange(2 * C, dtype=jnp.int32)
    slot = i // C

    def place(which):
        chunk = pick(which == 0, slot * 3, slot + 1)
        return chunk * C + i % C

    lanes = jnp.arange(128, dtype=jnp.int32) % 64

    def doc_hot(pos):
        doc = jnp.sum((pos[:, None] >= ends[None, :]).astype(jnp.int32), axis=-1)
        return doc[:, None] == lanes[None, :]

    own_pos, peer_pos = place(core), place(1 - core)
    k_aug = [doc_hot(own_pos).astype(BF), doc_hot(peer_pos).astype(BF)]
    q_aug = jnp.where(doc_hot(own_pos) | (lanes >= docs)[None, :], 0.0, NEG).astype(BF)
    ck_aug = [((pos[:, None] >= src_len) & (lanes == 0)[None, :]).astype(BF) for pos in (own_pos, peer_pos)]
    cq_aug = jnp.broadcast_to(jnp.where(lanes == 0, NEG, 0.0).astype(BF)[None, :], (2 * C, 128))

    scale = jnp.full((8, 128), (step_index[0] + 1).astype(F32) / 5.0, F32)
    src = send_pieces(gate(take_pieces(source, s), t))
    far = gate(
        second_hop(near, low), (*src, info, q_aug, *k_aug, cq_aug, *ck_aug, scale, e1, e2)
    )
    a1, b1 = all_parts(near, far, low)
    w_key, w_query = Pieces(n, (a1, 0, n, 0)), Pieces(n, (b1, 0, n, 0))
    w_value = Pieces(n, (a1, n, h, 0), (b1, n, h, h))
    x = Slots(t, 0, C)
    q, kv = project_qkv(info, x, w_query, w_key, w_value, ())
    q, kv, e1, e2 = barrier(q, kv, e1, e2)
    kv_peer = flip(kv, 1)
    first3, second3 = first_hop([e1, e2], low), second_hop([e1, e2], low)
    attended, p_self, r_self = attend_self(info, q, kv, kv_peer, (q_aug, *k_aug), ())
    *first3, attended, c_shard = barrier(*first3, attended, c_shard)
    w_contract = lax.all_gather(c_shard, "dp", axis=0, tiled=True)
    far3 = second_hop(first3, low)
    flips = [flip(v, low) for v in (e1, e2, *first3)]
    skv, y1, y1_low, inv1, cq = between(info, x, attended, w_out, c_query, Slots(src, 0, C), c_key, c_value, ())
    *flips, skv, cq, h0, h1, g0, g1 = barrier(*flips, skv, cq, *second3, *take_pieces(grad_output, s))
    second3, pieces = [h0, h1], [g0, g1]
    g_out = send_pieces(pieces)
    skv_peer = flip(skv, 1)
    cross_attended, p_cross, r_cross, second_low, inv2, squeezed, gn, base = attend_cross(
        info, cq, skv, skv_peer, (cq_aug, *ck_aug), y1, c_out, adapter_down, adapter_up, scale
    )
    f0, f1, h0, h1, g0, g1, second_low = barrier(*far3, *second3, *g_out, second_low)
    far3, second3, g_out = [f0, f1], [h0, h1], [g0, g1]
    a3, b3 = [
        [(v, 0) for _, v in sorted(
            {0: own, 1: flips[i], b1: first3[i], b1 ^ 1: flips[2 + i], b2: second3[i], b2 ^ 1: flip(second3[i], low),
             6: far3[i], 7: flip(far3[i], low)}.items()
        )]
        for i, (own, b1, b2) in enumerate(((e1, 2, 4), (e2, 4, 2)))
    ]
    ea, eb = Pieces(n, (a3, 0, n, 0)), Pieces(n, (b3, 0, n, 0))
    hidden, gp = expand(info, second_low, ea, eb)
    o0, o1, g3, kept, sent, gnar = contract(
        info, hidden, w_contract, base, second_low, squeezed, gn, adapter_up, Slots(g_out, 0, C), scale
    )
    output = send_back([o0, o1])
    total = Reduce(kept, sent, d, s, low)
    g2, grad_cross = ffn_back(info, g3, w_contract, ea, eb, gp, gnar, adapter_down, second_low, inv2, c_out, ())
    *total.got, g2, grad_cross = barrier(*total.got, g2, grad_cross)
    total.add()
    total.scatter_plane()
    gkv, gkv_peer, g1, grad_self = attend_cross_back(
        info, cq, skv, skv_peer, grad_cross, cross_attended, r_cross, p_cross, g2, y1_low, inv1, c_query, w_out, (total.kept,)
    )
    *total.got, o0, o1, grad_self, gkv_peer = barrier(*total.got, *output, grad_self, gkv_peer)
    output = [o0, o1]
    total.add()
    total.line(2)
    got = flip(gkv_peer, 1)
    pieces = source_grad(info, gkv, got, c_key, c_value, (grad_self, total.kept))
    pieces = send_back(pieces)
    gkv, gkv_peer, acc = attend_self_back(
        info, q, kv, kv_peer, grad_self, attended, r_self, p_self, g1, w_query, pieces[:0]
    )
    *total.got, s0, s1, gkv_peer = barrier(*total.got, *pieces, gkv_peer)
    got = flip(gkv_peer, 1)
    total.add()
    total.line(1)
    pieces = token_grad(info, acc, gkv, got, w_key, w_value, (total.kept,))
    *total.got, o0, o1, s0, s1, t0, t1 = barrier(*total.got, *output, s0, s1, *pieces)
    tokens_back = send_back([t0, t1])
    output = [o0, o1]
    total.add()
    total.low_bits()
    total.gather_plane()
    total.put()
    grads, other = total.value, flip(total.value, low)
    high = (d // low) % 2 == 1
    grad_up = pick(high, other, grads).astype(F32)
    grad_down = pick(high, grads, other).astype(F32).T
    output, grad_source, grad_tokens = [join_rows(v, s) for v in (output, [s0, s1], tokens_back)]
    return (output, grad_tokens, grad_source, grad_down, grad_up)


def solution(mesh):
    rows = P("dp", "seq", None)
    weight = P("dp", None)
    return jax.shard_map(
        local,
        mesh=mesh,
        in_specs=(rows, rows, weight, P("dp"), P()) + (weight,) * 10 + (P(), P(), rows),
        out_specs=(rows, rows, rows, P(), P()),
        check_vma=False,
    )
```

```python
import functools

import jax
import jax.numpy as jnp
from jax import lax
from jax.experimental import pallas as pl
from jax.experimental.pallas import tpu as pltpu
from jax.sharding import PartitionSpec as P

BF, F32 = jnp.bfloat16, jnp.float32
NEG = -1e30
LOG2E = 1.4426950408889634
PER = 2

SELF_PLANS = (
    (((0, True),), ((0, False), (2, False), (3, False), (1, True))),
    (((2, False), (0, True)), ((2, False), (0, False), (1, True))),
)
CROSS_PLANS = ((((0, False), (1, False), (2, False), (3, False)),) * 2,)


def nt(a, b):
    return lax.dot_general(a, b, (((1,), (1,)), ((), ())), preferred_element_type=F32)


def nn(a, b):
    return lax.dot_general(a, b, (((1,), (0,)), ((), ())), preferred_element_type=F32)


def tn(a, b):
    return lax.dot_general(a, b, (((0,), (0,)), ((), ())), preferred_element_type=F32)


def cost(us):
    return pl.CostEstimate(flops=int(us * 3e8), bytes_accessed=1024, transcendentals=0)


def params():
    return pltpu.CompilerParams(vmem_limit_bytes=64 * 1024 * 1024)


def shape(rows, cols, dtype):
    return jax.ShapeDtypeStruct((rows, cols), dtype)


class Whole:
    def __init__(self, array):
        self.arrays, self.shape, self.dtype, self.count = [array], array.shape, array.dtype, 1

    def copies(self, info, refs, buf, sem, first):
        return [pltpu.make_async_copy(refs[0], buf, sem.at[first])]


class Pieces:
    def __init__(self, stride, *pieces):
        self.stride, self.pieces = stride, pieces
        self.arrays = [a for parts, *_ in pieces for a, _ in parts]
        self.shape, self.dtype = (8 * stride, self.arrays[0].shape[1]), self.arrays[0].dtype
        self.count = len(self.arrays)

    def copies(self, info, refs, buf, sem, first):
        out = []
        for parts, at, rows, base in self.pieces:
            for m, (_, start) in enumerate(parts):
                to = pl.multiple_of((info[1] ^ m) * self.stride + base, 16)
                i = len(out)
                out.append(
                    pltpu.make_async_copy(
                        refs[i].at[pl.ds(start + at, rows)], buf.at[pl.ds(to, rows)], sem.at[first + i]
                    )
                )
        return out


class Shards:
    def __init__(self, array, owners, at, rows):
        self.arrays, self.count, self.at, self.rows = [array], owners, at, rows
        self.each = array.shape[0] // owners
        self.shape, self.dtype = (owners * rows, array.shape[1]), array.dtype

    def copies(self, info, refs, buf, sem, first):
        return [
            pltpu.make_async_copy(
                refs[0].at[pl.ds(j * self.each + self.at, self.rows)],
                buf.at[pl.ds(j * self.rows, self.rows)],
                sem.at[first + j],
            )
            for j in range(self.count)
        ]


class Slots:
    def __init__(self, arrays, at, rows):
        self.arrays, self.at, self.rows, self.count = list(arrays), at, rows, 2
        self.shape, self.dtype = (2 * rows, arrays[0].shape[1]), arrays[0].dtype

    def copies(self, info, refs, buf, sem, first):
        return [
            pltpu.make_async_copy(
                refs[k].at[pl.ds(self.at, self.rows)],
                buf.at[pl.ds(pl.multiple_of((info[2] ^ k) * self.rows, 16), self.rows)],
                sem.at[first + k],
            )
            for k in range(2)
        ]


class Chunk:
    def __init__(self, array, k):
        self.arrays, self.k, self.count = [array], k, 1
        self.shape, self.dtype = (array.shape[0] // 2, array.shape[1]), array.dtype

    def copies(self, info, refs, buf, sem, first):
        rows = self.shape[0]
        at = pl.multiple_of((info[2] ^ self.k) * rows, 16)
        return [pltpu.make_async_copy(refs[0].at[pl.ds(at, rows)], buf, sem.at[first])]


class Loads:
    def __init__(self, loads):
        self.loads = [v if hasattr(v, "copies") else Whole(v) for v in loads]
        self.arrays = [a for v in self.loads for a in v.arrays]
        self.specs = [pl.BlockSpec(memory_space=pl.ANY)] * len(self.arrays)
        self.scratch = [pltpu.VMEM(v.shape, v.dtype) for v in self.loads]
        self.scratch.append(pltpu.SemaphoreType.DMA((sum(v.count for v in self.loads),)))

    def bind(self, info, refs, scratch):
        bufs, sem = scratch[:-1], scratch[-1]
        at = first = 0
        out = []
        for v, buf in zip(self.loads, bufs):
            out.append((v.copies(info, refs[at : at + len(v.arrays)], buf, sem, first), buf))
            at += len(v.arrays)
            first += v.count
        return out


def start_all(bound):
    for copies, _ in bound:
        for c in copies:
            c.start()


def getter(bound):
    ready = set()

    def get(i):
        copies, buf = bound[i]
        if i not in ready:
            for c in copies:
                c.wait()
            ready.add(i)
        return buf

    return get


ANYWHERE = pl.BlockSpec(memory_space=pl.ANY)


def half_mask(shape, h):
    lane = lax.broadcasted_iota(jnp.int32, shape, 1)
    return (lane < 64) if h == 0 else (lane >= 64)


def top(parts):
    rows = 64
    pieces = [p[i : i + rows] for p in parts for i in range(0, p.shape[0], rows)]
    while len(pieces) > 1:
        pieces = [jnp.maximum(*pieces[i : i + 2]) if i + 1 < len(pieces) else pieces[i] for i in range(0, len(pieces), 2)]
    return jnp.max(pieces[0], axis=0, keepdims=True)


def forward_pair(plan, C, q, ks, vs, qa, kas, put, p_ref):
    kaug = [[jnp.where(half_mask(k.shape, h), k, a) for k, a in zip(ks, kas)] for h in range(2)]
    vts = [v.T for v in vs]
    ones = jnp.ones((16, C), BF)
    units, n = [], 0
    for slot, blocks in enumerate(plan):
        units += [(slot, h, n, blocks) for h in range(2)]
        n += len(blocks)

    def scores_of(unit):
        slot, h, _, blocks = unit
        rows = slice(slot * C, (slot + 1) * C)
        qh = jnp.where(half_mask((C, 128), h), q[rows], qa[rows])
        scores = []
        for kb, diagonal in blocks:
            s = nt(kaug[h][kb], qh)
            if diagonal:
                ki = lax.broadcasted_iota(jnp.int32, s.shape, 0)
                qi = lax.broadcasted_iota(jnp.int32, s.shape, 1)
                s = jnp.where(ki <= qi, s, NEG)
            scores.append(s)
        return scores, top(scores)

    def rest(unit, scores, m):
        _, h, n, blocks = unit
        ps = [jnp.exp2(s - m).astype(BF) for s in scores]
        for i, p in enumerate(ps):
            p_ref[h, n + i] = p
        values = [jnp.concatenate([vts[kb][64 * h : 64 * h + 64], ones], axis=0) for kb, _ in blocks]
        both = nn(jnp.concatenate(values, axis=1), jnp.concatenate(ps, axis=0))
        inv = 1.0 / both[64:65]
        return both[:64] * inv, jnp.broadcast_to(inv, (64, C))

    done = []
    AHEAD = 2
    pending = [scores_of(u) for u in units[:AHEAD]]
    for i, unit in enumerate(units):
        if i + AHEAD < len(units):
            pending.append(scores_of(units[i + AHEAD]))
        done.append(rest(unit, *pending[i]))
        if i % 2:
            halves, inverses = zip(*done[-2:])
            put(unit[0], jnp.concatenate(halves, axis=0).T.astype(BF), jnp.concatenate(inverses, axis=0).T)


def by_plan(plans, info, run):
    if len(plans) == 1:
        run(plans[0])
    else:
        for v, plan in enumerate(plans):
            pl.when(info[0] == v)(functools.partial(run, plan))


def attend(plans, info, q, own, peer, qa, kao, kap, loads, outs, finish, deps=()):
    T, D = q.shape
    C, pairs = T // 2, D // 128
    steps = pairs // PER
    nb = sum(len(b) for b in plans[0])
    held = Loads(loads)

    def kernel(info_ref, q_ref, ko, vo, kp, vp, qa_ref, kao_ref, kap_ref, *refs):
        ins = refs[: len(held.arrays)]
        o_ref, p_ref, r_ref, *out_refs = refs[len(held.arrays) + len(deps) :][: 3 + len(outs)]
        att, *scratch = refs[len(held.arrays) + len(deps) + 3 + len(outs) :]
        step = pl.program_id(0)
        bound = held.bind(info_ref, ins, scratch)
        pl.when(step == 0)(lambda: start_all(bound))

        def run(plan):
            for j in range(PER):
                at = slice(128 * j, 128 * j + 128)
                cols = pl.ds(pl.multiple_of((step * PER + j) * 128, 128), 128)

                def put(slot, value, inverse):
                    o_ref[slot * C : (slot + 1) * C, at] = value
                    r_ref[slot * C : (slot + 1) * C, at] = inverse
                    att[slot * C : (slot + 1) * C, cols] = value

                def chunks(*rs):
                    return [r[i * C : (i + 1) * C, at] for r in rs for i in range(2)]

                masks = [m[i * C : (i + 1) * C] for m in (kao_ref, kap_ref) for i in range(2)]
                forward_pair(plan, C, q_ref[:, at], chunks(ko, kp), chunks(vo, vp), qa_ref[...], masks, put, p_ref.at[j])

        by_plan(plans, info_ref, run)

        @pl.when(step == steps - 1)
        def _():
            finish(getter(bound), att, *out_refs)

    col = pl.BlockSpec((T, 128 * PER), lambda h, *_: (0, h))
    val = pl.BlockSpec((T, 128 * PER), lambda h, *_: (0, steps + h))
    fix = pl.BlockSpec((T, 128), lambda h, *_: (0, 0))
    return pl.pallas_call(
        kernel,
        grid_spec=pltpu.PrefetchScalarGridSpec(
            num_scalar_prefetch=1,
            grid=(steps,),
            in_specs=[col] + [col, val] * 2 + [fix] * 3 + held.specs + [ANYWHERE] * len(deps),
            out_specs=[col, pl.BlockSpec((PER, 2, nb, C, C), lambda h, *_: (h, 0, 0, 0, 0)), col]
            + [pl.BlockSpec(o.shape, lambda h, *_: (0, 0)) for o in outs],
            scratch_shapes=[pltpu.VMEM((T, D), BF)] + held.scratch,
        ),
        out_shape=[shape(T, D, BF), jax.ShapeDtypeStruct((pairs, 2, nb, C, C), BF), shape(T, D, F32)] + list(outs),
        compiler_params=params(),
        cost_estimate=cost(25),
        name="attend",
    )(info, q, own, own, peer, peer, qa, kao, kap, *held.arrays, *deps)


def backward_pair(plan, C, q, ks, vs, do, o, r, p_ref, put, gown, gpeer):
    lane = lax.broadcasted_iota(jnp.int32, (C, 128), 1)
    l64 = lax.rem(lane, 64)
    ones = jnp.where(l64 < 2, 1.0, 0.0).astype(BF)
    vaug = [[jnp.where(half_mask(v.shape, h), v, ones) for v in vs] for h in range(2)]
    kts = [k.T for k in ks]
    by_key = [[] for _ in range(4)]
    zero = jnp.zeros((C, 128), BF)
    units, n = [], 0
    for slot, blocks in enumerate(plan):
        units += [(slot, h, n, blocks) for h in range(2)]
        n += len(blocks)

    def probs_back(unit):
        slot, h, n, blocks = unit
        rows = slice(slot * C, (slot + 1) * C)
        scaled = do[rows].astype(F32) * r[rows]
        dos = scaled.astype(BF)
        hm = lane < 64 if h == 0 else lane >= 64
        d = -jnp.sum(jnp.where(hm, scaled * o[rows].astype(F32), 0.0), axis=1, keepdims=True)
        hi = d.astype(BF)
        lo = (d - hi.astype(F32)).astype(BF)
        tail = jnp.where(l64 == 0, jnp.broadcast_to(hi, (C, 128)), jnp.where(l64 == 1, jnp.broadcast_to(lo, (C, 128)), zero))
        doa = jnp.where(hm, dos, tail)
        return [nt(vaug[h][kb], doa) for kb, _ in blocks], jnp.where(hm, dos, zero), jnp.where(hm, q[rows], zero)

    def rest(unit, dps, dom, qm):
        slot, h, n, blocks = unit
        grads = []
        for i, ((kb, _), dp) in enumerate(zip(blocks, dps)):
            pb = p_ref[h, n + i]
            ds = (pb.astype(F32) * dp).astype(BF)
            grads.append(ds)
            by_key[kb].append((pb, ds, dom, qm))
        wide = jnp.concatenate([kts[kb][64 * h : 64 * h + 64] for kb, _ in blocks], axis=1)
        return nn(wide, jnp.concatenate(grads, axis=0))

    done = []
    BACK = 2
    pending = [probs_back(u) for u in units[:BACK]]
    for i, unit in enumerate(units):
        if i + BACK < len(units):
            pending.append(probs_back(units[i + BACK]))
        done.append(rest(unit, *pending[i]))
        if i % 2:
            put(unit[0], jnp.concatenate(done[-2:], axis=0).T.astype(BF))
    for kb in range(4):
        ref = gown if kb < 2 else gpeer
        rows = slice((kb % 2) * C, (kb % 2) * C + C)
        if by_key[kb]:
            pbs, dss, doms, qms = zip(*by_key[kb])
            gk = nn(jnp.concatenate(dss, axis=1), jnp.concatenate(qms, axis=0))
            gv = nn(jnp.concatenate(pbs, axis=1), jnp.concatenate(doms, axis=0))
        else:
            gk = gv = jnp.zeros((C, 128), F32)
        ref[rows, 0:128] = (gk * (1.0 / LOG2E)).astype(BF)
        ref[rows, 128:256] = gv.astype(BF)


def attend_back(plans, info, q, own, peer, do, o, r, p, loads, outs, finish, deps=()):
    T, D = q.shape
    C, pairs, nb = T // 2, D // 128, p.shape[2]
    steps = pairs // PER
    held = Loads(loads)

    def kernel(info_ref, q_ref, ko, vo, kp, vp, do_ref, o_ref, r_ref, p_ref, *refs):
        ins = refs[: len(held.arrays)]
        gown, gpeer, *out_refs = refs[len(held.arrays) + len(deps) :][: 2 + len(outs)]
        gq, *scratch = refs[len(held.arrays) + len(deps) + 2 + len(outs) :]
        step = pl.program_id(0)
        bound = held.bind(info_ref, ins, scratch)
        pl.when(step == 0)(lambda: start_all(bound))

        def run(plan):
            for j in range(PER):
                at = slice(128 * j, 128 * j + 128)
                wide = slice(256 * j, 256 * j + 256)
                cols = pl.ds(pl.multiple_of((step * PER + j) * 128, 128), 128)

                def put(slot, value):
                    gq[slot * C : (slot + 1) * C, cols] = value

                def chunks(*rs):
                    return [r[i * C : (i + 1) * C, at] for r in rs for i in range(2)]

                backward_pair(plan, C, q_ref[:, at], chunks(ko, kp), chunks(vo, vp), do_ref[:, at], o_ref[:, at],
                              r_ref[:, at], p_ref.at[j], put, gown.at[:, wide], gpeer.at[:, wide])

        by_plan(plans, info_ref, run)

        @pl.when(step == steps - 1)
        def _():
            finish(getter(bound), gq, *out_refs)

    col = pl.BlockSpec((T, 128 * PER), lambda h, *_: (0, h))
    val = pl.BlockSpec((T, 128 * PER), lambda h, *_: (0, steps + h))
    wide = pl.BlockSpec((T, 256 * PER), lambda h, *_: (0, h))
    return pl.pallas_call(
        kernel,
        grid_spec=pltpu.PrefetchScalarGridSpec(
            num_scalar_prefetch=1,
            grid=(steps,),
            in_specs=[col] + [col, val] * 2 + [col] * 3
            + [pl.BlockSpec((PER, 2, nb, C, C), lambda h, *_: (h, 0, 0, 0, 0))] + held.specs + [ANYWHERE] * len(deps),
            out_specs=[wide] * 2 + [pl.BlockSpec(v.shape, lambda h, *_: (0, 0)) for v in outs],
            scratch_shapes=[pltpu.VMEM((T, D), BF)] + held.scratch,
        ),
        out_shape=[shape(T, 2 * D, BF)] * 2 + list(outs),
        compiler_params=params(),
        cost_estimate=cost(25),
        name="attend_back",
    )(info, q, own, own, peer, peer, do, o, r, p, *held.arrays, *deps)


def gate(values, deps):
    def kernel(*refs):
        del refs

    n = len(values)
    return pl.pallas_call(
        kernel,
        in_specs=[ANYWHERE] * (n + len(deps)),
        out_specs=[ANYWHERE] * n,
        out_shape=[jax.ShapeDtypeStruct(v.shape, v.dtype) for v in values],
        input_output_aliases={i: i for i in range(n)},
        cost_estimate=cost(0.1),
        name="gate",
    )(*values, *deps)


def barrier(*values):
    return gate(values, ())


def beside(pair, got, deps=()):
    def kernel(a, b, c, d, *refs):
        ab, cd = refs[-2:]
        n, m = a.shape[0], c.shape[0]
        ab[:n] = a[...]
        ab[n:] = b[...]
        cd[:m] = c[...]
        cd[m:] = d[...]

    full = pl.BlockSpec(memory_space=pltpu.VMEM)
    return pl.pallas_call(
        kernel,
        in_specs=[full] * 4 + [ANYWHERE] * len(deps),
        out_specs=[full] * 2,
        out_shape=[shape(2 * v.shape[0], v.shape[1], BF) for v in pair],
        cost_estimate=cost(2),
        compiler_params=params(),
        name="beside",
    )(pair[0], got[0], pair[1], got[1], *deps)


def join_up(arrays, deps):
    rows = [a.shape[0] for a in arrays]

    def kernel(*refs):
        at = 0
        for r, n in zip(refs, rows):
            refs[-1][at : at + n] = r[...]
            at += n

    full = pl.BlockSpec(memory_space=pltpu.VMEM)
    return pl.pallas_call(
        kernel,
        in_specs=[full] * len(arrays) + [ANYWHERE] * len(deps),
        out_specs=full,
        out_shape=shape(sum(rows), arrays[0].shape[1], BF),
        cost_estimate=cost(2),
        compiler_params=params(),
        name="join_up",
    )(*arrays, *deps)


def stage(expand_shard, contract_shard, deps):
    rows, cols = expand_shard.shape
    half = cols // 2

    def kernel(e_ref, c_ref, *refs):
        e1, e2, c = refs[-3:]
        e1[...] = e_ref[:, :half]
        e2[...] = e_ref[:, half:]
        c[...] = c_ref[...]

    full = pl.BlockSpec(memory_space=pltpu.VMEM)
    return pl.pallas_call(
        kernel,
        in_specs=[full, full] + [ANYWHERE] * len(deps),
        out_specs=[full] * 3,
        out_shape=[shape(rows, half, BF)] * 2 + [shape(*contract_shard.shape, BF)],
        cost_estimate=cost(3),
        compiler_params=params(),
        name="stage",
    )(expand_shard, contract_shard, *deps)


def fused(name, info, body, loads, outs, deps=(), extra=()):
    held = Loads(loads)
    total, nout = len(held.arrays), len(outs)

    def kernel(info_ref, *refs):
        out_refs = refs[total + len(deps) :][:nout]
        scratch = refs[total + len(deps) + nout :]
        bound = held.bind(info_ref, refs[:total], scratch[len(extra) :])
        start_all(bound)
        body(info_ref, getter(bound), *out_refs, *scratch[: len(extra)])

    return pl.pallas_call(
        kernel,
        grid_spec=pltpu.PrefetchScalarGridSpec(
            num_scalar_prefetch=1,
            grid=(1,),
            in_specs=held.specs + [ANYWHERE] * len(deps),
            out_specs=[pl.BlockSpec(o.shape, lambda i, *_: (0, 0)) for o in outs],
            scratch_shapes=list(extra) + held.scratch,
        ),
        out_shape=list(outs),
        compiler_params=params(),
        cost_estimate=cost(6),
        name=name,
    )(info, *held.arrays, *deps)


def norm_parts(v):
    mean = jnp.mean(v, axis=-1, keepdims=True)
    c = v - mean
    inv = lax.rsqrt(jnp.mean(c * c, axis=-1, keepdims=True) + 1e-05)
    return c * inv, inv


def norm_back(y, inv, g):
    return inv * (g - jnp.mean(g, axis=-1, keepdims=True) - y * jnp.mean(g * y, axis=-1, keepdims=True))


def gelu_pair(v):
    phi = 0.5 + 0.5 * lax.erf(v * 0.7071067811865476)
    pdf = jnp.exp(v * v * -0.5) * 0.3989422804014327
    return v * phi, phi + v * pdf


def put_slots(info_ref, value, first, second):
    C = value.shape[0] // 2
    for k, ref in enumerate((first, second)):
        ref[...] = value[pl.ds(pl.multiple_of((info_ref[2] ^ k) * C, 16), C)].astype(BF)


def project_qkv(info, x, w_query, w_key, w_value, deps):
    T, D = x.shape

    def body(info_ref, get, q, kv):
        xv = get(0)[...]
        kv[:, :D] = nn(xv, get(1)[...]).astype(BF)
        kv[:, D:] = nn(xv, get(2)[...]).astype(BF)
        q[...] = (nn(xv, get(3)[...]) * (0.125 * LOG2E)).astype(BF)

    return fused("qkv", info, body, [x, w_key, w_value, w_query], [shape(T, D, BF), shape(T, 2 * D, BF)], deps=deps)


def project_source(info, x, w_key, w_value, deps):
    T, D = x.shape

    def body(info_ref, get, kv):
        xv = get(0)[...]
        kv[:, :D] = nn(xv, get(1)[...]).astype(BF)
        kv[:, D:] = nn(xv, get(2)[...]).astype(BF)

    return fused("source_kv", info, body, [x, w_key, w_value], [shape(T, 2 * D, BF)], deps=deps)[0]


def attend_self(info, q, kv, kv_peer, masks, deps):
    return attend(SELF_PLANS, info, q, kv, kv_peer, *masks, [], [], lambda get, att: None, deps)


def between(info, x, att, w_out, c_query, src, c_key, c_value, deps):
    T, D = x.shape

    def body(info_ref, get, kv, y_ref, low_ref, inv_ref, cq_ref):
        xv = get(0)[...]
        kv[:, :D] = nn(xv, get(1)[...]).astype(BF)
        kv[:, D:] = nn(xv, get(2)[...]).astype(BF)
        y, inv = norm_parts(get(5)[...].astype(F32) + nn(get(3)[...], get(4)[...]))
        low = y.astype(BF)
        y_ref[...] = y
        low_ref[...] = low
        inv_ref[...] = jnp.broadcast_to(inv, inv_ref.shape)
        cq_ref[...] = (nn(low, get(6)[...]) * (0.125 * LOG2E)).astype(BF)

    outs = [shape(T, 2 * D, BF), shape(T, D, F32), shape(T, D, BF), shape(T, 128, F32), shape(T, D, BF)]
    return fused("between", info, body, [src, c_key, c_value, att, w_out, x, c_query], outs, deps=deps)


def attend_cross(info, q, kv, kv_peer, masks, y1, c_out, down, up, scale):
    T, D = q.shape
    A = down.shape[1]

    def finish(get, att, low_ref, inv_ref, sq_ref, gn_ref, base_ref):
        y, inv = norm_parts(get(1)[...] + nn(att[...], get(0)[...]))
        inv_ref[...] = jnp.broadcast_to(inv, inv_ref.shape)
        low = y.astype(BF)
        low_ref[...] = low
        h, g = gelu_pair(nn(low, get(2)[...]))
        hb = h.astype(BF)
        sq_ref[...] = hb
        gn_ref[...] = g.astype(BF)
        base_ref[...] = y + get(4)[0:1, 0:1] * nn(hb, get(3)[...])

    outs = [shape(T, D, BF), shape(T, 128, F32), shape(T, A, BF), shape(T, A, BF), shape(T, D, F32)]
    return attend(CROSS_PLANS, info, q, kv, kv_peer, *masks, [c_out, y1, down, up, scale], outs, finish)


def feed_forward(info, x, first, second, c, base, sq, gn, up, g_out, scale, block=1024):
    T, D = x.shape
    width = first.shape[1]
    F = 2 * width
    per = width // block
    A = sq.shape[1]
    held = Loads([first, second, base, g_out, scale, sq, up, gn])

    def kernel(info_ref, x_ref, c_ref, *refs):
        ins = refs[: len(held.arrays)]
        gp_ref, out0, out1, g3_ref, kept_ref, sent_ref, gnar_ref, acc, *scratch = refs[len(held.arrays) :]
        i = pl.program_id(0)
        bound = held.bind(info_ref, ins, scratch)
        pl.when(i == 0)(lambda: start_all(bound))
        cols = pl.ds(pl.multiple_of(lax.rem(i, per) * block, 128), block)
        for v in range(2):
            copies, buf = bound[v]

            @pl.when(i == v * per)
            def _():
                for copy in copies:
                    copy.wait()

            @pl.when(i // per == v)
            def _():
                h, g = gelu_pair(nn(x_ref[...], buf[:, cols]))
                gp_ref[...] = g.astype(BF)
                part = nn(h.astype(BF), c_ref[...])

                @pl.when(i == 0)
                def _():
                    acc[...] = part

                @pl.when(i > 0)
                def _():
                    acc[...] += part

        @pl.when(i == F // block - 1)
        def _():
            get = getter(bound)
            y, inv = norm_parts(acc[...] + get(2)[...])
            g3 = norm_back(y, inv, get(3)[...].astype(F32))
            g3_ref[...] = g3
            acc[...] = y
            put_slots(info_ref, acc, out0, out1)
            ga = (get(4)[0:1, 0:1] * g3).astype(BF)
            gup = tn(get(5)[...], ga).astype(BF)
            gnar = (get(7)[...].astype(F32) * nt(ga, get(6)[...])).astype(BF)
            gnar_ref[...] = gnar
            gdown = tn(gnar, x_ref[...]).astype(BF)
            for side, keep, send in ((0, gup, gdown), (1, gdown, gup)):
                @pl.when(info_ref[3] == side)
                def _():
                    kept_ref[...] = keep
                    sent_ref[...] = send

    outs = [shape(T // 2, D, BF)] * 2 + [shape(T, D, F32), shape(A, D, BF), shape(A, D, BF), shape(T, A, BF)]
    return pl.pallas_call(
        kernel,
        grid_spec=pltpu.PrefetchScalarGridSpec(
            num_scalar_prefetch=1,
            grid=(F // block,),
            in_specs=[pl.BlockSpec((T, D), lambda i, *_: (0, 0)), pl.BlockSpec((block, D), lambda i, *_: (i, 0))]
            + held.specs,
            out_specs=[pl.BlockSpec((T, block), lambda i, *_: (0, i))]
            + [pl.BlockSpec(o.shape, lambda i, *_: (0, 0)) for o in outs],
            scratch_shapes=[pltpu.VMEM((T, D), F32)] + held.scratch,
        ),
        out_shape=[shape(T, F, BF)] + outs,
        compiler_params=params(),
        cost_estimate=cost(26),
        name="feed_forward",
    )(info, x, c, *held.arrays)


def ffn_back(info, g3, c, first, second, gp, gnar, down, low, inv, c_out, deps, block=1024):
    T, D = g3.shape
    F = c.shape[0]
    width = first.shape[1]
    per = width // block
    held = Loads([first, second, gnar, down, c_out, low, inv])

    def kernel(info_ref, g3_ref, c_ref, gp_ref, *refs):
        ins = refs[: len(held.arrays)]
        g2_ref, ga_ref, acc, *scratch = refs[len(held.arrays) + len(deps) :]
        i = pl.program_id(0)
        bound = held.bind(info_ref, ins, scratch)
        pl.when(i == 0)(lambda: start_all(bound))
        gh = (nt(g3_ref[...].astype(BF), c_ref[...]) * gp_ref[...].astype(F32)).astype(BF)

        @pl.when(i == 0)
        def _():
            acc[...] = g3_ref[...]

        for v in range(2):
            copies, e = bound[v]

            @pl.when(i == v * per)
            def _():
                for copy in copies:
                    copy.wait()

            @pl.when(i // per == v)
            def _():
                acc[...] += nt(gh, e[:, pl.ds(pl.multiple_of(lax.rem(i, per) * block, 128), block)])

        @pl.when(i == F // block - 1)
        def _():
            get = getter(bound)
            g2 = norm_back(get(5)[...].astype(F32), get(6)[:, 0:1], acc[...] + nt(get(2)[...], get(3)[...]))
            g2_ref[...] = g2
            ga_ref[...] = nt(g2.astype(BF), get(4)[...]).astype(BF)

    outs = [shape(T, D, F32), shape(T, D, BF)]
    return pl.pallas_call(
        kernel,
        grid_spec=pltpu.PrefetchScalarGridSpec(
            num_scalar_prefetch=1,
            grid=(F // block,),
            in_specs=[pl.BlockSpec((T, D), lambda i, *_: (0, 0)), pl.BlockSpec((block, D), lambda i, *_: (i, 0)),
                      pl.BlockSpec((T, block), lambda i, *_: (0, i))] + held.specs + [ANYWHERE] * len(deps),
            out_specs=[pl.BlockSpec(o.shape, lambda i, *_: (0, 0)) for o in outs],
            scratch_shapes=[pltpu.VMEM((T, D), F32)] + held.scratch,
        ),
        out_shape=outs,
        compiler_params=params(),
        cost_estimate=cost(18),
        name="ffn_back",
    )(info, g3, c, gp, *held.arrays, *deps)


def attend_cross_back(info, q, kv, kv_peer, do, o, r, p, g2, y1, inv1, c_query, w_out, deps):
    T, D = q.shape

    def finish(get, gq, g1_ref, ga_ref):
        g = get(1)[...] + 0.125 * nt(gq[...], get(0)[...])
        g1 = norm_back(get(2)[...].astype(F32), get(3)[:, 0:1], g)
        g1_ref[...] = g1
        ga_ref[...] = nt(g1.astype(BF), get(4)[...]).astype(BF)

    return attend_back(CROSS_PLANS, info, q, kv, kv_peer, do, o, r, p, [c_query, g2, y1, inv1, w_out],
                       [shape(T, D, F32), shape(T, D, BF)], finish, deps)


def attend_self_back(info, q, kv, kv_peer, do, o, r, p, g1, w_query, deps):
    T, D = q.shape

    def finish(get, gq, acc_ref):
        acc_ref[...] = get(1)[...] + 0.125 * nt(gq[...], get(0)[...])

    return attend_back(SELF_PLANS, info, q, kv, kv_peer, do, o, r, p, [w_query, g1], [shape(T, D, F32)], finish, deps)


def add_pairs(mine, got, part):
    D = mine.shape[1] // 2
    out = []
    for h in range(D // 128):
        at = slice(256 * h + 128 * part, 256 * h + 128 * part + 128)
        out.append((mine[:, at].astype(F32) + got[:, at].astype(F32)).astype(BF))
    return jnp.concatenate(out, axis=1)


def source_grad(info, gkv, got, w_key, w_value, deps):
    T, D = gkv.shape[0], gkv.shape[1] // 2

    def body(info_ref, get, out0, out1, total):
        mine, other = get(0), get(1)
        acc = nt(add_pairs(mine, other, 0), get(2)[...])
        total[...] = acc + nt(add_pairs(mine, other, 1), get(3)[...])
        put_slots(info_ref, total, out0, out1)

    return fused("source_grad", info, body, [gkv, got, w_key, w_value], [shape(T // 2, D, BF)] * 2, deps=deps,
                 extra=[pltpu.VMEM((T, D), F32)])


def token_grad(info, acc, gkv, got, w_key, w_value, deps):
    T, D = acc.shape

    def body(info_ref, get, out0, out1):
        mine, other = get(0), get(1)
        total = nt(add_pairs(mine, other, 0), get(2)[...])
        total += nt(add_pairs(mine, other, 1), get(3)[...])
        g = get(4)
        g[...] += total
        put_slots(info_ref, g, out0, out1)

    return fused("token_grad", info, body, [gkv, got, w_key, w_value, acc], [shape(T // 2, D, BF)] * 2, deps=deps)


def move(value, target):
    dp, seq = lax.axis_size("dp"), lax.axis_size("seq")
    pairs = []
    for d in range(dp):
        for s in range(seq):
            a, b = target(d, s)
            pairs.append((d * seq + s, a * seq + b))
    return lax.ppermute(value, ("dp", "seq"), pairs)


def flip(value, bit):
    return move(value, lambda d, s: (d ^ bit, s))


def core_of(chunk):
    return (0, 1, 1, 0)[chunk]


def pick(flag, first, second):
    return jnp.where(flag, first, second)


def send_pieces(pieces):
    return [
        move(piece, lambda a, q, k=k: (2 * (a // 2) + core_of(q), 2 * (a % 2) + (q + k) % 2))
        for k, piece in enumerate(pieces)
    ]


def take_pieces(value, s):
    return [lax.dynamic_index_in_dim(value, (s + k) % 2, 0, keepdims=False) for k in range(2)]


def send_back(pieces):
    dp, seq = lax.axis_size("dp"), lax.axis_size("seq")
    got = []
    for k, piece in enumerate(pieces):
        back = {}
        for a in range(dp):
            for q in range(seq):
                back[(2 * (a // 2) + core_of(q), 2 * (a % 2) + (q + k) % 2)] = (a, q)
        got.append(move(piece, lambda a, b: back[(a, b)]))
    return got


def join_rows(got, s):
    even = s % 2 == 0
    return jnp.stack([pick(even, got[0], got[1]), pick(even, got[1], got[0])])


def first_hop(pair, low):
    return [flip(pair[0], 2 * low), flip(pair[1], 4 * low)]


def second_hop(near, low):
    return [flip(near[0], 4 * low), flip(near[1], 2 * low)]


def all_parts(near, far, low):
    out = []
    for v in range(2):
        half = near[v].shape[0] // 2
        b1, b2 = ((2, 4), (4, 2))[v]
        arrays = [near[v], far[v], flip(near[v], low), flip(far[v], low)]
        parts = {}
        for a, m in zip(arrays, (0, b2, 1, b2 ^ 1)):
            parts[m] = (a, 0)
            parts[m ^ b1] = (a, half)
        out.append([parts[m] for m in range(8)])
    return out


class Reduce:
    def __init__(self, kept, sent, d, s, low):
        self.d, self.s, self.low = d, s, low
        self.kept, self.got = kept, [flip(sent, low)]

    def plane(self, v, m):
        return flip(v, 2 * self.low * m)

    def scatter_plane(self):
        me = self.d // (2 * self.low)
        parts = self.value.reshape(4, -1, self.value.shape[1])
        take = [lax.dynamic_index_in_dim(parts, me ^ m, 0, keepdims=False) for m in range(4)]
        self.kept, self.got = take[0], [self.plane(take[m], m) for m in range(1, 4)]

    def line(self, bit):
        self.kept, self.got = self.value, [move(self.value, lambda a, b: (a, b ^ bit))]

    def add(self):
        total = self.kept.astype(F32)
        for got in self.got:
            total += got.astype(F32)
        self.value = total.astype(BF)

    def low_bits(self):
        bit = 1
        while bit < self.low:
            got = flip(self.value, bit)
            self.value = (self.value.astype(F32) + got.astype(F32)).astype(BF)
            bit *= 2

    def gather_plane(self):
        self.me = self.d // (2 * self.low)
        self.got = [self.value] + [self.plane(self.value, m) for m in range(1, 4)]

    def put(self):
        got = self.got
        n, rows = len(got), []
        for j in range(n):
            part = got[n - 1]
            for m in range(n - 1):
                part = pick((self.me ^ j) == m, got[m], part)
            rows.append(part)
        self.value = jnp.concatenate(rows, axis=0)


def local(tokens, source, target_lengths, source_lengths, step_index, self_query, self_key, self_value,
          self_out, cross_query, cross_key, cross_value, cross_out, ffn_expand, ffn_contract, adapter_down,
          adapter_up, grad_output):
    rows, C, D = tokens.shape
    dp, seq = lax.axis_size("dp"), lax.axis_size("seq")
    assert rows == 2 and seq == 4 and dp % 8 == 0
    low = dp // 8
    d, s = lax.axis_index("dp"), lax.axis_index("seq")
    core = d % 2
    info = jnp.stack([core, d // low, (s + d) % 2, (d // low) % 2]).astype(jnp.int32)

    def widen(shard):
        if low == 1:
            return shard
        groups = [[g * low + i for i in range(low)] for g in range(8)]
        return lax.all_gather(shard, "dp", axis=0, tiled=True, axis_index_groups=groups)

    def rows_of(*weights):
        return jnp.concatenate(weights, axis=0)

    t = send_pieces(take_pieces(tokens, s))
    sq, sk, sv, ex = [widen(w) for w in (self_query, self_key, self_value, ffn_expand)]
    n = sq.shape[0]
    h = n // 2
    pair = [rows_of(sk, sv[:h]), rows_of(sq, sv[h:])]
    rest = join_up([self_out, cross_key, cross_value, cross_query, cross_out], ())
    near = beside(pair, first_hop(pair, low), (t[0],))
    e1, e2, c_shard = stage(ex, ffn_contract, near)
    rest = lax.all_gather(rest, "dp", axis=0, tiled=True)
    each = self_out.shape[0]
    w_out, c_key, c_value, c_query, c_out = [Shards(rest, dp, j * each, each) for j in range(5)]

    mine = jnp.concatenate([target_lengths, source_lengths[:, None]], axis=1)
    other = flip(mine, 1)
    table = jnp.concatenate([pick(core == 0, mine, other), pick(core == 0, other, mine)], axis=0)
    row = lax.dynamic_index_in_dim(table, s, 0, keepdims=False)
    lens, src_len = row[:-1], row[-1]
    docs = lens.shape[0]
    ends = jnp.cumsum(lens)[:-1]
    i = jnp.arange(2 * C, dtype=jnp.int32)
    slot = i // C

    def place(which):
        chunk = pick(which == 0, slot * 3, slot + 1)
        return chunk * C + i % C

    lanes = jnp.arange(128, dtype=jnp.int32) % 64

    def doc_hot(pos):
        doc = jnp.sum((pos[:, None] >= ends[None, :]).astype(jnp.int32), axis=-1)
        return doc[:, None] == lanes[None, :]

    own_pos, peer_pos = place(core), place(1 - core)
    k_aug = [doc_hot(own_pos).astype(BF), doc_hot(peer_pos).astype(BF)]
    q_aug = jnp.where(doc_hot(own_pos) | (lanes >= docs)[None, :], 0.0, NEG).astype(BF)
    ck_aug = [((pos[:, None] >= src_len) & (lanes == 0)[None, :]).astype(BF) for pos in (own_pos, peer_pos)]
    cq_aug = jnp.broadcast_to(jnp.where(lanes == 0, NEG, 0.0).astype(BF)[None, :], (2 * C, 128))

    scale = jnp.full((8, 128), (step_index[0] + 1).astype(F32) / 5.0, F32)
    src = send_pieces(gate(take_pieces(source, s), t))
    far = gate(
        second_hop(near, low), (*src, info, q_aug, *k_aug, cq_aug, *ck_aug, scale, e1, e2)
    )
    a1, b1 = all_parts(near, far, low)
    w_key, w_query = Pieces(n, (a1, 0, n, 0)), Pieces(n, (b1, 0, n, 0))
    w_value = Pieces(n, (a1, n, h, 0), (b1, n, h, h))
    x = Slots(t, 0, C)
    q, kv = project_qkv(info, x, w_query, w_key, w_value, ())
    q, kv, e1, e2 = barrier(q, kv, e1, e2)
    kv_peer = flip(kv, 1)
    first3, second3 = first_hop([e1, e2], low), second_hop([e1, e2], low)
    attended, p_self, r_self = attend_self(info, q, kv, kv_peer, (q_aug, *k_aug), ())
    *first3, attended, c_shard = barrier(*first3, attended, c_shard)
    w_contract = lax.all_gather(c_shard, "dp", axis=0, tiled=True)
    far3 = second_hop(first3, low)
    flips = [flip(v, low) for v in (e1, e2, *first3)]
    skv, y1, y1_low, inv1, cq = between(info, x, attended, w_out, c_query, Slots(src, 0, C), c_key, c_value, ())
    *flips, skv, cq, h0, h1, g0, g1 = barrier(*flips, skv, cq, *second3, *take_pieces(grad_output, s))
    second3, pieces = [h0, h1], [g0, g1]
    g_out = send_pieces(pieces)
    skv_peer = flip(skv, 1)
    cross_attended, p_cross, r_cross, second_low, inv2, squeezed, gn, base = attend_cross(
        info, cq, skv, skv_peer, (cq_aug, *ck_aug), y1, c_out, adapter_down, adapter_up, scale
    )
    f0, f1, h0, h1, g0, g1, second_low = barrier(*far3, *second3, *g_out, second_low)
    far3, second3, g_out = [f0, f1], [h0, h1], [g0, g1]
    a3, b3 = [
        [(v, 0) for _, v in sorted(
            {0: own, 1: flips[i], b1: first3[i], b1 ^ 1: flips[2 + i], b2: second3[i], b2 ^ 1: flip(second3[i], low),
             6: far3[i], 7: flip(far3[i], low)}.items()
        )]
        for i, (own, b1, b2) in enumerate(((e1, 2, 4), (e2, 4, 2)))
    ]
    ea, eb = Pieces(n, (a3, 0, n, 0)), Pieces(n, (b3, 0, n, 0))
    gp, o0, o1, g3, kept, sent, gnar = feed_forward(
        info, second_low, ea, eb, w_contract, base, squeezed, gn, adapter_up, Slots(g_out, 0, C), scale
    )
    output = send_back([o0, o1])
    total = Reduce(kept, sent, d, s, low)
    g2, grad_cross = ffn_back(info, g3, w_contract, ea, eb, gp, gnar, adapter_down, second_low, inv2, c_out, ())
    *total.got, g2, grad_cross = barrier(*total.got, g2, grad_cross)
    total.add()
    total.scatter_plane()
    gkv, gkv_peer, g1, grad_self = attend_cross_back(
        info, cq, skv, skv_peer, grad_cross, cross_attended, r_cross, p_cross, g2, y1_low, inv1, c_query, w_out, (total.kept,)
    )
    *total.got, o0, o1, grad_self, gkv_peer = barrier(*total.got, *output, grad_self, gkv_peer)
    output = [o0, o1]
    total.add()
    total.line(2)
    got = flip(gkv_peer, 1)
    pieces = source_grad(info, gkv, got, c_key, c_value, (grad_self, total.kept))
    pieces = send_back(pieces)
    gkv, gkv_peer, acc = attend_self_back(
        info, q, kv, kv_peer, grad_self, attended, r_self, p_self, g1, w_query, pieces[:0]
    )
    *total.got, s0, s1, gkv_peer = barrier(*total.got, *pieces, gkv_peer)
    got = flip(gkv_peer, 1)
    total.add()
    total.line(1)
    pieces = token_grad(info, acc, gkv, got, w_key, w_value, (total.kept,))
    *total.got, o0, o1, s0, s1, t0, t1 = barrier(*total.got, *output, s0, s1, *pieces)
    tokens_back = send_back([t0, t1])
    output = [o0, o1]
    total.add()
    total.low_bits()
    total.gather_plane()
    total.put()
    grads, other = total.value, flip(total.value, low)
    high = (d // low) % 2 == 1
    grad_up = pick(high, other, grads).astype(F32)
    grad_down = pick(high, grads, other).astype(F32).T
    output, grad_source, grad_tokens = [join_rows(v, s) for v in (output, [s0, s1], tokens_back)]
    return (output, grad_tokens, grad_source, grad_down, grad_up)


def solution(mesh):
    rows = P("dp", "seq", None)
    weight = P("dp", None)
    return jax.shard_map(
        local,
        mesh=mesh,
        in_specs=(rows, rows, weight, P("dp"), P()) + (weight,) * 10 + (P(), P(), rows),
        out_specs=(rows, rows, rows, P(), P()),
        check_vma=False,
    )
```

```python
import functools

import jax
import jax.numpy as jnp
from jax import lax
from jax.experimental import pallas as pl
from jax.experimental.pallas import tpu as pltpu
from jax.sharding import PartitionSpec as P

BF, F32 = jnp.bfloat16, jnp.float32
NEG = -1e30
LOG2E = 1.4426950408889634
PER = 2

SELF_PLANS = (
    (((0, True),), ((0, False), (2, False), (3, False), (1, True))),
    (((2, False), (0, True)), ((2, False), (0, False), (1, True))),
)
CROSS_PLANS = ((((0, False), (1, False), (2, False), (3, False)),) * 2,)


def nt(a, b):
    return lax.dot_general(a, b, (((1,), (1,)), ((), ())), preferred_element_type=F32)


def nn(a, b):
    return lax.dot_general(a, b, (((1,), (0,)), ((), ())), preferred_element_type=F32)


def tn(a, b):
    return lax.dot_general(a, b, (((0,), (0,)), ((), ())), preferred_element_type=F32)


def cost(us):
    return pl.CostEstimate(flops=int(us * 3e8), bytes_accessed=1024, transcendentals=0)


def params():
    return pltpu.CompilerParams(vmem_limit_bytes=64 * 1024 * 1024)


def shape(rows, cols, dtype):
    return jax.ShapeDtypeStruct((rows, cols), dtype)


class Whole:
    def __init__(self, array):
        self.arrays, self.shape, self.dtype, self.count = [array], array.shape, array.dtype, 1

    def copies(self, info, refs, buf, sem, first):
        return [pltpu.make_async_copy(refs[0], buf, sem.at[first])]


class Pieces:
    def __init__(self, stride, *pieces):
        self.stride, self.pieces = stride, pieces
        self.arrays = [a for parts, *_ in pieces for a, _ in parts]
        self.shape, self.dtype = (8 * stride, self.arrays[0].shape[1]), self.arrays[0].dtype
        self.count = len(self.arrays)

    def copies(self, info, refs, buf, sem, first):
        out = []
        for parts, at, rows, base in self.pieces:
            for m, (_, start) in enumerate(parts):
                to = pl.multiple_of((info[1] ^ m) * self.stride + base, 16)
                i = len(out)
                out.append(
                    pltpu.make_async_copy(
                        refs[i].at[pl.ds(start + at, rows)], buf.at[pl.ds(to, rows)], sem.at[first + i]
                    )
                )
        return out


class Shards:
    def __init__(self, array, owners, at, rows):
        self.arrays, self.count, self.at, self.rows = [array], owners, at, rows
        self.each = array.shape[0] // owners
        self.shape, self.dtype = (owners * rows, array.shape[1]), array.dtype

    def copies(self, info, refs, buf, sem, first):
        return [
            pltpu.make_async_copy(
                refs[0].at[pl.ds(j * self.each + self.at, self.rows)],
                buf.at[pl.ds(j * self.rows, self.rows)],
                sem.at[first + j],
            )
            for j in range(self.count)
        ]


class Slots:
    def __init__(self, arrays, at, rows):
        self.arrays, self.at, self.rows, self.count = list(arrays), at, rows, 2
        self.shape, self.dtype = (2 * rows, arrays[0].shape[1]), arrays[0].dtype

    def copies(self, info, refs, buf, sem, first):
        return [
            pltpu.make_async_copy(
                refs[k].at[pl.ds(self.at, self.rows)],
                buf.at[pl.ds(pl.multiple_of((info[2] ^ k) * self.rows, 16), self.rows)],
                sem.at[first + k],
            )
            for k in range(2)
        ]


class Chunk:
    def __init__(self, array, k):
        self.arrays, self.k, self.count = [array], k, 1
        self.shape, self.dtype = (array.shape[0] // 2, array.shape[1]), array.dtype

    def copies(self, info, refs, buf, sem, first):
        rows = self.shape[0]
        at = pl.multiple_of((info[2] ^ self.k) * rows, 16)
        return [pltpu.make_async_copy(refs[0].at[pl.ds(at, rows)], buf, sem.at[first])]


class Loads:
    def __init__(self, loads):
        self.loads = [v if hasattr(v, "copies") else Whole(v) for v in loads]
        self.arrays = [a for v in self.loads for a in v.arrays]
        self.specs = [pl.BlockSpec(memory_space=pl.ANY)] * len(self.arrays)
        self.scratch = [pltpu.VMEM(v.shape, v.dtype) for v in self.loads]
        self.scratch.append(pltpu.SemaphoreType.DMA((sum(v.count for v in self.loads),)))

    def bind(self, info, refs, scratch):
        bufs, sem = scratch[:-1], scratch[-1]
        at = first = 0
        out = []
        for v, buf in zip(self.loads, bufs):
            out.append((v.copies(info, refs[at : at + len(v.arrays)], buf, sem, first), buf))
            at += len(v.arrays)
            first += v.count
        return out


def start_all(bound):
    for copies, _ in bound:
        for c in copies:
            c.start()


def getter(bound):
    ready = set()

    def get(i):
        copies, buf = bound[i]
        if i not in ready:
            for c in copies:
                c.wait()
            ready.add(i)
        return buf

    return get


ANYWHERE = pl.BlockSpec(memory_space=pl.ANY)


def half_mask(shape, h):
    lane = lax.broadcasted_iota(jnp.int32, shape, 1)
    return (lane < 64) if h == 0 else (lane >= 64)


def top(parts):
    rows = 64
    pieces = [p[i : i + rows] for p in parts for i in range(0, p.shape[0], rows)]
    while len(pieces) > 1:
        pieces = [jnp.maximum(*pieces[i : i + 2]) if i + 1 < len(pieces) else pieces[i] for i in range(0, len(pieces), 2)]
    return jnp.max(pieces[0], axis=0, keepdims=True)


def forward_pair(plan, C, q, ks, vs, qa, kas, put, p_ref):
    kaug = [[jnp.where(half_mask(k.shape, h), k, a) for k, a in zip(ks, kas)] for h in range(2)]
    vts = [v.T for v in vs]
    ones = jnp.ones((16, C), BF)
    units, n = [], 0
    for slot, blocks in enumerate(plan):
        units += [(slot, h, n, blocks) for h in range(2)]
        n += len(blocks)

    def scores_of(unit):
        slot, h, _, blocks = unit
        rows = slice(slot * C, (slot + 1) * C)
        qh = jnp.where(half_mask((C, 128), h), q[rows], qa[rows])
        scores = []
        for kb, diagonal in blocks:
            s = nt(kaug[h][kb], qh)
            if diagonal:
                ki = lax.broadcasted_iota(jnp.int32, s.shape, 0)
                qi = lax.broadcasted_iota(jnp.int32, s.shape, 1)
                s = jnp.where(ki <= qi, s, NEG)
            scores.append(s)
        return scores, top(scores)

    def rest(unit, scores, m):
        _, h, n, blocks = unit
        ps = [jnp.exp2(s - m).astype(BF) for s in scores]
        for i, p in enumerate(ps):
            p_ref[h, n + i] = p
        values = [jnp.concatenate([vts[kb][64 * h : 64 * h + 64], ones], axis=0) for kb, _ in blocks]
        both = nn(jnp.concatenate(values, axis=1), jnp.concatenate(ps, axis=0))
        inv = 1.0 / both[64:65]
        return both[:64] * inv, jnp.broadcast_to(inv, (64, C))

    done = []
    AHEAD = 2
    pending = [scores_of(u) for u in units[:AHEAD]]
    for i, unit in enumerate(units):
        if i + AHEAD < len(units):
            pending.append(scores_of(units[i + AHEAD]))
        done.append(rest(unit, *pending[i]))
        if i % 2:
            halves, inverses = zip(*done[-2:])
            put(unit[0], jnp.concatenate(halves, axis=0).T.astype(BF), jnp.concatenate(inverses, axis=0).T)


def by_plan(plans, info, run):
    if len(plans) == 1:
        run(plans[0])
    else:
        for v, plan in enumerate(plans):
            pl.when(info[0] == v)(functools.partial(run, plan))


def attend(plans, info, q, own, peer, qa, kao, kap, loads, outs, finish, deps=()):
    T, D = q.shape
    C, pairs = T // 2, D // 128
    steps = pairs // PER
    nb = sum(len(b) for b in plans[0])
    held = Loads(loads)

    def kernel(info_ref, q_ref, ko, vo, kp, vp, qa_ref, kao_ref, kap_ref, *refs):
        ins = refs[: len(held.arrays)]
        o_ref, p_ref, r_ref, *out_refs = refs[len(held.arrays) + len(deps) :][: 3 + len(outs)]
        att, *scratch = refs[len(held.arrays) + len(deps) + 3 + len(outs) :]
        step = pl.program_id(0)
        bound = held.bind(info_ref, ins, scratch)
        pl.when(step == 0)(lambda: start_all(bound))

        def run(plan):
            for j in range(PER):
                at = slice(128 * j, 128 * j + 128)
                cols = pl.ds(pl.multiple_of((step * PER + j) * 128, 128), 128)

                def put(slot, value, inverse):
                    o_ref[slot * C : (slot + 1) * C, at] = value
                    r_ref[slot * C : (slot + 1) * C, at] = inverse
                    att[slot * C : (slot + 1) * C, cols] = value

                def chunks(*rs):
                    return [r[i * C : (i + 1) * C, at] for r in rs for i in range(2)]

                masks = [m[i * C : (i + 1) * C] for m in (kao_ref, kap_ref) for i in range(2)]
                forward_pair(plan, C, q_ref[:, at], chunks(ko, kp), chunks(vo, vp), qa_ref[...], masks, put, p_ref.at[j])

        by_plan(plans, info_ref, run)

        @pl.when(step == steps - 1)
        def _():
            finish(getter(bound), att, *out_refs)

    col = pl.BlockSpec((T, 128 * PER), lambda h, *_: (0, h))
    val = pl.BlockSpec((T, 128 * PER), lambda h, *_: (0, steps + h))
    fix = pl.BlockSpec((T, 128), lambda h, *_: (0, 0))
    return pl.pallas_call(
        kernel,
        grid_spec=pltpu.PrefetchScalarGridSpec(
            num_scalar_prefetch=1,
            grid=(steps,),
            in_specs=[col] + [col, val] * 2 + [fix] * 3 + held.specs + [ANYWHERE] * len(deps),
            out_specs=[col, pl.BlockSpec((PER, 2, nb, C, C), lambda h, *_: (h, 0, 0, 0, 0)), col]
            + [pl.BlockSpec(o.shape, lambda h, *_: (0, 0)) for o in outs],
            scratch_shapes=[pltpu.VMEM((T, D), BF)] + held.scratch,
        ),
        out_shape=[shape(T, D, BF), jax.ShapeDtypeStruct((pairs, 2, nb, C, C), BF), shape(T, D, F32)] + list(outs),
        compiler_params=params(),
        cost_estimate=cost(25),
        name="attend",
    )(info, q, own, own, peer, peer, qa, kao, kap, *held.arrays, *deps)


def backward_pair(plan, C, q, ks, vs, do, o, r, p_ref, put, gown, gpeer):
    lane = lax.broadcasted_iota(jnp.int32, (C, 128), 1)
    l64 = lax.rem(lane, 64)
    ones = jnp.where(l64 < 2, 1.0, 0.0).astype(BF)
    vaug = [[jnp.where(half_mask(v.shape, h), v, ones) for v in vs] for h in range(2)]
    kts = [k.T for k in ks]
    by_key = [[] for _ in range(4)]
    zero = jnp.zeros((C, 128), BF)
    units, n = [], 0
    for slot, blocks in enumerate(plan):
        units += [(slot, h, n, blocks) for h in range(2)]
        n += len(blocks)

    def probs_back(unit):
        slot, h, n, blocks = unit
        rows = slice(slot * C, (slot + 1) * C)
        scaled = do[rows].astype(F32) * r[rows]
        dos = scaled.astype(BF)
        hm = lane < 64 if h == 0 else lane >= 64
        d = -jnp.sum(jnp.where(hm, scaled * o[rows].astype(F32), 0.0), axis=1, keepdims=True)
        hi = d.astype(BF)
        lo = (d - hi.astype(F32)).astype(BF)
        tail = jnp.where(l64 == 0, jnp.broadcast_to(hi, (C, 128)), jnp.where(l64 == 1, jnp.broadcast_to(lo, (C, 128)), zero))
        doa = jnp.where(hm, dos, tail)
        return [nt(vaug[h][kb], doa) for kb, _ in blocks], jnp.where(hm, dos, zero), jnp.where(hm, q[rows], zero)

    def rest(unit, dps, dom, qm):
        slot, h, n, blocks = unit
        grads = []
        for i, ((kb, _), dp) in enumerate(zip(blocks, dps)):
            pb = p_ref[h, n + i]
            ds = (pb.astype(F32) * dp).astype(BF)
            grads.append(ds)
            by_key[kb].append((pb, ds, dom, qm))
        wide = jnp.concatenate([kts[kb][64 * h : 64 * h + 64] for kb, _ in blocks], axis=1)
        return nn(wide, jnp.concatenate(grads, axis=0))

    done = []
    BACK = 2
    pending = [probs_back(u) for u in units[:BACK]]
    for i, unit in enumerate(units):
        if i + BACK < len(units):
            pending.append(probs_back(units[i + BACK]))
        done.append(rest(unit, *pending[i]))
        if i % 2:
            put(unit[0], jnp.concatenate(done[-2:], axis=0).T.astype(BF))
    for kb in range(4):
        ref = gown if kb < 2 else gpeer
        rows = slice((kb % 2) * C, (kb % 2) * C + C)
        if by_key[kb]:
            pbs, dss, doms, qms = zip(*by_key[kb])
            gk = nn(jnp.concatenate(dss, axis=1), jnp.concatenate(qms, axis=0))
            gv = nn(jnp.concatenate(pbs, axis=1), jnp.concatenate(doms, axis=0))
        else:
            gk = gv = jnp.zeros((C, 128), F32)
        ref[rows, 0:128] = (gk * (1.0 / LOG2E)).astype(BF)
        ref[rows, 128:256] = gv.astype(BF)


def attend_back(plans, info, q, own, peer, do, o, r, p, loads, outs, finish, deps=()):
    T, D = q.shape
    C, pairs, nb = T // 2, D // 128, p.shape[2]
    steps = pairs // PER
    held = Loads(loads)

    def kernel(info_ref, q_ref, ko, vo, kp, vp, do_ref, o_ref, r_ref, p_ref, *refs):
        ins = refs[: len(held.arrays)]
        gown, gpeer, *out_refs = refs[len(held.arrays) + len(deps) :][: 2 + len(outs)]
        gq, *scratch = refs[len(held.arrays) + len(deps) + 2 + len(outs) :]
        step = pl.program_id(0)
        bound = held.bind(info_ref, ins, scratch)
        pl.when(step == 0)(lambda: start_all(bound))

        def run(plan):
            for j in range(PER):
                at = slice(128 * j, 128 * j + 128)
                wide = slice(256 * j, 256 * j + 256)
                cols = pl.ds(pl.multiple_of((step * PER + j) * 128, 128), 128)

                def put(slot, value):
                    gq[slot * C : (slot + 1) * C, cols] = value

                def chunks(*rs):
                    return [r[i * C : (i + 1) * C, at] for r in rs for i in range(2)]

                backward_pair(plan, C, q_ref[:, at], chunks(ko, kp), chunks(vo, vp), do_ref[:, at], o_ref[:, at],
                              r_ref[:, at], p_ref.at[j], put, gown.at[:, wide], gpeer.at[:, wide])

        by_plan(plans, info_ref, run)

        @pl.when(step == steps - 1)
        def _():
            finish(getter(bound), gq, *out_refs)

    col = pl.BlockSpec((T, 128 * PER), lambda h, *_: (0, h))
    val = pl.BlockSpec((T, 128 * PER), lambda h, *_: (0, steps + h))
    wide = pl.BlockSpec((T, 256 * PER), lambda h, *_: (0, h))
    return pl.pallas_call(
        kernel,
        grid_spec=pltpu.PrefetchScalarGridSpec(
            num_scalar_prefetch=1,
            grid=(steps,),
            in_specs=[col] + [col, val] * 2 + [col] * 3
            + [pl.BlockSpec((PER, 2, nb, C, C), lambda h, *_: (h, 0, 0, 0, 0))] + held.specs + [ANYWHERE] * len(deps),
            out_specs=[wide] * 2 + [pl.BlockSpec(v.shape, lambda h, *_: (0, 0)) for v in outs],
            scratch_shapes=[pltpu.VMEM((T, D), BF)] + held.scratch,
        ),
        out_shape=[shape(T, 2 * D, BF)] * 2 + list(outs),
        compiler_params=params(),
        cost_estimate=cost(25),
        name="attend_back",
    )(info, q, own, own, peer, peer, do, o, r, p, *held.arrays, *deps)


def gate(values, deps):
    def kernel(*refs):
        del refs

    n = len(values)
    return pl.pallas_call(
        kernel,
        in_specs=[ANYWHERE] * (n + len(deps)),
        out_specs=[ANYWHERE] * n,
        out_shape=[jax.ShapeDtypeStruct(v.shape, v.dtype) for v in values],
        input_output_aliases={i: i for i in range(n)},
        cost_estimate=cost(0.1),
        name="gate",
    )(*values, *deps)


def barrier(*values):
    return gate(values, ())


def beside(pair, got, deps=()):
    def kernel(a, b, c, d, *refs):
        ab, cd = refs[-2:]
        n, m = a.shape[0], c.shape[0]
        ab[:n] = a[...]
        ab[n:] = b[...]
        cd[:m] = c[...]
        cd[m:] = d[...]

    full = pl.BlockSpec(memory_space=pltpu.VMEM)
    return pl.pallas_call(
        kernel,
        in_specs=[full] * 4 + [ANYWHERE] * len(deps),
        out_specs=[full] * 2,
        out_shape=[shape(2 * v.shape[0], v.shape[1], BF) for v in pair],
        cost_estimate=cost(2),
        compiler_params=params(),
        name="beside",
    )(pair[0], got[0], pair[1], got[1], *deps)


def join_up(arrays, deps):
    rows = [a.shape[0] for a in arrays]

    def kernel(*refs):
        at = 0
        for r, n in zip(refs, rows):
            refs[-1][at : at + n] = r[...]
            at += n

    full = pl.BlockSpec(memory_space=pltpu.VMEM)
    return pl.pallas_call(
        kernel,
        in_specs=[full] * len(arrays) + [ANYWHERE] * len(deps),
        out_specs=full,
        out_shape=shape(sum(rows), arrays[0].shape[1], BF),
        cost_estimate=cost(2),
        compiler_params=params(),
        name="join_up",
    )(*arrays, *deps)


def stage(expand_shard, contract_shard, deps):
    rows, cols = expand_shard.shape
    half = cols // 2

    def kernel(e_ref, c_ref, *refs):
        e1, e2, c = refs[-3:]
        e1[...] = e_ref[:, :half]
        e2[...] = e_ref[:, half:]
        c[...] = c_ref[...]

    full = pl.BlockSpec(memory_space=pltpu.VMEM)
    return pl.pallas_call(
        kernel,
        in_specs=[full, full] + [ANYWHERE] * len(deps),
        out_specs=[full] * 3,
        out_shape=[shape(rows, half, BF)] * 2 + [shape(*contract_shard.shape, BF)],
        cost_estimate=cost(3),
        compiler_params=params(),
        name="stage",
    )(expand_shard, contract_shard, *deps)


def fused(name, info, body, loads, outs, deps=(), extra=()):
    held = Loads(loads)
    total, nout = len(held.arrays), len(outs)

    def kernel(info_ref, *refs):
        out_refs = refs[total + len(deps) :][:nout]
        scratch = refs[total + len(deps) + nout :]
        bound = held.bind(info_ref, refs[:total], scratch[len(extra) :])
        start_all(bound)
        body(info_ref, getter(bound), *out_refs, *scratch[: len(extra)])

    return pl.pallas_call(
        kernel,
        grid_spec=pltpu.PrefetchScalarGridSpec(
            num_scalar_prefetch=1,
            grid=(1,),
            in_specs=held.specs + [ANYWHERE] * len(deps),
            out_specs=[pl.BlockSpec(o.shape, lambda i, *_: (0, 0)) for o in outs],
            scratch_shapes=list(extra) + held.scratch,
        ),
        out_shape=list(outs),
        compiler_params=params(),
        cost_estimate=cost(6),
        name=name,
    )(info, *held.arrays, *deps)


def norm_parts(v):
    mean = jnp.mean(v, axis=-1, keepdims=True)
    c = v - mean
    inv = lax.rsqrt(jnp.mean(c * c, axis=-1, keepdims=True) + 1e-05)
    return c * inv, inv


def norm_back(y, inv, g):
    return inv * (g - jnp.mean(g, axis=-1, keepdims=True) - y * jnp.mean(g * y, axis=-1, keepdims=True))


def gelu_pair(v):
    phi = 0.5 + 0.5 * lax.erf(v * 0.7071067811865476)
    pdf = jnp.exp(v * v * -0.5) * 0.3989422804014327
    return v * phi, phi + v * pdf


def put_slots(info_ref, value, first, second):
    C = value.shape[0] // 2
    for k, ref in enumerate((first, second)):
        ref[...] = value[pl.ds(pl.multiple_of((info_ref[2] ^ k) * C, 16), C)].astype(BF)


def project_qkv(info, x, w_query, w_key, w_value, deps):
    T, D = x.shape

    def body(info_ref, get, q, kv):
        xv = get(0)[...]
        kv[:, :D] = nn(xv, get(1)[...]).astype(BF)
        kv[:, D:] = nn(xv, get(2)[...]).astype(BF)
        q[...] = (nn(xv, get(3)[...]) * (0.125 * LOG2E)).astype(BF)

    return fused("qkv", info, body, [x, w_key, w_value, w_query], [shape(T, D, BF), shape(T, 2 * D, BF)], deps=deps)


def project_source(info, x, w_key, w_value, deps):
    T, D = x.shape

    def body(info_ref, get, kv):
        xv = get(0)[...]
        kv[:, :D] = nn(xv, get(1)[...]).astype(BF)
        kv[:, D:] = nn(xv, get(2)[...]).astype(BF)

    return fused("source_kv", info, body, [x, w_key, w_value], [shape(T, 2 * D, BF)], deps=deps)[0]


def attend_self(info, q, kv, kv_peer, masks, deps):
    return attend(SELF_PLANS, info, q, kv, kv_peer, *masks, [], [], lambda get, att: None, deps)


def between(info, x, att, w_out, c_query, src, c_key, c_value, deps):
    T, D = x.shape

    def body(info_ref, get, kv, y_ref, low_ref, inv_ref, cq_ref):
        xv = get(0)[...]
        kv[:, :D] = nn(xv, get(1)[...]).astype(BF)
        kv[:, D:] = nn(xv, get(2)[...]).astype(BF)
        y, inv = norm_parts(get(5)[...].astype(F32) + nn(get(3)[...], get(4)[...]))
        low = y.astype(BF)
        y_ref[...] = y
        low_ref[...] = low
        inv_ref[...] = jnp.broadcast_to(inv, inv_ref.shape)
        cq_ref[...] = (nn(low, get(6)[...]) * (0.125 * LOG2E)).astype(BF)

    outs = [shape(T, 2 * D, BF), shape(T, D, F32), shape(T, D, BF), shape(T, 128, F32), shape(T, D, BF)]
    return fused("between", info, body, [src, c_key, c_value, att, w_out, x, c_query], outs, deps=deps)


def attend_cross(info, q, kv, kv_peer, masks, y1, c_out):
    T, D = q.shape

    def finish(get, att, low_ref, inv_ref, y_ref):
        y, inv = norm_parts(get(1)[...] + nn(att[...], get(0)[...]))
        inv_ref[...] = jnp.broadcast_to(inv, inv_ref.shape)
        low_ref[...] = y.astype(BF)
        y_ref[...] = y

    outs = [shape(T, D, BF), shape(T, 128, F32), shape(T, D, F32)]
    return attend(CROSS_PLANS, info, q, kv, kv_peer, *masks, [c_out, y1], outs, finish)


def feed_forward(info, x, first, second, c, y2, down, up, g_out, scale, block=1024):
    T, D = x.shape
    width = first.shape[1]
    F = 2 * width
    per = width // block
    A = down.shape[1]
    held = Loads([down, up, scale, first, second, y2, g_out])

    def kernel(info_ref, x_ref, c_ref, *refs):
        ins = refs[: len(held.arrays)]
        gp_ref, out0, out1, g3_ref, kept_ref, sent_ref, gnar_ref, acc, sq, gn, *scratch = refs[len(held.arrays) :]
        i = pl.program_id(0)
        bound = held.bind(info_ref, ins, scratch)
        pl.when(i == 0)(lambda: start_all(bound))
        cols = pl.ds(pl.multiple_of(lax.rem(i, per) * block, 128), block)

        @pl.when(i == 0)
        def _():
            get = getter(bound)
            h, g = gelu_pair(nn(x_ref[...], get(0)[...]))
            sq[...] = h.astype(BF)
            gn[...] = g.astype(BF)
            acc[...] = get(2)[0:1, 0:1] * nn(sq[...], get(1)[...])

        for v in range(2):
            copies, buf = bound[3 + v]

            @pl.when(i == v * per)
            def _():
                for copy in copies:
                    copy.wait()

            @pl.when(i // per == v)
            def _():
                h, g = gelu_pair(nn(x_ref[...], buf[:, cols]))
                gp_ref[...] = g.astype(BF)
                acc[...] += nn(h.astype(BF), c_ref[...])

        @pl.when(i == F // block - 1)
        def _():
            get = getter(bound[5:])
            y, inv = norm_parts(acc[...] + get(0)[...])
            g3 = norm_back(y, inv, get(1)[...].astype(F32))
            g3_ref[...] = g3
            acc[...] = y
            put_slots(info_ref, acc, out0, out1)
            ga = (bound[2][1][0:1, 0:1] * g3).astype(BF)
            gup = tn(sq[...], ga).astype(BF)
            gnar = (gn[...].astype(F32) * nt(ga, bound[1][1][...])).astype(BF)
            gnar_ref[...] = gnar
            gdown = tn(x_ref[...], gnar).astype(BF)
            gdown = jnp.concatenate([gdown[k : k + A] for k in range(0, D, A)], axis=1)
            for side, keep, send in ((0, gup, gdown), (1, gdown, gup)):
                @pl.when(info_ref[3] == side)
                def _():
                    kept_ref[...] = keep
                    sent_ref[...] = send

    outs = [shape(T // 2, D, BF)] * 2 + [shape(T, D, F32), shape(A, D, BF), shape(A, D, BF), shape(T, A, BF)]
    return pl.pallas_call(
        kernel,
        grid_spec=pltpu.PrefetchScalarGridSpec(
            num_scalar_prefetch=1,
            grid=(F // block,),
            in_specs=[pl.BlockSpec((T, D), lambda i, *_: (0, 0)), pl.BlockSpec((block, D), lambda i, *_: (i, 0))]
            + held.specs,
            out_specs=[pl.BlockSpec((T, block), lambda i, *_: (0, i))]
            + [pl.BlockSpec(o.shape, lambda i, *_: (0, 0)) for o in outs],
            scratch_shapes=[pltpu.VMEM((T, D), F32)] + [pltpu.VMEM((T, A), BF)] * 2 + held.scratch,
        ),
        out_shape=[shape(T, F, BF)] + outs,
        compiler_params=params(),
        cost_estimate=cost(26),
        name="feed_forward",
    )(info, x, c, *held.arrays)


def ffn_back(info, g3, c, first, second, gp, gnar, down, low, inv, c_out, deps, block=1024):
    T, D = g3.shape
    F = c.shape[0]
    width = first.shape[1]
    per = width // block
    held = Loads([first, second, gnar, down, c_out, low, inv])

    def kernel(info_ref, g3_ref, c_ref, gp_ref, *refs):
        ins = refs[: len(held.arrays)]
        g2_ref, ga_ref, acc, *scratch = refs[len(held.arrays) + len(deps) :]
        i = pl.program_id(0)
        bound = held.bind(info_ref, ins, scratch)
        pl.when(i == 0)(lambda: start_all(bound))
        gh = (nt(g3_ref[...].astype(BF), c_ref[...]) * gp_ref[...].astype(F32)).astype(BF)

        @pl.when(i == 0)
        def _():
            acc[...] = g3_ref[...]

        for v in range(2):
            copies, e = bound[v]

            @pl.when(i == v * per)
            def _():
                for copy in copies:
                    copy.wait()

            @pl.when(i // per == v)
            def _():
                acc[...] += nt(gh, e[:, pl.ds(pl.multiple_of(lax.rem(i, per) * block, 128), block)])

        @pl.when(i == F // block - 1)
        def _():
            get = getter(bound)
            g2 = norm_back(get(5)[...].astype(F32), get(6)[:, 0:1], acc[...] + nt(get(2)[...], get(3)[...]))
            g2_ref[...] = g2
            ga_ref[...] = nt(g2.astype(BF), get(4)[...]).astype(BF)

    outs = [shape(T, D, F32), shape(T, D, BF)]
    return pl.pallas_call(
        kernel,
        grid_spec=pltpu.PrefetchScalarGridSpec(
            num_scalar_prefetch=1,
            grid=(F // block,),
            in_specs=[pl.BlockSpec((T, D), lambda i, *_: (0, 0)), pl.BlockSpec((block, D), lambda i, *_: (i, 0)),
                      pl.BlockSpec((T, block), lambda i, *_: (0, i))] + held.specs + [ANYWHERE] * len(deps),
            out_specs=[pl.BlockSpec(o.shape, lambda i, *_: (0, 0)) for o in outs],
            scratch_shapes=[pltpu.VMEM((T, D), F32)] + held.scratch,
        ),
        out_shape=outs,
        compiler_params=params(),
        cost_estimate=cost(18),
        name="ffn_back",
    )(info, g3, c, gp, *held.arrays, *deps)


def attend_cross_back(info, q, kv, kv_peer, do, o, r, p, g2, y1, inv1, c_query, w_out, deps):
    T, D = q.shape

    def finish(get, gq, g1_ref, ga_ref):
        g = get(1)[...] + 0.125 * nt(gq[...], get(0)[...])
        g1 = norm_back(get(2)[...].astype(F32), get(3)[:, 0:1], g)
        g1_ref[...] = g1
        ga_ref[...] = nt(g1.astype(BF), get(4)[...]).astype(BF)

    return attend_back(CROSS_PLANS, info, q, kv, kv_peer, do, o, r, p, [c_query, g2, y1, inv1, w_out],
                       [shape(T, D, F32), shape(T, D, BF)], finish, deps)


def attend_self_back(info, q, kv, kv_peer, do, o, r, p, g1, w_query, deps):
    T, D = q.shape

    def finish(get, gq, acc_ref):
        acc_ref[...] = get(1)[...] + 0.125 * nt(gq[...], get(0)[...])

    return attend_back(SELF_PLANS, info, q, kv, kv_peer, do, o, r, p, [w_query, g1], [shape(T, D, F32)], finish, deps)


def add_pairs(mine, got, part):
    D = mine.shape[1] // 2
    out = []
    for h in range(D // 128):
        at = slice(256 * h + 128 * part, 256 * h + 128 * part + 128)
        out.append((mine[:, at].astype(F32) + got[:, at].astype(F32)).astype(BF))
    return jnp.concatenate(out, axis=1)


def source_grad(info, gkv, got, w_key, w_value, deps):
    T, D = gkv.shape[0], gkv.shape[1] // 2

    def body(info_ref, get, out0, out1, total):
        mine, other = get(0), get(1)
        acc = nt(add_pairs(mine, other, 0), get(2)[...])
        total[...] = acc + nt(add_pairs(mine, other, 1), get(3)[...])
        put_slots(info_ref, total, out0, out1)

    return fused("source_grad", info, body, [gkv, got, w_key, w_value], [shape(T // 2, D, BF)] * 2, deps=deps,
                 extra=[pltpu.VMEM((T, D), F32)])


def token_grad(info, acc, gkv, got, w_key, w_value, deps):
    T, D = acc.shape

    def body(info_ref, get, out0, out1):
        mine, other = get(0), get(1)
        total = nt(add_pairs(mine, other, 0), get(2)[...])
        total += nt(add_pairs(mine, other, 1), get(3)[...])
        g = get(4)
        g[...] += total
        put_slots(info_ref, g, out0, out1)

    return fused("token_grad", info, body, [gkv, got, w_key, w_value, acc], [shape(T // 2, D, BF)] * 2, deps=deps)


def move(value, target):
    dp, seq = lax.axis_size("dp"), lax.axis_size("seq")
    pairs = []
    for d in range(dp):
        for s in range(seq):
            a, b = target(d, s)
            pairs.append((d * seq + s, a * seq + b))
    return lax.ppermute(value, ("dp", "seq"), pairs)


def flip(value, bit):
    return move(value, lambda d, s: (d ^ bit, s))


def core_of(chunk):
    return (0, 1, 1, 0)[chunk]


def pick(flag, first, second):
    return jnp.where(flag, first, second)


def send_pieces(pieces):
    return [
        move(piece, lambda a, q, k=k: (2 * (a // 2) + core_of(q), 2 * (a % 2) + (q + k) % 2))
        for k, piece in enumerate(pieces)
    ]


def take_pieces(value, s):
    return [lax.dynamic_index_in_dim(value, (s + k) % 2, 0, keepdims=False) for k in range(2)]


def send_back(pieces):
    dp, seq = lax.axis_size("dp"), lax.axis_size("seq")
    got = []
    for k, piece in enumerate(pieces):
        back = {}
        for a in range(dp):
            for q in range(seq):
                back[(2 * (a // 2) + core_of(q), 2 * (a % 2) + (q + k) % 2)] = (a, q)
        got.append(move(piece, lambda a, b: back[(a, b)]))
    return got


def join_rows(got, s):
    even = s % 2 == 0
    return jnp.stack([pick(even, got[0], got[1]), pick(even, got[1], got[0])])


def first_hop(pair, low):
    return [flip(pair[0], 2 * low), flip(pair[1], 4 * low)]


def second_hop(near, low):
    return [flip(near[0], 4 * low), flip(near[1], 2 * low)]


def all_parts(near, far, low):
    out = []
    for v in range(2):
        half = near[v].shape[0] // 2
        b1, b2 = ((2, 4), (4, 2))[v]
        arrays = [near[v], far[v], flip(near[v], low), flip(far[v], low)]
        parts = {}
        for a, m in zip(arrays, (0, b2, 1, b2 ^ 1)):
            parts[m] = (a, 0)
            parts[m ^ b1] = (a, half)
        out.append([parts[m] for m in range(8)])
    return out


class Reduce:
    def __init__(self, kept, sent, d, s, low):
        self.d, self.s, self.low = d, s, low
        self.kept, self.got = kept, [flip(sent, low)]

    def plane(self, v, m):
        return flip(v, 2 * self.low * m)

    def scatter_plane(self):
        me = self.d // (2 * self.low)
        parts = self.value.reshape(4, -1, self.value.shape[1])
        take = [lax.dynamic_index_in_dim(parts, me ^ m, 0, keepdims=False) for m in range(4)]
        self.kept, self.got = take[0], [self.plane(take[m], m) for m in range(1, 4)]

    def line(self, bit):
        self.kept, self.got = self.value, [move(self.value, lambda a, b: (a, b ^ bit))]

    def add(self):
        total = self.kept.astype(F32)
        for got in self.got:
            total += got.astype(F32)
        self.value = total.astype(BF)

    def low_bits(self):
        bit = 1
        while bit < self.low:
            got = flip(self.value, bit)
            self.value = (self.value.astype(F32) + got.astype(F32)).astype(BF)
            bit *= 2

    def gather_plane(self):
        self.me = self.d // (2 * self.low)
        self.got = [self.value] + [self.plane(self.value, m) for m in range(1, 4)]

    def put(self):
        got = self.got
        n, rows = len(got), []
        for j in range(n):
            part = got[n - 1]
            for m in range(n - 1):
                part = pick((self.me ^ j) == m, got[m], part)
            rows.append(part)
        self.value = jnp.concatenate(rows, axis=0)


def local(tokens, source, target_lengths, source_lengths, step_index, self_query, self_key, self_value,
          self_out, cross_query, cross_key, cross_value, cross_out, ffn_expand, ffn_contract, adapter_down,
          adapter_up, grad_output):
    rows, C, D = tokens.shape
    dp, seq = lax.axis_size("dp"), lax.axis_size("seq")
    assert rows == 2 and seq == 4 and dp % 8 == 0
    low = dp // 8
    d, s = lax.axis_index("dp"), lax.axis_index("seq")
    core = d % 2
    info = jnp.stack([core, d // low, (s + d) % 2, (d // low) % 2]).astype(jnp.int32)

    def widen(shard):
        if low == 1:
            return shard
        groups = [[g * low + i for i in range(low)] for g in range(8)]
        return lax.all_gather(shard, "dp", axis=0, tiled=True, axis_index_groups=groups)

    def rows_of(*weights):
        return jnp.concatenate(weights, axis=0)

    t = send_pieces(take_pieces(tokens, s))
    sq, sk, sv, ex = [widen(w) for w in (self_query, self_key, self_value, ffn_expand)]
    n = sq.shape[0]
    h = n // 2
    pair = [rows_of(sk, sv[:h]), rows_of(sq, sv[h:])]
    rest = join_up([self_out, cross_key, cross_value, cross_query, cross_out], ())
    near = beside(pair, first_hop(pair, low), (t[0],))
    e1, e2, c_shard = stage(ex, ffn_contract, near)
    rest = lax.all_gather(rest, "dp", axis=0, tiled=True)
    each = self_out.shape[0]
    w_out, c_key, c_value, c_query, c_out = [Shards(rest, dp, j * each, each) for j in range(5)]

    mine = jnp.concatenate([target_lengths, source_lengths[:, None]], axis=1)
    other = flip(mine, 1)
    table = jnp.concatenate([pick(core == 0, mine, other), pick(core == 0, other, mine)], axis=0)
    row = lax.dynamic_index_in_dim(table, s, 0, keepdims=False)
    lens, src_len = row[:-1], row[-1]
    docs = lens.shape[0]
    ends = jnp.cumsum(lens)[:-1]
    i = jnp.arange(2 * C, dtype=jnp.int32)
    slot = i // C

    def place(which):
        chunk = pick(which == 0, slot * 3, slot + 1)
        return chunk * C + i % C

    lanes = jnp.arange(128, dtype=jnp.int32) % 64

    def doc_hot(pos):
        doc = jnp.sum((pos[:, None] >= ends[None, :]).astype(jnp.int32), axis=-1)
        return doc[:, None] == lanes[None, :]

    own_pos, peer_pos = place(core), place(1 - core)
    k_aug = [doc_hot(own_pos).astype(BF), doc_hot(peer_pos).astype(BF)]
    q_aug = jnp.where(doc_hot(own_pos) | (lanes >= docs)[None, :], 0.0, NEG).astype(BF)
    ck_aug = [((pos[:, None] >= src_len) & (lanes == 0)[None, :]).astype(BF) for pos in (own_pos, peer_pos)]
    cq_aug = jnp.broadcast_to(jnp.where(lanes == 0, NEG, 0.0).astype(BF)[None, :], (2 * C, 128))

    scale = jnp.full((8, 128), (step_index[0] + 1).astype(F32) / 5.0, F32)
    src = send_pieces(gate(take_pieces(source, s), t))
    far = gate(
        second_hop(near, low), (*src, info, q_aug, *k_aug, cq_aug, *ck_aug, scale, e1, e2)
    )
    a1, b1 = all_parts(near, far, low)
    w_key, w_query = Pieces(n, (a1, 0, n, 0)), Pieces(n, (b1, 0, n, 0))
    w_value = Pieces(n, (a1, n, h, 0), (b1, n, h, h))
    x = Slots(t, 0, C)
    q, kv = project_qkv(info, x, w_query, w_key, w_value, ())
    q, kv, e1, e2 = barrier(q, kv, e1, e2)
    kv_peer = flip(kv, 1)
    first3, second3 = first_hop([e1, e2], low), second_hop([e1, e2], low)
    attended, p_self, r_self = attend_self(info, q, kv, kv_peer, (q_aug, *k_aug), ())
    *first3, attended, c_shard = barrier(*first3, attended, c_shard)
    w_contract = lax.all_gather(c_shard, "dp", axis=0, tiled=True)
    far3 = second_hop(first3, low)
    flips = [flip(v, low) for v in (e1, e2, *first3)]
    skv, y1, y1_low, inv1, cq = between(info, x, attended, w_out, c_query, Slots(src, 0, C), c_key, c_value, ())
    *flips, skv, cq, h0, h1, g0, g1 = barrier(*flips, skv, cq, *second3, *take_pieces(grad_output, s))
    second3, pieces = [h0, h1], [g0, g1]
    g_out = send_pieces(pieces)
    skv_peer = flip(skv, 1)
    cross_attended, p_cross, r_cross, second_low, inv2, y2 = attend_cross(
        info, cq, skv, skv_peer, (cq_aug, *ck_aug), y1, c_out
    )
    f0, f1, h0, h1, g0, g1, second_low = barrier(*far3, *second3, *g_out, second_low)
    far3, second3, g_out = [f0, f1], [h0, h1], [g0, g1]
    a3, b3 = [
        [(v, 0) for _, v in sorted(
            {0: own, 1: flips[i], b1: first3[i], b1 ^ 1: flips[2 + i], b2: second3[i], b2 ^ 1: flip(second3[i], low),
             6: far3[i], 7: flip(far3[i], low)}.items()
        )]
        for i, (own, b1, b2) in enumerate(((e1, 2, 4), (e2, 4, 2)))
    ]
    ea, eb = Pieces(n, (a3, 0, n, 0)), Pieces(n, (b3, 0, n, 0))
    gp, o0, o1, g3, kept, sent, gnar = feed_forward(
        info, second_low, ea, eb, w_contract, y2, adapter_down, adapter_up, Slots(g_out, 0, C), scale
    )
    output = send_back([o0, o1])
    total = Reduce(kept, sent, d, s, low)
    g2, grad_cross = ffn_back(info, g3, w_contract, ea, eb, gp, gnar, adapter_down, second_low, inv2, c_out, ())
    *total.got, g2, grad_cross = barrier(*total.got, g2, grad_cross)
    total.add()
    total.scatter_plane()
    gkv, gkv_peer, g1, grad_self = attend_cross_back(
        info, cq, skv, skv_peer, grad_cross, cross_attended, r_cross, p_cross, g2, y1_low, inv1, c_query, w_out, (total.kept,)
    )
    *total.got, o0, o1, grad_self, gkv_peer = barrier(*total.got, *output, grad_self, gkv_peer)
    output = [o0, o1]
    total.add()
    total.line(2)
    got = flip(gkv_peer, 1)
    pieces = source_grad(info, gkv, got, c_key, c_value, (grad_self, total.kept))
    pieces = send_back(pieces)
    gkv, gkv_peer, acc = attend_self_back(
        info, q, kv, kv_peer, grad_self, attended, r_self, p_self, g1, w_query, pieces[:0]
    )
    *total.got, s0, s1, gkv_peer = barrier(*total.got, *pieces, gkv_peer)
    got = flip(gkv_peer, 1)
    total.add()
    total.line(1)
    pieces = token_grad(info, acc, gkv, got, w_key, w_value, (total.kept,))
    *total.got, o0, o1, s0, s1, t0, t1 = barrier(*total.got, *output, s0, s1, *pieces)
    tokens_back = send_back([t0, t1])
    output = [o0, o1]
    total.add()
    total.low_bits()
    total.gather_plane()
    total.put()
    grads, other = total.value, flip(total.value, low)
    high = (d // low) % 2 == 1
    grad_up = pick(high, other, grads).astype(F32)
    A = adapter_down.shape[1]
    grad_down = pick(high, grads, other).astype(F32)
    grad_down = rows_of(*[grad_down[:, k : k + A] for k in range(0, D, A)])
    output, grad_source, grad_tokens = [join_rows(v, s) for v in (output, [s0, s1], tokens_back)]
    return (output, grad_tokens, grad_source, grad_down, grad_up)


def solution(mesh):
    rows = P("dp", "seq", None)
    weight = P("dp", None)
    return jax.shard_map(
        local,
        mesh=mesh,
        in_specs=(rows, rows, weight, P("dp"), P()) + (weight,) * 10 + (P(), P(), rows),
        out_specs=(rows, rows, rows, P(), P()),
        check_vma=False,
    )
```

```python
import functools

import jax
import jax.numpy as jnp
from jax import lax
from jax.experimental import pallas as pl
from jax.experimental.pallas import tpu as pltpu
from jax.sharding import PartitionSpec as P

BF, F32 = jnp.bfloat16, jnp.float32
NEG = -1e30
LOG2E = 1.4426950408889634
PER = 2

SELF_PLANS = (
    (((0, True),), ((0, False), (2, False), (3, False), (1, True))),
    (((2, False), (0, True)), ((2, False), (0, False), (1, True))),
)
CROSS_PLANS = ((((0, False), (1, False), (2, False), (3, False)),) * 2,)


def nt(a, b):
    return lax.dot_general(a, b, (((1,), (1,)), ((), ())), preferred_element_type=F32)


def nn(a, b):
    return lax.dot_general(a, b, (((1,), (0,)), ((), ())), preferred_element_type=F32)


def tn(a, b):
    return lax.dot_general(a, b, (((0,), (0,)), ((), ())), preferred_element_type=F32)


def cost(us):
    return pl.CostEstimate(flops=int(us * 3e8), bytes_accessed=1024, transcendentals=0)


def params():
    return pltpu.CompilerParams(vmem_limit_bytes=64 * 1024 * 1024)


def shape(rows, cols, dtype):
    return jax.ShapeDtypeStruct((rows, cols), dtype)


class Whole:
    def __init__(self, array):
        self.arrays, self.shape, self.dtype, self.count = [array], array.shape, array.dtype, 1

    def copies(self, info, refs, buf, sem, first):
        return [pltpu.make_async_copy(refs[0], buf, sem.at[first])]


class Pieces:
    def __init__(self, stride, *pieces):
        self.stride, self.pieces = stride, pieces
        self.arrays = [a for parts, *_ in pieces for a, _ in parts]
        self.shape, self.dtype = (8 * stride, self.arrays[0].shape[1]), self.arrays[0].dtype
        self.count = len(self.arrays)

    def copies(self, info, refs, buf, sem, first):
        out = []
        for parts, at, rows, base in self.pieces:
            for m, (_, start) in enumerate(parts):
                to = pl.multiple_of((info[1] ^ m) * self.stride + base, 16)
                i = len(out)
                out.append(
                    pltpu.make_async_copy(
                        refs[i].at[pl.ds(start + at, rows)], buf.at[pl.ds(to, rows)], sem.at[first + i]
                    )
                )
        return out


class Shards:
    def __init__(self, array, owners, at, rows):
        self.arrays, self.count, self.at, self.rows = [array], owners, at, rows
        self.each = array.shape[0] // owners
        self.shape, self.dtype = (owners * rows, array.shape[1]), array.dtype

    def copies(self, info, refs, buf, sem, first):
        return [
            pltpu.make_async_copy(
                refs[0].at[pl.ds(j * self.each + self.at, self.rows)],
                buf.at[pl.ds(j * self.rows, self.rows)],
                sem.at[first + j],
            )
            for j in range(self.count)
        ]


class Slots:
    def __init__(self, arrays, at, rows):
        self.arrays, self.at, self.rows, self.count = list(arrays), at, rows, 2
        self.shape, self.dtype = (2 * rows, arrays[0].shape[1]), arrays[0].dtype

    def copies(self, info, refs, buf, sem, first):
        return [
            pltpu.make_async_copy(
                refs[k].at[pl.ds(self.at, self.rows)],
                buf.at[pl.ds(pl.multiple_of((info[2] ^ k) * self.rows, 16), self.rows)],
                sem.at[first + k],
            )
            for k in range(2)
        ]


class Chunk:
    def __init__(self, array, k):
        self.arrays, self.k, self.count = [array], k, 1
        self.shape, self.dtype = (array.shape[0] // 2, array.shape[1]), array.dtype

    def copies(self, info, refs, buf, sem, first):
        rows = self.shape[0]
        at = pl.multiple_of((info[2] ^ self.k) * rows, 16)
        return [pltpu.make_async_copy(refs[0].at[pl.ds(at, rows)], buf, sem.at[first])]


class Loads:
    def __init__(self, loads):
        self.loads = [v if hasattr(v, "copies") else Whole(v) for v in loads]
        self.arrays = [a for v in self.loads for a in v.arrays]
        self.specs = [pl.BlockSpec(memory_space=pl.ANY)] * len(self.arrays)
        self.scratch = [pltpu.VMEM(v.shape, v.dtype) for v in self.loads]
        self.scratch.append(pltpu.SemaphoreType.DMA((sum(v.count for v in self.loads),)))

    def bind(self, info, refs, scratch):
        bufs, sem = scratch[:-1], scratch[-1]
        at = first = 0
        out = []
        for v, buf in zip(self.loads, bufs):
            out.append((v.copies(info, refs[at : at + len(v.arrays)], buf, sem, first), buf))
            at += len(v.arrays)
            first += v.count
        return out


def start_all(bound):
    for copies, _ in bound:
        for c in copies:
            c.start()


def getter(bound):
    ready = set()

    def get(i):
        copies, buf = bound[i]
        if i not in ready:
            for c in copies:
                c.wait()
            ready.add(i)
        return buf

    return get


ANYWHERE = pl.BlockSpec(memory_space=pl.ANY)


def half_mask(shape, h):
    lane = lax.broadcasted_iota(jnp.int32, shape, 1)
    return (lane < 64) if h == 0 else (lane >= 64)


def top(parts):
    rows = 64
    pieces = [p[i : i + rows] for p in parts for i in range(0, p.shape[0], rows)]
    while len(pieces) > 1:
        pieces = [jnp.maximum(*pieces[i : i + 2]) if i + 1 < len(pieces) else pieces[i] for i in range(0, len(pieces), 2)]
    return jnp.max(pieces[0], axis=0, keepdims=True)


def forward_pair(plan, C, q, ks, vs, qa, kas, put, p_ref):
    kaug = [[jnp.where(half_mask(k.shape, h), k, a) for k, a in zip(ks, kas)] for h in range(2)]
    vts = [v.T for v in vs]
    ones = jnp.ones((16, C), BF)
    units, n = [], 0
    for slot, blocks in enumerate(plan):
        units += [(slot, h, n, blocks) for h in range(2)]
        n += len(blocks)

    def scores_of(unit):
        slot, h, _, blocks = unit
        rows = slice(slot * C, (slot + 1) * C)
        qh = jnp.where(half_mask((C, 128), h), q[rows], qa[rows])
        scores = []
        for kb, diagonal in blocks:
            s = nt(kaug[h][kb], qh)
            if diagonal:
                ki = lax.broadcasted_iota(jnp.int32, s.shape, 0)
                qi = lax.broadcasted_iota(jnp.int32, s.shape, 1)
                s = jnp.where(ki <= qi, s, NEG)
            scores.append(s)
        return scores, top(scores)

    def rest(unit, scores, m):
        _, h, n, blocks = unit
        ps = [jnp.exp2(s - m).astype(BF) for s in scores]
        for i, p in enumerate(ps):
            p_ref[h, n + i] = p
        values = [jnp.concatenate([vts[kb][64 * h : 64 * h + 64], ones], axis=0) for kb, _ in blocks]
        both = nn(jnp.concatenate(values, axis=1), jnp.concatenate(ps, axis=0))
        inv = 1.0 / both[64:65]
        return both[:64] * inv, jnp.broadcast_to(inv, (64, C))

    done = []
    AHEAD = 2
    pending = [scores_of(u) for u in units[:AHEAD]]
    for i, unit in enumerate(units):
        if i + AHEAD < len(units):
            pending.append(scores_of(units[i + AHEAD]))
        done.append(rest(unit, *pending[i]))
        if i % 2:
            halves, inverses = zip(*done[-2:])
            put(unit[0], jnp.concatenate(halves, axis=0).T.astype(BF), jnp.concatenate(inverses, axis=0).T)


def by_plan(plans, info, run):
    if len(plans) == 1:
        run(plans[0])
    else:
        for v, plan in enumerate(plans):
            pl.when(info[0] == v)(functools.partial(run, plan))


def attend(plans, info, q, own, peer, qa, kao, kap, loads, outs, finish, deps=()):
    T, D = q.shape
    C, pairs = T // 2, D // 128
    steps = pairs // PER
    nb = sum(len(b) for b in plans[0])
    held = Loads(loads)

    def kernel(info_ref, q_ref, ko, vo, kp, vp, qa_ref, kao_ref, kap_ref, *refs):
        ins = refs[: len(held.arrays)]
        o_ref, p_ref, r_ref, *out_refs = refs[len(held.arrays) + len(deps) :][: 3 + len(outs)]
        att, *scratch = refs[len(held.arrays) + len(deps) + 3 + len(outs) :]
        step = pl.program_id(0)
        bound = held.bind(info_ref, ins, scratch)
        pl.when(step == 0)(lambda: start_all(bound))

        def run(plan):
            for j in range(PER):
                at = slice(128 * j, 128 * j + 128)
                cols = pl.ds(pl.multiple_of((step * PER + j) * 128, 128), 128)

                def put(slot, value, inverse):
                    o_ref[slot * C : (slot + 1) * C, at] = value
                    r_ref[slot * C : (slot + 1) * C, at] = inverse
                    att[slot * C : (slot + 1) * C, cols] = value

                def chunks(*rs):
                    return [r[i * C : (i + 1) * C, at] for r in rs for i in range(2)]

                masks = [m[i * C : (i + 1) * C] for m in (kao_ref, kap_ref) for i in range(2)]
                forward_pair(plan, C, q_ref[:, at], chunks(ko, kp), chunks(vo, vp), qa_ref[...], masks, put, p_ref.at[j])

        by_plan(plans, info_ref, run)

        @pl.when(step == steps - 1)
        def _():
            finish(getter(bound), att, *out_refs)

    col = pl.BlockSpec((T, 128 * PER), lambda h, *_: (0, h))
    val = pl.BlockSpec((T, 128 * PER), lambda h, *_: (0, steps + h))
    fix = pl.BlockSpec((T, 128), lambda h, *_: (0, 0))
    return pl.pallas_call(
        kernel,
        grid_spec=pltpu.PrefetchScalarGridSpec(
            num_scalar_prefetch=1,
            grid=(steps,),
            in_specs=[col] + [col, val] * 2 + [fix] * 3 + held.specs + [ANYWHERE] * len(deps),
            out_specs=[col, pl.BlockSpec((PER, 2, nb, C, C), lambda h, *_: (h, 0, 0, 0, 0)), col]
            + [pl.BlockSpec(o.shape, lambda h, *_: (0, 0)) for o in outs],
            scratch_shapes=[pltpu.VMEM((T, D), BF)] + held.scratch,
        ),
        out_shape=[shape(T, D, BF), jax.ShapeDtypeStruct((pairs, 2, nb, C, C), BF), shape(T, D, F32)] + list(outs),
        compiler_params=params(),
        cost_estimate=cost(25),
        name="attend",
    )(info, q, own, own, peer, peer, qa, kao, kap, *held.arrays, *deps)


def backward_pair(plan, C, q, ks, vs, do, o, r, p_ref, put, gown, gpeer):
    lane = lax.broadcasted_iota(jnp.int32, (C, 128), 1)
    l64 = lax.rem(lane, 64)
    ones = jnp.where(l64 < 2, 1.0, 0.0).astype(BF)
    vaug = [[jnp.where(half_mask(v.shape, h), v, ones) for v in vs] for h in range(2)]
    kts = [k.T for k in ks]
    by_key = [[] for _ in range(4)]
    zero = jnp.zeros((C, 128), BF)
    units, n = [], 0
    for slot, blocks in enumerate(plan):
        units += [(slot, h, n, blocks) for h in range(2)]
        n += len(blocks)

    def probs_back(unit):
        slot, h, n, blocks = unit
        rows = slice(slot * C, (slot + 1) * C)
        scaled = do[rows].astype(F32) * r[rows]
        dos = scaled.astype(BF)
        hm = lane < 64 if h == 0 else lane >= 64
        d = -jnp.sum(jnp.where(hm, scaled * o[rows].astype(F32), 0.0), axis=1, keepdims=True)
        hi = d.astype(BF)
        lo = (d - hi.astype(F32)).astype(BF)
        tail = jnp.where(l64 == 0, jnp.broadcast_to(hi, (C, 128)), jnp.where(l64 == 1, jnp.broadcast_to(lo, (C, 128)), zero))
        doa = jnp.where(hm, dos, tail)
        return [nt(vaug[h][kb], doa) for kb, _ in blocks], jnp.where(hm, dos, zero), jnp.where(hm, q[rows], zero)

    def rest(unit, dps, dom, qm):
        slot, h, n, blocks = unit
        grads = []
        for i, ((kb, _), dp) in enumerate(zip(blocks, dps)):
            pb = p_ref[h, n + i]
            ds = (pb.astype(F32) * dp).astype(BF)
            grads.append(ds)
            by_key[kb].append((pb, ds, dom, qm))
        wide = jnp.concatenate([kts[kb][64 * h : 64 * h + 64] for kb, _ in blocks], axis=1)
        return nn(wide, jnp.concatenate(grads, axis=0))

    done = []
    BACK = 2
    pending = [probs_back(u) for u in units[:BACK]]
    for i, unit in enumerate(units):
        if i + BACK < len(units):
            pending.append(probs_back(units[i + BACK]))
        done.append(rest(unit, *pending[i]))
        if i % 2:
            put(unit[0], jnp.concatenate(done[-2:], axis=0).T.astype(BF))
    for kb in range(4):
        ref = gown if kb < 2 else gpeer
        rows = slice((kb % 2) * C, (kb % 2) * C + C)
        if by_key[kb]:
            pbs, dss, doms, qms = zip(*by_key[kb])
            gk = nn(jnp.concatenate(dss, axis=1), jnp.concatenate(qms, axis=0))
            gv = nn(jnp.concatenate(pbs, axis=1), jnp.concatenate(doms, axis=0))
        else:
            gk = gv = jnp.zeros((C, 128), F32)
        ref[rows, 0:128] = (gk * (1.0 / LOG2E)).astype(BF)
        ref[rows, 128:256] = gv.astype(BF)


def attend_back(plans, info, q, own, peer, do, o, r, p, loads, outs, finish, deps=()):
    T, D = q.shape
    C, pairs, nb = T // 2, D // 128, p.shape[2]
    steps = pairs // PER
    held = Loads(loads)

    def kernel(info_ref, q_ref, ko, vo, kp, vp, do_ref, o_ref, r_ref, p_ref, *refs):
        ins = refs[: len(held.arrays)]
        gown, gpeer, *out_refs = refs[len(held.arrays) + len(deps) :][: 2 + len(outs)]
        gq, *scratch = refs[len(held.arrays) + len(deps) + 2 + len(outs) :]
        step = pl.program_id(0)
        bound = held.bind(info_ref, ins, scratch)
        pl.when(step == 0)(lambda: start_all(bound))

        def run(plan):
            for j in range(PER):
                at = slice(128 * j, 128 * j + 128)
                wide = slice(256 * j, 256 * j + 256)
                cols = pl.ds(pl.multiple_of((step * PER + j) * 128, 128), 128)

                def put(slot, value):
                    gq[slot * C : (slot + 1) * C, cols] = value

                def chunks(*rs):
                    return [r[i * C : (i + 1) * C, at] for r in rs for i in range(2)]

                backward_pair(plan, C, q_ref[:, at], chunks(ko, kp), chunks(vo, vp), do_ref[:, at], o_ref[:, at],
                              r_ref[:, at], p_ref.at[j], put, gown.at[:, wide], gpeer.at[:, wide])

        by_plan(plans, info_ref, run)

        @pl.when(step == steps - 1)
        def _():
            finish(getter(bound), gq, *out_refs)

    col = pl.BlockSpec((T, 128 * PER), lambda h, *_: (0, h))
    val = pl.BlockSpec((T, 128 * PER), lambda h, *_: (0, steps + h))
    wide = pl.BlockSpec((T, 256 * PER), lambda h, *_: (0, h))
    return pl.pallas_call(
        kernel,
        grid_spec=pltpu.PrefetchScalarGridSpec(
            num_scalar_prefetch=1,
            grid=(steps,),
            in_specs=[col] + [col, val] * 2 + [col] * 3
            + [pl.BlockSpec((PER, 2, nb, C, C), lambda h, *_: (h, 0, 0, 0, 0))] + held.specs + [ANYWHERE] * len(deps),
            out_specs=[wide] * 2 + [pl.BlockSpec(v.shape, lambda h, *_: (0, 0)) for v in outs],
            scratch_shapes=[pltpu.VMEM((T, D), BF)] + held.scratch,
        ),
        out_shape=[shape(T, 2 * D, BF)] * 2 + list(outs),
        compiler_params=params(),
        cost_estimate=cost(25),
        name="attend_back",
    )(info, q, own, own, peer, peer, do, o, r, p, *held.arrays, *deps)


def gate(values, deps):
    def kernel(*refs):
        del refs

    n = len(values)
    return pl.pallas_call(
        kernel,
        in_specs=[ANYWHERE] * (n + len(deps)),
        out_specs=[ANYWHERE] * n,
        out_shape=[jax.ShapeDtypeStruct(v.shape, v.dtype) for v in values],
        input_output_aliases={i: i for i in range(n)},
        cost_estimate=cost(0.1),
        name="gate",
    )(*values, *deps)


def barrier(*values):
    return gate(values, ())


def beside(pair, got, deps=()):
    def kernel(a, b, c, d, *refs):
        ab, cd = refs[-2:]
        n, m = a.shape[0], c.shape[0]
        ab[:n] = a[...]
        ab[n:] = b[...]
        cd[:m] = c[...]
        cd[m:] = d[...]

    full = pl.BlockSpec(memory_space=pltpu.VMEM)
    return pl.pallas_call(
        kernel,
        in_specs=[full] * 4 + [ANYWHERE] * len(deps),
        out_specs=[full] * 2,
        out_shape=[shape(2 * v.shape[0], v.shape[1], BF) for v in pair],
        cost_estimate=cost(2),
        compiler_params=params(),
        name="beside",
    )(pair[0], got[0], pair[1], got[1], *deps)


def join_up(arrays, deps):
    rows = [a.shape[0] for a in arrays]

    def kernel(*refs):
        at = 0
        for r, n in zip(refs, rows):
            refs[-1][at : at + n] = r[...]
            at += n

    full = pl.BlockSpec(memory_space=pltpu.VMEM)
    return pl.pallas_call(
        kernel,
        in_specs=[full] * len(arrays) + [ANYWHERE] * len(deps),
        out_specs=full,
        out_shape=shape(sum(rows), arrays[0].shape[1], BF),
        cost_estimate=cost(2),
        compiler_params=params(),
        name="join_up",
    )(*arrays, *deps)


def stage(expand_shard, contract_shard, deps):
    rows, cols = expand_shard.shape
    half = cols // 2

    def kernel(e_ref, c_ref, *refs):
        e1, e2, c = refs[-3:]
        e1[...] = e_ref[:, :half]
        e2[...] = e_ref[:, half:]
        c[...] = c_ref[...]

    full = pl.BlockSpec(memory_space=pltpu.VMEM)
    return pl.pallas_call(
        kernel,
        in_specs=[full, full] + [ANYWHERE] * len(deps),
        out_specs=[full] * 3,
        out_shape=[shape(rows, half, BF)] * 2 + [shape(*contract_shard.shape, BF)],
        cost_estimate=cost(3),
        compiler_params=params(),
        name="stage",
    )(expand_shard, contract_shard, *deps)


def fused(name, info, body, loads, outs, deps=(), extra=()):
    held = Loads(loads)
    total, nout = len(held.arrays), len(outs)

    def kernel(info_ref, *refs):
        out_refs = refs[total + len(deps) :][:nout]
        scratch = refs[total + len(deps) + nout :]
        bound = held.bind(info_ref, refs[:total], scratch[len(extra) :])
        start_all(bound)
        body(info_ref, getter(bound), *out_refs, *scratch[: len(extra)])

    return pl.pallas_call(
        kernel,
        grid_spec=pltpu.PrefetchScalarGridSpec(
            num_scalar_prefetch=1,
            grid=(1,),
            in_specs=held.specs + [ANYWHERE] * len(deps),
            out_specs=[pl.BlockSpec(o.shape, lambda i, *_: (0, 0)) for o in outs],
            scratch_shapes=list(extra) + held.scratch,
        ),
        out_shape=list(outs),
        compiler_params=params(),
        cost_estimate=cost(6),
        name=name,
    )(info, *held.arrays, *deps)


def norm_parts(v):
    mean = jnp.mean(v, axis=-1, keepdims=True)
    c = v - mean
    inv = lax.rsqrt(jnp.mean(c * c, axis=-1, keepdims=True) + 1e-05)
    return c * inv, inv


def norm_back(y, inv, g):
    return inv * (g - jnp.mean(g, axis=-1, keepdims=True) - y * jnp.mean(g * y, axis=-1, keepdims=True))


def gelu_pair(v):
    phi = 0.5 + 0.5 * lax.erf(v * 0.7071067811865476)
    pdf = jnp.exp(v * v * -0.5) * 0.3989422804014327
    return v * phi, phi + v * pdf


def put_slots(info_ref, value, first, second):
    C = value.shape[0] // 2
    for k, ref in enumerate((first, second)):
        ref[...] = value[pl.ds(pl.multiple_of((info_ref[2] ^ k) * C, 16), C)].astype(BF)


def project_qkv(info, x, w_query, w_key, w_value, deps):
    T, D = x.shape

    def body(info_ref, get, q, kv):
        xv = get(0)[...]
        kv[:, :D] = nn(xv, get(1)[...]).astype(BF)
        kv[:, D:] = nn(xv, get(2)[...]).astype(BF)
        q[...] = (nn(xv, get(3)[...]) * (0.125 * LOG2E)).astype(BF)

    return fused("qkv", info, body, [x, w_key, w_value, w_query], [shape(T, D, BF), shape(T, 2 * D, BF)], deps=deps)


def project_source(info, x, w_key, w_value, deps):
    T, D = x.shape

    def body(info_ref, get, kv):
        xv = get(0)[...]
        kv[:, :D] = nn(xv, get(1)[...]).astype(BF)
        kv[:, D:] = nn(xv, get(2)[...]).astype(BF)

    return fused("source_kv", info, body, [x, w_key, w_value], [shape(T, 2 * D, BF)], deps=deps)[0]


def attend_self(info, q, kv, kv_peer, masks, deps):
    return attend(SELF_PLANS, info, q, kv, kv_peer, *masks, [], [], lambda get, att: None, deps)


def between(info, x, att, w_out, c_query, src, c_key, c_value, deps):
    T, D = x.shape

    def body(info_ref, get, kv, y_ref, low_ref, inv_ref, cq_ref):
        xv = get(0)[...]
        kv[:, :D] = nn(xv, get(1)[...]).astype(BF)
        kv[:, D:] = nn(xv, get(2)[...]).astype(BF)
        y, inv = norm_parts(get(5)[...].astype(F32) + nn(get(3)[...], get(4)[...]))
        low = y.astype(BF)
        y_ref[...] = y
        low_ref[...] = low
        inv_ref[...] = jnp.broadcast_to(inv, inv_ref.shape)
        cq_ref[...] = (nn(low, get(6)[...]) * (0.125 * LOG2E)).astype(BF)

    outs = [shape(T, 2 * D, BF), shape(T, D, F32), shape(T, D, BF), shape(T, 128, F32), shape(T, D, BF)]
    return fused("between", info, body, [src, c_key, c_value, att, w_out, x, c_query], outs, deps=deps)


def attend_cross(info, q, kv, kv_peer, masks, y1, c_out):
    T, D = q.shape

    def finish(get, att, low_ref, inv_ref, y_ref):
        y, inv = norm_parts(get(1)[...] + nn(att[...], get(0)[...]))
        inv_ref[...] = jnp.broadcast_to(inv, inv_ref.shape)
        low_ref[...] = y.astype(BF)
        y_ref[...] = y

    outs = [shape(T, D, BF), shape(T, 128, F32), shape(T, D, F32)]
    return attend(CROSS_PLANS, info, q, kv, kv_peer, *masks, [c_out, y1], outs, finish)


def feed_forward(info, x, first, second, c, y2, down, up, g_out, scale, block=1024):
    T, D = x.shape
    width = first.shape[1]
    F = 2 * width
    per = width // block
    A = down.shape[1]
    held = Loads([down, up, scale, first, second, y2, g_out])

    def kernel(info_ref, x_ref, c_ref, *refs):
        ins = refs[: len(held.arrays)]
        gp_ref, out0, out1, g3_ref, kept_ref, sent_ref, gnar_ref, acc, sq, gn, *scratch = refs[len(held.arrays) :]
        i = pl.program_id(0)
        bound = held.bind(info_ref, ins, scratch)
        pl.when(i == 0)(lambda: start_all(bound))
        cols = pl.ds(pl.multiple_of(lax.rem(i, per) * block, 128), block)

        @pl.when(i == 0)
        def _():
            get = getter(bound)
            h, g = gelu_pair(nn(x_ref[...], get(0)[...]))
            sq[...] = h.astype(BF)
            gn[...] = g.astype(BF)
            acc[...] = get(2)[0:1, 0:1] * nn(sq[...], get(1)[...])

        for v in range(2):
            copies, buf = bound[3 + v]

            @pl.when(i == v * per)
            def _():
                for copy in copies:
                    copy.wait()

            @pl.when(i // per == v)
            def _():
                h, g = gelu_pair(nn(x_ref[...], buf[:, cols]))
                gp_ref[...] = g.astype(BF)
                acc[...] += nn(h.astype(BF), c_ref[...])

        @pl.when(i == F // block - 1)
        def _():
            get = getter(bound[5:])
            y, inv = norm_parts(acc[...] + get(0)[...])
            g3 = norm_back(y, inv, get(1)[...].astype(F32))
            g3_ref[...] = g3
            acc[...] = y
            put_slots(info_ref, acc, out0, out1)
            ga = (bound[2][1][0:1, 0:1] * g3).astype(BF)
            gup = tn(sq[...], ga).astype(BF)
            gnar = (gn[...].astype(F32) * nt(ga, bound[1][1][...])).astype(BF)
            gnar_ref[...] = gnar
            gdown = tn(x_ref[...], gnar).astype(BF)
            gdown = jnp.concatenate([gdown[k : k + A] for k in range(0, D, A)], axis=1)
            for side, keep, send in ((0, gup, gdown), (1, gdown, gup)):
                @pl.when(info_ref[3] == side)
                def _():
                    kept_ref[...] = keep
                    sent_ref[...] = send

    outs = [shape(T // 2, D, BF)] * 2 + [shape(T, D, F32), shape(A, D, BF), shape(A, D, BF), shape(T, A, BF)]
    return pl.pallas_call(
        kernel,
        grid_spec=pltpu.PrefetchScalarGridSpec(
            num_scalar_prefetch=1,
            grid=(F // block,),
            in_specs=[pl.BlockSpec((T, D), lambda i, *_: (0, 0)), pl.BlockSpec((block, D), lambda i, *_: (i, 0))]
            + held.specs,
            out_specs=[pl.BlockSpec((T, block), lambda i, *_: (0, i))]
            + [pl.BlockSpec(o.shape, lambda i, *_: (0, 0)) for o in outs],
            scratch_shapes=[pltpu.VMEM((T, D), F32)] + [pltpu.VMEM((T, A), BF)] * 2 + held.scratch,
        ),
        out_shape=[shape(T, F, BF)] + outs,
        compiler_params=params(),
        cost_estimate=cost(26),
        name="feed_forward",
    )(info, x, c, *held.arrays)


def ffn_back(info, g3, c, first, second, gp, gnar, down, low, inv, c_out, deps, block=1024):
    T, D = g3.shape
    F = c.shape[0]
    width = first.shape[1]
    per = width // block
    held = Loads([gnar, down, first, second, c_out, low, inv])

    def kernel(info_ref, g3_ref, c_ref, gp_ref, *refs):
        ins = refs[: len(held.arrays)]
        g2_ref, ga_ref, acc, *scratch = refs[len(held.arrays) + len(deps) :]
        i = pl.program_id(0)
        bound = held.bind(info_ref, ins, scratch)
        pl.when(i == 0)(lambda: start_all(bound))
        gh = (nt(g3_ref[...].astype(BF), c_ref[...]) * gp_ref[...].astype(F32)).astype(BF)

        @pl.when(i == 0)
        def _():
            get = getter(bound[:2])
            acc[...] = g3_ref[...] + nt(get(0)[...], get(1)[...])

        for v in range(2):
            copies, e = bound[2 + v]

            @pl.when(i == v * per)
            def _():
                for copy in copies:
                    copy.wait()

            @pl.when(i // per == v)
            def _():
                acc[...] += nt(gh, e[:, pl.ds(pl.multiple_of(lax.rem(i, per) * block, 128), block)])

        @pl.when(i == F // block - 1)
        def _():
            get = getter(bound[4:])
            g2 = norm_back(get(1)[...].astype(F32), get(2)[:, 0:1], acc[...])
            g2_ref[...] = g2
            ga_ref[...] = nt(g2.astype(BF), get(0)[...]).astype(BF)

    outs = [shape(T, D, F32), shape(T, D, BF)]
    return pl.pallas_call(
        kernel,
        grid_spec=pltpu.PrefetchScalarGridSpec(
            num_scalar_prefetch=1,
            grid=(F // block,),
            in_specs=[pl.BlockSpec((T, D), lambda i, *_: (0, 0)), pl.BlockSpec((block, D), lambda i, *_: (i, 0)),
                      pl.BlockSpec((T, block), lambda i, *_: (0, i))] + held.specs + [ANYWHERE] * len(deps),
            out_specs=[pl.BlockSpec(o.shape, lambda i, *_: (0, 0)) for o in outs],
            scratch_shapes=[pltpu.VMEM((T, D), F32)] + held.scratch,
        ),
        out_shape=outs,
        compiler_params=params(),
        cost_estimate=cost(18),
        name="ffn_back",
    )(info, g3, c, gp, *held.arrays, *deps)


def attend_cross_back(info, q, kv, kv_peer, do, o, r, p, g2, y1, inv1, c_query, w_out, deps):
    T, D = q.shape

    def finish(get, gq, g1_ref, ga_ref):
        g = get(1)[...] + 0.125 * nt(gq[...], get(0)[...])
        g1 = norm_back(get(2)[...].astype(F32), get(3)[:, 0:1], g)
        g1_ref[...] = g1
        ga_ref[...] = nt(g1.astype(BF), get(4)[...]).astype(BF)

    return attend_back(CROSS_PLANS, info, q, kv, kv_peer, do, o, r, p, [c_query, g2, y1, inv1, w_out],
                       [shape(T, D, F32), shape(T, D, BF)], finish, deps)


def attend_self_back(info, q, kv, kv_peer, do, o, r, p, g1, w_query, deps):
    T, D = q.shape

    def finish(get, gq, acc_ref):
        acc_ref[...] = get(1)[...] + 0.125 * nt(gq[...], get(0)[...])

    return attend_back(SELF_PLANS, info, q, kv, kv_peer, do, o, r, p, [w_query, g1], [shape(T, D, F32)], finish, deps)


def add_pairs(mine, got, part):
    D = mine.shape[1] // 2
    out = []
    for h in range(D // 128):
        at = slice(256 * h + 128 * part, 256 * h + 128 * part + 128)
        out.append((mine[:, at].astype(F32) + got[:, at].astype(F32)).astype(BF))
    return jnp.concatenate(out, axis=1)


def source_grad(info, gkv, got, w_key, w_value, deps):
    T, D = gkv.shape[0], gkv.shape[1] // 2

    def body(info_ref, get, out0, out1, total):
        mine, other = get(0), get(1)
        acc = nt(add_pairs(mine, other, 0), get(2)[...])
        total[...] = acc + nt(add_pairs(mine, other, 1), get(3)[...])
        put_slots(info_ref, total, out0, out1)

    return fused("source_grad", info, body, [gkv, got, w_key, w_value], [shape(T // 2, D, BF)] * 2, deps=deps,
                 extra=[pltpu.VMEM((T, D), F32)])


def token_grad(info, acc, gkv, got, w_key, w_value, deps):
    T, D = acc.shape

    def body(info_ref, get, out0, out1):
        mine, other = get(0), get(1)
        total = nt(add_pairs(mine, other, 0), get(2)[...])
        total += nt(add_pairs(mine, other, 1), get(3)[...])
        g = get(4)
        g[...] += total
        put_slots(info_ref, g, out0, out1)

    return fused("token_grad", info, body, [gkv, got, w_key, w_value, acc], [shape(T // 2, D, BF)] * 2, deps=deps)


def move(value, target):
    dp, seq = lax.axis_size("dp"), lax.axis_size("seq")
    pairs = []
    for d in range(dp):
        for s in range(seq):
            a, b = target(d, s)
            pairs.append((d * seq + s, a * seq + b))
    return lax.ppermute(value, ("dp", "seq"), pairs)


def flip(value, bit):
    return move(value, lambda d, s: (d ^ bit, s))


def core_of(chunk):
    return (0, 1, 1, 0)[chunk]


def pick(flag, first, second):
    return jnp.where(flag, first, second)


def send_pieces(pieces):
    return [
        move(piece, lambda a, q, k=k: (2 * (a // 2) + core_of(q), 2 * (a % 2) + (q + k) % 2))
        for k, piece in enumerate(pieces)
    ]


def take_pieces(value, s):
    return [lax.dynamic_index_in_dim(value, (s + k) % 2, 0, keepdims=False) for k in range(2)]


def send_back(pieces):
    dp, seq = lax.axis_size("dp"), lax.axis_size("seq")
    got = []
    for k, piece in enumerate(pieces):
        back = {}
        for a in range(dp):
            for q in range(seq):
                back[(2 * (a // 2) + core_of(q), 2 * (a % 2) + (q + k) % 2)] = (a, q)
        got.append(move(piece, lambda a, b: back[(a, b)]))
    return got


def join_rows(got, s):
    even = s % 2 == 0
    return jnp.stack([pick(even, got[0], got[1]), pick(even, got[1], got[0])])


def first_hop(pair, low):
    return [flip(pair[0], 2 * low), flip(pair[1], 4 * low)]


def second_hop(near, low):
    return [flip(near[0], 4 * low), flip(near[1], 2 * low)]


def all_parts(near, far, low):
    out = []
    for v in range(2):
        half = near[v].shape[0] // 2
        b1, b2 = ((2, 4), (4, 2))[v]
        arrays = [near[v], far[v], flip(near[v], low), flip(far[v], low)]
        parts = {}
        for a, m in zip(arrays, (0, b2, 1, b2 ^ 1)):
            parts[m] = (a, 0)
            parts[m ^ b1] = (a, half)
        out.append([parts[m] for m in range(8)])
    return out


class Reduce:
    def __init__(self, kept, sent, d, s, low):
        self.d, self.s, self.low = d, s, low
        self.kept, self.got = kept, [flip(sent, low)]

    def plane(self, v, m):
        return flip(v, 2 * self.low * m)

    def scatter_plane(self):
        me = self.d // (2 * self.low)
        parts = self.value.reshape(4, -1, self.value.shape[1])
        take = [lax.dynamic_index_in_dim(parts, me ^ m, 0, keepdims=False) for m in range(4)]
        self.kept, self.got = take[0], [self.plane(take[m], m) for m in range(1, 4)]

    def line(self, bit):
        self.kept, self.got = self.value, [move(self.value, lambda a, b: (a, b ^ bit))]

    def add(self):
        total = self.kept.astype(F32)
        for got in self.got:
            total += got.astype(F32)
        self.value = total.astype(BF)

    def low_bits(self):
        bit = 1
        while bit < self.low:
            got = flip(self.value, bit)
            self.value = (self.value.astype(F32) + got.astype(F32)).astype(BF)
            bit *= 2

    def gather_plane(self):
        self.me = self.d // (2 * self.low)
        self.got = [self.value] + [self.plane(self.value, m) for m in range(1, 4)]

    def put(self):
        got = self.got
        n, rows = len(got), []
        for j in range(n):
            part = got[n - 1]
            for m in range(n - 1):
                part = pick((self.me ^ j) == m, got[m], part)
            rows.append(part)
        self.value = jnp.concatenate(rows, axis=0)


def local(tokens, source, target_lengths, source_lengths, step_index, self_query, self_key, self_value,
          self_out, cross_query, cross_key, cross_value, cross_out, ffn_expand, ffn_contract, adapter_down,
          adapter_up, grad_output):
    rows, C, D = tokens.shape
    dp, seq = lax.axis_size("dp"), lax.axis_size("seq")
    assert rows == 2 and seq == 4 and dp % 8 == 0
    low = dp // 8
    d, s = lax.axis_index("dp"), lax.axis_index("seq")
    core = d % 2
    info = jnp.stack([core, d // low, (s + d) % 2, (d // low) % 2]).astype(jnp.int32)

    def widen(shard):
        if low == 1:
            return shard
        groups = [[g * low + i for i in range(low)] for g in range(8)]
        return lax.all_gather(shard, "dp", axis=0, tiled=True, axis_index_groups=groups)

    def rows_of(*weights):
        return jnp.concatenate(weights, axis=0)

    t = send_pieces(take_pieces(tokens, s))
    sq, sk, sv, ex = [widen(w) for w in (self_query, self_key, self_value, ffn_expand)]
    n = sq.shape[0]
    h = n // 2
    pair = [rows_of(sk, sv[:h]), rows_of(sq, sv[h:])]
    rest = join_up([self_out, cross_key, cross_value, cross_query, cross_out], ())
    near = beside(pair, first_hop(pair, low), (t[0],))
    e1, e2, c_shard = stage(ex, ffn_contract, near)
    rest = lax.all_gather(rest, "dp", axis=0, tiled=True)
    each = self_out.shape[0]
    w_out, c_key, c_value, c_query, c_out = [Shards(rest, dp, j * each, each) for j in range(5)]

    mine = jnp.concatenate([target_lengths, source_lengths[:, None]], axis=1)
    other = flip(mine, 1)
    table = jnp.concatenate([pick(core == 0, mine, other), pick(core == 0, other, mine)], axis=0)
    row = lax.dynamic_index_in_dim(table, s, 0, keepdims=False)
    lens, src_len = row[:-1], row[-1]
    docs = lens.shape[0]
    ends = jnp.cumsum(lens)[:-1]
    i = jnp.arange(2 * C, dtype=jnp.int32)
    slot = i // C

    def place(which):
        chunk = pick(which == 0, slot * 3, slot + 1)
        return chunk * C + i % C

    lanes = jnp.arange(128, dtype=jnp.int32) % 64

    def doc_hot(pos):
        doc = jnp.sum((pos[:, None] >= ends[None, :]).astype(jnp.int32), axis=-1)
        return doc[:, None] == lanes[None, :]

    own_pos, peer_pos = place(core), place(1 - core)
    k_aug = [doc_hot(own_pos).astype(BF), doc_hot(peer_pos).astype(BF)]
    q_aug = jnp.where(doc_hot(own_pos) | (lanes >= docs)[None, :], 0.0, NEG).astype(BF)
    ck_aug = [((pos[:, None] >= src_len) & (lanes == 0)[None, :]).astype(BF) for pos in (own_pos, peer_pos)]
    cq_aug = jnp.broadcast_to(jnp.where(lanes == 0, NEG, 0.0).astype(BF)[None, :], (2 * C, 128))

    scale = jnp.full((8, 128), (step_index[0] + 1).astype(F32) / 5.0, F32)
    src = send_pieces(gate(take_pieces(source, s), t))
    far = gate(
        second_hop(near, low), (*src, info, q_aug, *k_aug, cq_aug, *ck_aug, scale, e1, e2)
    )
    a1, b1 = all_parts(near, far, low)
    w_key, w_query = Pieces(n, (a1, 0, n, 0)), Pieces(n, (b1, 0, n, 0))
    w_value = Pieces(n, (a1, n, h, 0), (b1, n, h, h))
    x = Slots(t, 0, C)
    q, kv = project_qkv(info, x, w_query, w_key, w_value, ())
    q, kv, e1, e2 = barrier(q, kv, e1, e2)
    kv_peer = flip(kv, 1)
    first3, second3 = first_hop([e1, e2], low), second_hop([e1, e2], low)
    attended, p_self, r_self = attend_self(info, q, kv, kv_peer, (q_aug, *k_aug), ())
    *first3, attended, c_shard = barrier(*first3, attended, c_shard)
    w_contract = lax.all_gather(c_shard, "dp", axis=0, tiled=True)
    far3 = second_hop(first3, low)
    flips = [flip(v, low) for v in (e1, e2, *first3)]
    skv, y1, y1_low, inv1, cq = between(info, x, attended, w_out, c_query, Slots(src, 0, C), c_key, c_value, ())
    *flips, skv, cq, h0, h1, g0, g1 = barrier(*flips, skv, cq, *second3, *take_pieces(grad_output, s))
    second3, pieces = [h0, h1], [g0, g1]
    g_out = send_pieces(pieces)
    skv_peer = flip(skv, 1)
    cross_attended, p_cross, r_cross, second_low, inv2, y2 = attend_cross(
        info, cq, skv, skv_peer, (cq_aug, *ck_aug), y1, c_out
    )
    f0, f1, h0, h1, g0, g1, second_low = barrier(*far3, *second3, *g_out, second_low)
    far3, second3, g_out = [f0, f1], [h0, h1], [g0, g1]
    a3, b3 = [
        [(v, 0) for _, v in sorted(
            {0: own, 1: flips[i], b1: first3[i], b1 ^ 1: flips[2 + i], b2: second3[i], b2 ^ 1: flip(second3[i], low),
             6: far3[i], 7: flip(far3[i], low)}.items()
        )]
        for i, (own, b1, b2) in enumerate(((e1, 2, 4), (e2, 4, 2)))
    ]
    ea, eb = Pieces(n, (a3, 0, n, 0)), Pieces(n, (b3, 0, n, 0))
    gp, o0, o1, g3, kept, sent, gnar = feed_forward(
        info, second_low, ea, eb, w_contract, y2, adapter_down, adapter_up, Slots(g_out, 0, C), scale
    )
    output = send_back([o0, o1])
    total = Reduce(kept, sent, d, s, low)
    g2, grad_cross = ffn_back(info, g3, w_contract, ea, eb, gp, gnar, adapter_down, second_low, inv2, c_out, ())
    *total.got, g2, grad_cross = barrier(*total.got, g2, grad_cross)
    total.add()
    total.scatter_plane()
    gkv, gkv_peer, g1, grad_self = attend_cross_back(
        info, cq, skv, skv_peer, grad_cross, cross_attended, r_cross, p_cross, g2, y1_low, inv1, c_query, w_out, (total.kept,)
    )
    *total.got, o0, o1, grad_self, gkv_peer = barrier(*total.got, *output, grad_self, gkv_peer)
    output = [o0, o1]
    total.add()
    total.line(2)
    got = flip(gkv_peer, 1)
    pieces = source_grad(info, gkv, got, c_key, c_value, (grad_self, total.kept))
    pieces = send_back(pieces)
    gkv, gkv_peer, acc = attend_self_back(
        info, q, kv, kv_peer, grad_self, attended, r_self, p_self, g1, w_query, pieces[:0]
    )
    *total.got, s0, s1, gkv_peer = barrier(*total.got, *pieces, gkv_peer)
    got = flip(gkv_peer, 1)
    total.add()
    total.line(1)
    pieces = token_grad(info, acc, gkv, got, w_key, w_value, (total.kept,))
    *total.got, o0, o1, s0, s1, t0, t1 = barrier(*total.got, *output, s0, s1, *pieces)
    tokens_back = send_back([t0, t1])
    output = [o0, o1]
    total.add()
    total.low_bits()
    total.gather_plane()
    total.put()
    grads, other = total.value, flip(total.value, low)
    high = (d // low) % 2 == 1
    grad_up = pick(high, other, grads).astype(F32)
    A = adapter_down.shape[1]
    grad_down = pick(high, grads, other).astype(F32)
    grad_down = rows_of(*[grad_down[:, k : k + A] for k in range(0, D, A)])
    output, grad_source, grad_tokens = [join_rows(v, s) for v in (output, [s0, s1], tokens_back)]
    return (output, grad_tokens, grad_source, grad_down, grad_up)


def solution(mesh):
    rows = P("dp", "seq", None)
    weight = P("dp", None)
    return jax.shard_map(
        local,
        mesh=mesh,
        in_specs=(rows, rows, weight, P("dp"), P()) + (weight,) * 10 + (P(), P(), rows),
        out_specs=(rows, rows, rows, P(), P()),
        check_vma=False,
    )
```
